256 devices in a mesh: wide: 32 (over z, y), narrow: 8 (over x, core).
Axes of the slice: x: 4, y: 4, z: 8, core: 2. Of those that a mesh axis runs over, the one named last changes fastest.
Arguments:
- solution: float32 [8, 131072], P(None, ('wide', 'narrow')), may hold values from -6 to 6
- residual: float32 [8, 131072], P(None, ('wide', 'narrow')), may hold values from -600 to 600
- direction: float32 [8, 131072], P(None, ('wide', 'narrow')), may hold values from -600 to 600
- error_var: float32 [131072], P(('wide', 'narrow')), may hold values from 0.25 to 2
- footprint: bfloat16 [131072, 4, 128], P(('wide', 'narrow')), may hold values from -0.25 to 0.25
- tiles: int32 [131072, 4], P(('wide', 'narrow')), may hold values from 0 to 159
- window: int32 [131072, 1], P(('wide', 'narrow')), may hold values from 0 to 31; in each aligned block of 512 rows (0 to 511, 512 to 1023, ...) at most 40 rows name the same one
- temporal: bfloat16 [320, 320], replicated, may hold values from -40 to 40, as said below
- spatial_lat: bfloat16 [128, 128], replicated, may hold values from -40 to 40, as said below
- spatial_lon: bfloat16 [128, 128], replicated, may hold values from -40 to 40, as said below
Outputs:
- solution_new: float32 [8, 131072], P(None, ('wide', 'narrow'))
- residual_new: float32 [8, 131072], P(None, ('wide', 'narrow'))
- direction_new: float32 [8, 131072], P(None, ('wide', 'narrow'))
The draws below stay inside these ranges and needn't reach their ends.
Inputs may be any that keep to these rules, and one draw needn't show every extreme that they name: At most 40 of the observations held by one device share a window, and some device reaches that in every draw. `temporal`: A symmetric positive definite covariance. `spatial_lat`: A symmetric positive definite covariance. `spatial_lon`: A symmetric positive definite covariance.
All inputs are finite; a program needn't handle non-finite values.
Results may differ from the reference program's by a relative error of at most 0.004.
Values may be sent and summed in bfloat16 or wider, within the bound.
No kernel may reach another device: no remote copies, remote signals or barrier semaphores. Data moves between devices by JAX's collectives and lax.ppermute only.
A program may use at most 128 MiB of HBM per device.

```python
import math
import jax
import jax.numpy as jnp
import numpy as np
from jax import lax

LAT = 128
LON = 128
DAYS = 320
RHS = 8
NT = 4
OBS_DEV = 512
OBS = 131072
CAP = 40
DAY_DEV = 10
LATB = 16
TILES = 160
N_WIDE = 32
N_NARROW = 8


def covariance(key, order):
    length = max(order // 2, 1)
    normals = jnp.clip(jax.random.normal(key, (order, order), jnp.float32), -6.0, 6.0)
    position = jnp.arange(order, dtype=jnp.float32)
    decay = jnp.exp(-jnp.abs(position[:, None] - position[None, :]) / length)
    factor = normals * decay
    return jnp.dot(factor, factor.T, precision=lax.Precision.HIGHEST) / order + 0.5 * jnp.eye(order, dtype=jnp.float32)


def state_draw(key, salt):
    key = jax.random.fold_in(key, salt)
    key_rows = jax.random.fold_in(key, 0)
    key_cols = jax.random.fold_in(key, 1)
    key_base = jax.random.fold_in(key, 3)
    position = jnp.arange(OBS, dtype=jnp.float32) / max(OBS - 1, 1)
    row_scale = jnp.exp(jax.random.uniform(key_rows, (OBS,), jnp.float32, 0.0, math.log(10.0))) / math.sqrt(10.0)
    col_scale = jnp.exp(jax.random.uniform(key_cols, (RHS,), jnp.float32, 0.0, math.log(10.0))) / math.sqrt(10.0)
    base = jnp.clip(jax.random.normal(key_base, (RHS, OBS), jnp.float32), -6.0, 6.0)
    trend = 3.0 ** position
    return base * col_scale[:, None] * (trend * row_scale)[None, :]


def draw_temporal(key, part):
    return covariance(jax.random.fold_in(key, 11), DAYS).astype(jnp.bfloat16)


def draw_spatial_lat(key, part):
    return covariance(jax.random.fold_in(key, 12), LAT).astype(jnp.bfloat16)


def draw_spatial_lon(key, part):
    return covariance(jax.random.fold_in(key, 13), LON).astype(jnp.bfloat16)


def draw_residual(key, part):
    return state_draw(key, 21)


def draw_direction(key, part):
    return state_draw(key, 22)


def touch_ends(drawn, key, low, largest):
    place = [jax.random.randint(jax.random.fold_in(key, axis), (), 0, length) for axis, length in enumerate(drawn.shape)]
    widest = drawn.shape.index(max(drawn.shape))
    neighbour = place[:widest] + [(place[widest] + 1) % drawn.shape[widest]] + place[widest + 1:]
    return drawn.at[tuple(place)].set(low).at[tuple(neighbour)].set(largest)


def level_of(stream_key, shape, pieces, least, top_value):
    def one(dim, blocks):
        heights = jax.random.uniform(jax.random.fold_in(jax.random.fold_in(stream_key, 6), dim), (blocks,), jnp.float32, least / len(pieces), top_value / len(pieces))
        return jnp.repeat(jnp.exp(heights), shape[dim] // blocks).reshape((-1,) + (1,) * (len(shape) - dim - 1))

    level = one(*pieces[0])
    for cut in pieces[1:]:
        level = level * one(*cut)
    return level


def routed_block(own_key, own, number, rows, count, top, reach, lean):
    sequence = jax.random.permutation(own_key, count)
    packed, usual = load_shares(count, rows * top, reach, lean, True), load_shares(count, rows * top, reach, lean, False)
    places = jnp.arange(count)

    def named(sizes, rotation):
        used = int((sizes > 0).sum())
        fixed = max(1, used // 4)
        moved = fixed + (places - fixed + rotation * (used - fixed)) % max(1, count - fixed)
        return jnp.zeros((count,), jnp.int32).at[sequence[jnp.where(places < fixed, places, moved)]].set(jnp.asarray(sizes, jnp.int32))

    sizes = jnp.where(number % 4 == 0, named(packed, number // 4), named(usual, number - number // 4 - 1))
    mixed = jax.random.permutation(jax.random.fold_in(own, 3), count)
    giver, sink = mixed[0:count // 2 * 2:2], mixed[1:count // 2 * 2:2]
    margin = jnp.minimum(sizes[giver] - 1, reach - sizes[sink]) // 2
    margin = jnp.where((giver == sequence[0]) | (sink == sequence[0]) | (sizes[sink] == 0), 0, jnp.maximum(margin, 0))
    moved = jax.random.randint(jax.random.fold_in(own, 4), (count // 2,), 0, 1 << 20) % (margin + 1)
    sizes = sizes.at[giver].add(-moved).at[sink].add(moved)
    members = jnp.searchsorted(jnp.cumsum(sizes), jnp.arange(rows * top), side="right").astype(jnp.int32)
    table = members.reshape(top, rows).T
    table = table[jax.random.permutation(jax.random.fold_in(own, 1), rows)]
    rotation = jax.random.randint(jax.random.fold_in(own, 2), (rows, 1), 0, top)
    return jnp.take_along_axis(table, (jnp.arange(top)[None, :] + rotation) % top, axis=1)


def load_shares(amount, total, bound, slope, full):
    portions = [(1 << 20) // math.isqrt(standing ** slope) + 1 for standing in range(1, amount + 1)]
    largest = bound if full else min(bound, max(-(-total // amount), total * portions[0] // sum(portions)))
    least = 1 if total - largest >= amount - 1 else 0
    counts, spare = [largest] + [least] * (amount - 1), total - largest - least * (amount - 1)
    while spare > 0:
        candidates = [i for i in range(1, amount) if counts[i] < largest] or [i for i in range(1, amount) if counts[i] < bound]
        pool, remaining = sum([portions[i] for i in candidates]), spare
        for i in candidates:
            addition = min(bound - counts[i], max(1, remaining * portions[i] // pool), spare)
            counts[i] = counts[i] + addition
            spare = spare - addition
    return np.array(counts)


def centred(rng, dims, deviation, reach, pieces=(), kind=jnp.bfloat16):
    array = jax.random.normal(rng, dims, jnp.float32) * deviation
    if len(pieces) > 0:
        array = level_of(rng, dims, pieces, -0.22, 0.18) * array
    return jnp.clip(array, min=-reach, max=reach).astype(kind)


def setup_inputs(seed: int = 0) -> dict:
    key_of = jax.random.split(jax.random.key(seed), 11)
    solution = centred(key_of[0], (RHS, OBS), 1.0, 6.0, ((1, 256),), jnp.float32)
    residual = draw_residual(jax.random.fold_in(key_of[10], 71), 0)
    direction = draw_direction(jax.random.fold_in(key_of[10], 71), 0)
    error_var = jnp.clip(jnp.exp(math.log(2.0) - 2.0794415 * jax.random.uniform(key_of[3], (OBS,), jnp.float32) ** level_of(key_of[3], (OBS,), ((0, 256),), -0.2, 0.2)), 0.25, 2.0)
    footprint = centred(key_of[4], (OBS, NT, LON), (NT * LON) ** -0.5, 0.25, ((0, 256),))
    tiles = touch_ends(jax.random.randint(key_of[5], (OBS, NT), 0, TILES), jax.random.fold_in(key_of[5], 1), 0, TILES - 1).astype(jnp.int32)
    window_keys = jax.random.split(jax.random.fold_in(key_of[6], 1), OBS // OBS_DEV)
    window_turns = jax.random.permutation(jax.random.fold_in(key_of[6], 3), OBS // OBS_DEV)
    window = jax.vmap(lambda own, number: routed_block(jax.random.fold_in(key_of[6], 2), own, number, OBS_DEV, N_WIDE, 1, CAP, 1))(window_keys, window_turns).reshape((OBS, 1))
    temporal = draw_temporal(jax.random.fold_in(key_of[10], 71), 0)
    spatial_lat = draw_spatial_lat(jax.random.fold_in(key_of[10], 71), 0)
    spatial_lon = draw_spatial_lon(jax.random.fold_in(key_of[10], 71), 0)
    return {"solution": solution, "residual": residual, "direction": direction, "error_var": error_var, "footprint": footprint, "tiles": tiles, "window": window, "temporal": temporal, "spatial_lat": spatial_lat, "spatial_lon": spatial_lon}


HIGHEST = lax.Precision.HIGHEST

def chol_solve(matrix, right):
    chol_low = jnp.linalg.cholesky(matrix)
    half_solve = lax.linalg.triangular_solve(chol_low, right, left_side=True, lower=True)
    return lax.linalg.triangular_solve(chol_low, half_solve, left_side=True, lower=True, transpose_a=True)

def gram_matrix(left, right):
    return jnp.dot(left, right.T, precision=HIGHEST)

def reference(solution, residual, direction, error_var, footprint, tiles, window, temporal, spatial_lat, spatial_lon):
    obs_total = footprint.shape[0]
    obs_index = jnp.arange(obs_total, dtype=jnp.int32)
    band_index = obs_index // OBS_DEV % N_NARROW
    day_index = window[:, 0][:, None] * DAY_DEV + tiles // LATB
    lat_index = band_index[:, None] * LATB + tiles % LATB
    cell_index = (day_index * LAT + lat_index).astype(jnp.int32)
    dir_half = direction.astype(jnp.bfloat16)
    block_rows = math.gcd(obs_total, 4096)
    block_count = obs_total // block_rows
    foot_blocks = footprint.reshape(block_count, block_rows, NT, LON)
    dir_blocks = dir_half.T.reshape(block_count, block_rows, RHS)
    cell_blocks = cell_index.reshape(block_count, block_rows * NT)

    def adjoint_step(accum, inputs):
        foot_block, dir_block, cell_block = inputs
        contrib = foot_block.astype(jnp.float32)[:, :, None, :] * dir_block.astype(jnp.float32)[:, None, :, None]
        return (accum.at[cell_block].add(contrib.reshape(block_rows * NT, RHS * LON)), None)
    start_accum = jnp.zeros((DAYS * LAT, RHS * LON), jnp.float32)
    accum, _ = lax.scan(adjoint_step, start_accum, (foot_blocks, dir_blocks, cell_blocks))
    fluxes = accum.astype(jnp.bfloat16).reshape(DAYS, LAT, RHS, LON)
    timed_flux = jnp.einsum('ts,sarl->tarl', temporal.astype(jnp.float32), fluxes.astype(jnp.float32)).astype(jnp.bfloat16)
    spread_lat = jnp.einsum('ab,tbrl->tarl', spatial_lat.astype(jnp.float32), timed_flux.astype(jnp.float32)).astype(jnp.bfloat16)
    smoothed = jnp.einsum('tarm,lm->tarl', spread_lat.astype(jnp.float32), spatial_lon.astype(jnp.float32)).astype(jnp.bfloat16)
    flux_table = smoothed.reshape(DAYS * LAT, RHS * LON)

    def forward_step(accum_dummy, inputs):
        foot_block, cell_block = inputs
        picked = flux_table[cell_block].reshape(block_rows, NT, RHS, LON).astype(jnp.float32)
        return (accum_dummy, jnp.einsum('bkrl,bkl->rb', picked, foot_block.astype(jnp.float32)))
    _, model_blocks = lax.scan(forward_step, jnp.zeros((), jnp.float32), (foot_blocks, cell_blocks))
    model_part = jnp.transpose(model_blocks, (1, 0, 2)).reshape(RHS, obs_total)
    model_image = model_part + error_var[None, :] * direction
    curvature = gram_matrix(direction, model_image)
    sym = 0.5 * (curvature + curvature.T)
    res_norm = gram_matrix(residual, residual)
    step_matrix = chol_solve(sym, res_norm)
    solution_new = solution + jnp.dot(step_matrix.T, direction, precision=HIGHEST)
    residual_new = residual - jnp.dot(step_matrix.T, model_image, precision=HIGHEST)
    norm_new = gram_matrix(residual_new, residual_new)
    ratio_matrix = chol_solve(res_norm, norm_new)
    direction_new = residual_new + jnp.dot(ratio_matrix.T, direction, precision=HIGHEST)
    return (solution_new, residual_new, direction_new)
```

```python
import jax
import jax.numpy as jnp
from jax import lax
from jax.experimental import pallas as pl
from jax.experimental.pallas import tpu as pltpu
from jax.sharding import PartitionSpec as P

F32 = jnp.float32
BF16 = jnp.bfloat16
I32 = jnp.int32
HIGHEST = lax.Precision.HIGHEST
LANES = 128
RHS = 8
NT = 4
N_WIDE = 32
N_NARROW = 8
OBS_DEV = 512
CAP = 40
SLOTS = N_WIDE * CAP
DAY_DEV = 10
DAYS = N_WIDE * DAY_DEV
LAT = 128
CELLS = 160
QUAD = 4
CHUNK = DAY_DEV * QUAD
ROWS = RHS * CELLS
META = 48
PAYLOAD = NT * CAP + 16
GRAM_AT = CAP
VMEM_LIMIT = 48 * 1024 * 1024


def dot_rows(left, right, precision=None):
    return lax.dot_general(
        left, right, (((1,), (1,)), ((), ())), precision=precision, preferred_element_type=F32
    )


def dot(left, right, precision=None):
    return lax.dot_general(
        left, right, (((1,), (0,)), ((), ())), precision=precision, preferred_element_type=F32
    )


def lane_window(block):
    start = min(block * CAP // LANES * LANES, SLOTS - 2 * LANES)
    return start, block * CAP - start


def take_lanes(ref, row, rows, block):
    start, shift = lane_window(block)
    part = ref[row : row + rows, start : start + 2 * LANES]
    return pltpu.roll(part, (2 * LANES - shift) % (2 * LANES), 1)[:, :LANES]


def add_lanes(ref, row, rows, block, piece):
    start, shift = lane_window(block)
    wide = jnp.concatenate([piece, jnp.zeros((rows, LANES), F32)], axis=1)
    ref[row : row + rows, start : start + 2 * LANES] += pltpu.roll(wide, shift, 1)


def split_two(value):
    high = value.astype(BF16)
    return high.astype(F32), value - high.astype(F32)


def slot_matrix(slot_row):
    rows = lax.broadcasted_iota(I32, (SLOTS, OBS_DEV), 0)
    return jnp.where(rows == slot_row, 1.0, 0.0).astype(BF16)


def pack_kernel(
    window_ref, tiles_ref, foot_ref, dir_ref, res_ref, err_ref, send_ref, slot_ref, pick, moved, meta
):
    window = window_ref[...]
    named = lax.broadcasted_iota(I32, (N_WIDE, OBS_DEV), 0) == window
    named_f = jnp.where(named, 1.0, 0.0)
    earlier = lax.broadcasted_iota(I32, (OBS_DEV, OBS_DEV), 0) < lax.broadcasted_iota(
        I32, (OBS_DEV, OBS_DEV), 1
    )
    before = dot(named_f.astype(BF16), jnp.where(earlier, 1.0, 0.0).astype(BF16))
    position = jnp.sum(before * named_f, axis=0, keepdims=True).astype(I32)
    slot = window * CAP + position
    slot_ref[...] = slot
    pick[...] = slot_matrix(slot)
    moved[...] = dot(pick[...], foot_ref[...])
    tile = tiles_ref[...]
    day, row = tile >> 4, tile & 15
    cell = ((row >> 2) * CHUNK + day * QUAD + (row & 3)).astype(F32)
    dir_high, dir_low = split_two(dir_ref[...])
    res_high, res_low = split_two(res_ref[...])
    err_high, err_low = split_two(err_ref[...])
    zero = jnp.zeros((2, OBS_DEV), F32)
    values = jnp.concatenate(
        [
            dir_high,
            jnp.concatenate([cell, err_high, err_low, zero], axis=0),
            dir_low,
            res_high,
            res_low,
            jnp.zeros((8, OBS_DEV), F32),
        ],
        axis=0,
    ).astype(BF16)
    meta[...] = dot_rows(values, pick[...])
    lane = lax.broadcasted_iota(I32, (16, LANES), 1)
    for block in range(N_WIDE):
        rows = slice(block * CAP, (block + 1) * CAP)
        parts = [moved[rows, k * LANES : (k + 1) * LANES] for k in range(NT)]
        send_ref[block, : NT * CAP, :] = jnp.concatenate(parts, axis=0).astype(BF16)
        groups = [take_lanes(meta, 16 * g, 16, block) for g in range(3)]
        joined = jnp.where(
            lane < CAP,
            groups[0],
            jnp.where(
                lane < 2 * CAP,
                pltpu.roll(groups[1], CAP, 1),
                jnp.where(lane < 3 * CAP, pltpu.roll(groups[2], 2 * CAP, 1), 0.0),
            ),
        )
        send_ref[block, NT * CAP :, :] = joined.astype(BF16)


def adjoint_kernel(recv_ref, flux_ref, meta_ref, foot_ref, rows_f, hot, weighted, total):
    meta_ref[...] = jnp.zeros((META, SLOTS), F32)
    lane = lax.broadcasted_iota(I32, (16, LANES), 1)
    for block in range(N_WIDE):
        values = recv_ref[block, : NT * CAP, :].astype(F32)
        for k in range(NT):
            rows_f[k, block * CAP : (block + 1) * CAP, :] = values[k * CAP : (k + 1) * CAP, :]
        joined = recv_ref[block, NT * CAP :, :].astype(F32)
        for g in range(3):
            piece = joined if g == 0 else pltpu.roll(joined, LANES - g * CAP, 1)
            add_lanes(meta_ref, 16 * g, 16, block, jnp.where(lane < CAP, piece, 0.0))
    cells = lax.broadcasted_iota(I32, (CELLS, SLOTS), 0)
    for k in range(NT):
        foot = rows_f[k].astype(BF16)
        foot_ref[k] = foot
        ids = meta_ref[8 + k : 9 + k, :].astype(I32)
        hot[...] = jnp.where(cells == ids, 1.0, 0.0).astype(BF16)
        for r in range(RHS):
            row = jnp.broadcast_to(meta_ref[r : r + 1, :], (16, SLOTS)).astype(BF16)
            for t in range(CELLS // 16):
                weighted[r * CELLS + t * 16 : r * CELLS + (t + 1) * 16, :] = (
                    hot[t * 16 : (t + 1) * 16, :] * row
                )
        product = dot(weighted[...], foot)
        if k == 0:
            total[...] = product
        elif k < NT - 1:
            total[...] += product
        else:
            flux_ref[...] = (total[...] + product).astype(BF16)


def lat_kernel(mix_ref, flux_ref, out_ref, rows_f, columns):
    rows_f[...] = flux_ref[...].astype(F32)
    for a in range(QUAD):
        for d in range(DAY_DEV):
            columns[a * N_WIDE : (a + 1) * N_WIDE, d * LANES : (d + 1) * LANES] = rows_f[
                pl.ds(d * QUAD + a, N_WIDE, stride=CHUNK), :
            ].astype(BF16)
    mixed = dot(mix_ref[...], columns[...])
    for a in range(QUAD):
        for d in range(DAY_DEV):
            rows_f[pl.ds(d * QUAD + a, N_WIDE, stride=CHUNK), :] = mixed[
                a * N_WIDE : (a + 1) * N_WIDE, d * LANES : (d + 1) * LANES
            ]
    out_ref[...] = rows_f[...].astype(BF16)


def day_kernel(mix_ref, flux_ref, out_ref, rows_f, columns):
    rows_f[...] = flux_ref[...].astype(F32)
    for a in range(QUAD):
        columns[:, a * LANES : (a + 1) * LANES] = rows_f[
            pl.ds(a, DAYS, stride=QUAD), :
        ].astype(BF16)
    mixed = dot(mix_ref[...], columns[...])
    for a in range(QUAD):
        rows_f[pl.ds(a, DAYS, stride=QUAD), :] = mixed[:, a * LANES : (a + 1) * LANES]
    out_ref[...] = rows_f[...].astype(BF16)


def forward_kernel(
    lon_ref, spread_ref, foot_ref, meta_ref, dir_ref, res_ref, err_ref, send_ref, table, picked, model
):
    table[...] = dot_rows(spread_ref[...], lon_ref[...]).astype(BF16)
    width = 2 * LANES
    cells = lax.broadcasted_iota(I32, (CELLS, width), 0)
    for tile in range(SLOTS // width):
        at = slice(tile * width, (tile + 1) * width)
        sums = [jnp.zeros((1, width), F32)] * RHS
        for k in range(NT):
            picked[...] = dot_rows(table[...], foot_ref[k, at, :])
            mask = cells == meta_ref[8 + k : 9 + k, at].astype(I32)
            for r in range(RHS):
                rows = picked[r * CELLS : (r + 1) * CELLS, :]
                sums[r] = sums[r] + jnp.sum(jnp.where(mask, rows, 0.0), axis=0, keepdims=True)
        model[:, at] = jnp.concatenate(sums, axis=0)
    held_dir = meta_ref[0:8, :] + meta_ref[16:24, :]
    held_res = meta_ref[24:32, :] + meta_ref[32:40, :]
    held_err = meta_ref[12:13, :] + meta_ref[13:14, :]
    modelled = model[...]
    held = jnp.concatenate([modelled, held_dir, held_res, held_err * held_dir], axis=0)
    far = dot_rows(held, held, HIGHEST)
    direction = dir_ref[...]
    own = jnp.concatenate([direction, res_ref[...], err_ref[...] * direction], axis=0)
    near = dot_rows(own, own, HIGHEST)
    gram = jnp.concatenate(
        [
            jnp.zeros((RHS, GRAM_AT), F32),
            far[0:8, 8:16] + near[16:24, 0:8],
            far[8:16, 0:8] + near[0:8, 16:24],
            far[0:8, 16:24] + near[16:24, 8:16],
            far[16:24, 0:8] + near[8:16, 16:24],
            far[0:8, 0:8] + far[0:8, 24:32] + far[24:32, 0:8] + near[16:24, 16:24],
            near[8:16, 8:16],
            jnp.zeros((RHS, LANES - GRAM_AT - 48), F32),
        ],
        axis=1,
    )
    lane = lax.broadcasted_iota(I32, (RHS, LANES), 1)
    for block in range(N_WIDE):
        send_ref[block] = jnp.where(lane < CAP, take_lanes(model, 0, RHS, block), gram)


def gather_kernel(home_ref, slot_ref, dir_ref, err_ref, image_ref, lined):
    lined[...] = jnp.zeros((RHS, SLOTS), F32)
    lane = lax.broadcasted_iota(I32, (RHS, LANES), 1)
    for block in range(N_WIDE):
        add_lanes(lined, 0, RHS, block, jnp.where(lane < CAP, home_ref[block], 0.0))
    high, rest = split_two(lined[...])
    middle, low = split_two(rest)
    parts = jnp.concatenate([high, middle, low], axis=0).astype(BF16)
    placed = dot(parts, slot_matrix(slot_ref[...]))
    image_ref[...] = placed[0:8] + placed[8:16] + placed[16:24] + err_ref[...] * dir_ref[...]


def inverses(matrices):
    row = lax.broadcasted_iota(I32, (RHS, RHS), 0)
    column = lax.broadcasted_iota(I32, (RHS, RHS), 1)
    unit = jnp.where(row == column, 1.0, 0.0)
    state = [jnp.concatenate([m, unit], axis=1) for m in matrices]
    side = lax.broadcasted_iota(I32, (RHS, 2 * RHS), 0)
    for j in range(RHS):
        following = []
        for m in state:
            pivot = m[j : j + 1, :] / m[j : j + 1, j : j + 1]
            following.append(jnp.where(side == j, pivot, m - m[:, j : j + 1] * pivot))
        state = following
    return [m[:, RHS:] for m in state]


def update_kernel(gram_ref, sol_ref, res_ref, dir_ref, image_ref, sol_out, res_out, dir_out):
    total = gram_ref[0]
    for n in range(1, N_NARROW):
        total = total + gram_ref[n]
    block = lambda g: total[:, GRAM_AT + 8 * g : GRAM_AT + 8 * g + 8]
    image_dir, dir_image, image_res, res_image, image_image, res_norm = [block(g) for g in range(6)]
    sym = 0.5 * (image_dir + dir_image)
    sym_inverse, norm_inverse = inverses([sym, res_norm])
    step = dot(sym_inverse, res_norm, HIGHEST)
    step_t = dot(res_norm, sym_inverse, HIGHEST)
    crossed = dot(step_t, image_res, HIGHEST) + dot(res_image, step, HIGHEST)
    squared = dot(dot(step_t, image_image, HIGHEST), step, HIGHEST)
    norm_new = res_norm - crossed + squared
    ratio_t = dot(norm_new, norm_inverse, HIGHEST)
    direction = dir_ref[...]
    sol_out[...] = sol_ref[...] + dot(step_t, direction, HIGHEST)
    residual = res_ref[...] - dot(step_t, image_ref[...], HIGHEST)
    res_out[...] = residual
    dir_out[...] = residual + dot(ratio_t, direction, HIGHEST)


def call(kernel, outs, scratch, flops, moved):
    return pl.pallas_call(
        kernel,
        out_shape=[jax.ShapeDtypeStruct(shape, dtype) for shape, dtype in outs],
        scratch_shapes=[pltpu.VMEM(shape, dtype) for shape, dtype in scratch],
        compiler_params=pltpu.CompilerParams(vmem_limit_bytes=VMEM_LIMIT),
        cost_estimate=pl.CostEstimate(flops=flops, bytes_accessed=moved, transcendentals=0),
    )


def exchange(array, axis):
    return lax.all_to_all(array, axis, split_axis=0, concat_axis=0, tiled=True)


def on_device(
    solution,
    residual,
    direction,
    error_var,
    footprint,
    tiles,
    window,
    temporal,
    spatial_lat,
    spatial_lon,
):
    errors = error_var.reshape(1, OBS_DEV)
    with jax.named_scope("pack"):
        packed, slot = call(
            pack_kernel,
            [((N_WIDE, PAYLOAD, LANES), BF16), ((1, OBS_DEV), I32)],
            [
                ((SLOTS, OBS_DEV), BF16),
                ((SLOTS, NT * LANES), F32),
                ((META, SLOTS), F32),
            ],
            2 * SLOTS * OBS_DEV * NT * LANES,
            2 * SLOTS * OBS_DEV,
        )(
            window.reshape(1, OBS_DEV),
            tiles.T,
            footprint.reshape(OBS_DEV, NT * LANES),
            direction,
            residual,
            errors,
        )
    with jax.named_scope("route"):
        routed = exchange(packed, "wide")
    with jax.named_scope("adjoint"):
        flux, meta, foot = call(
            adjoint_kernel,
            [((ROWS, LANES), BF16), ((META, SLOTS), F32), ((NT, SLOTS, LANES), BF16)],
            [
                ((NT, SLOTS, LANES), F32),
                ((CELLS, SLOTS), BF16),
                ((ROWS, SLOTS), BF16),
                ((ROWS, LANES), F32),
            ],
            2 * ROWS * NT * SLOTS * LANES,
            4 * NT * SLOTS * LANES,
        )(routed)
    with jax.named_scope("to_rhs"):
        by_rhs = exchange(flux.reshape(N_NARROW, CELLS, LANES), "narrow")
    with jax.named_scope("lat_mix"):
        lat_mix = (
            spatial_lat.reshape(N_WIDE, QUAD, N_WIDE, QUAD).transpose(1, 0, 3, 2).reshape(LAT, LAT)
        )
        (spread,) = call(
            lat_kernel,
            [((ROWS, LANES), BF16)],
            [((ROWS, LANES), F32), ((LAT, DAY_DEV * LANES), BF16)],
            2 * LAT * LAT * DAY_DEV * LANES,
            4 * ROWS * LANES,
        )(lat_mix, by_rhs.reshape(ROWS, LANES))
    with jax.named_scope("to_days"):
        by_day = exchange(spread.reshape(N_WIDE, CHUNK, LANES), "wide")
    with jax.named_scope("day_mix"):
        (timed,) = call(
            day_kernel,
            [((ROWS, LANES), BF16)],
            [((ROWS, LANES), F32), ((DAYS, QUAD * LANES), BF16)],
            2 * DAYS * DAYS * QUAD * LANES,
            4 * ROWS * LANES,
        )(temporal, by_day.reshape(ROWS, LANES))
    with jax.named_scope("to_windows"):
        by_window = exchange(timed.reshape(N_WIDE, CHUNK, LANES), "wide")
    with jax.named_scope("to_bands"):
        by_band = exchange(by_window.reshape(N_NARROW, CELLS, LANES), "narrow")
    with jax.named_scope("forward"):
        (modelled,) = call(
            forward_kernel,
            [((N_WIDE, RHS, LANES), F32)],
            [((ROWS, LANES), BF16), ((ROWS, 2 * LANES), F32), ((RHS, SLOTS), F32)],
            2 * ROWS * NT * SLOTS * LANES,
            4 * NT * SLOTS * LANES,
        )(
            spatial_lon,
            by_band.reshape(ROWS, LANES),
            foot,
            meta,
            direction,
            residual,
            errors,
        )
    with jax.named_scope("home"):
        home = exchange(modelled, "wide")
    with jax.named_scope("gram_sum"):
        partial = jnp.broadcast_to(home.sum(axis=0)[None], (N_NARROW, RHS, LANES))
        grams = exchange(partial, "narrow")
    with jax.named_scope("image"):
        (image,) = call(
            gather_kernel,
            [((RHS, OBS_DEV), F32)],
            [((RHS, SLOTS), F32)],
            2 * 24 * SLOTS * OBS_DEV,
            4 * SLOTS * RHS,
        )(home, slot, direction, errors)
    with jax.named_scope("update"):
        return tuple(
            call(
                update_kernel,
                [((RHS, OBS_DEV), F32)] * 3,
                [],
                2 * 18 * 8 * 8 * OBS_DEV,
                28 * RHS * OBS_DEV,
            )(grams, solution, residual, direction, image)
        )


def solution(mesh):
    both = ("wide", "narrow")
    in_specs = (
        P(None, both),
        P(None, both),
        P(None, both),
        P(both),
        P(both, None, None),
        P(both, None),
        P(both, None),
        P(),
        P(),
        P(),
    )
    out_specs = (P(None, both), P(None, both), P(None, both))
    return jax.shard_map(
        on_device, mesh=mesh, in_specs=in_specs, out_specs=out_specs, check_vma=False
    )
```

```python
import jax
import jax.numpy as jnp
from jax import lax
from jax.experimental import pallas as pl
from jax.experimental.pallas import tpu as pltpu
from jax.sharding import PartitionSpec as P

F32 = jnp.float32
BF16 = jnp.bfloat16
I32 = jnp.int32
HIGHEST = lax.Precision.HIGHEST
LANES = 128
RHS = 8
NT = 4
N_WIDE = 32
N_NARROW = 8
OBS_DEV = 512
CAP = 40
SLOTS = N_WIDE * CAP
DAY_DEV = 10
DAYS = N_WIDE * DAY_DEV
LAT = 128
CELLS = 160
QUAD = 4
CHUNK = DAY_DEV * QUAD
ROWS = RHS * CELLS
META = 48
PAYLOAD = NT * CAP + 16
GRAM_AT = CAP
SEND_BLOCKS = 8
VMEM_LIMIT = 48 * 1024 * 1024
VMEM_WHOLE = 63 * 1024 * 1024


def dot_rows(left, right, precision=None):
    return lax.dot_general(
        left, right, (((1,), (1,)), ((), ())), precision=precision, preferred_element_type=F32
    )


def dot(left, right, precision=None):
    return lax.dot_general(
        left, right, (((1,), (0,)), ((), ())), precision=precision, preferred_element_type=F32
    )


def lane_window(block):
    start = min(block * CAP // LANES * LANES, SLOTS - 2 * LANES)
    return start, block * CAP - start


def take_lanes(ref, row, rows, block):
    start, shift = lane_window(block)
    part = ref[row : row + rows, start : start + 2 * LANES]
    return pltpu.roll(part, (2 * LANES - shift) % (2 * LANES), 1)[:, :LANES]


def add_lanes(ref, row, rows, block, piece):
    start, shift = lane_window(block)
    wide = jnp.concatenate([piece, jnp.zeros((rows, LANES), F32)], axis=1)
    ref[row : row + rows, start : start + 2 * LANES] += pltpu.roll(wide, shift, 1)


def split_two(value):
    high = value.astype(BF16)
    return high.astype(F32), value - high.astype(F32)


def slot_matrix(slot_row):
    rows = lax.broadcasted_iota(I32, (SLOTS, OBS_DEV), 0)
    return jnp.where(rows == slot_row, 1.0, 0.0).astype(BF16)


def pack_kernel(
    window_hbm,
    tiles_hbm,
    foot_hbm,
    dir_hbm,
    res_hbm,
    err_hbm,
    turn_ref,
    send_hbm,
    slot_ref,
    send_ref,
    window_ref,
    tiles_ref,
    foot_ref,
    dir_ref,
    res_ref,
    err_ref,
    by_tile,
    pick,
    moved,
    meta,
    sems,
    send_sems,
):
    copies = [
        pltpu.make_async_copy(source, target, sems.at[i])
        for i, (source, target) in enumerate(
            [
                (window_hbm, window_ref),
                (foot_hbm, foot_ref),
                (dir_hbm, dir_ref),
                (res_hbm, res_ref),
                (err_hbm, err_ref),
                (tiles_hbm, tiles_ref),
            ]
        )
    ]
    for copy in copies:
        copy.start()
    earlier = lax.broadcasted_iota(I32, (OBS_DEV, OBS_DEV), 0) < lax.broadcasted_iota(
        I32, (OBS_DEV, OBS_DEV), 1
    )
    earlier = jnp.where(earlier, 1.0, 0.0).astype(BF16)
    copies[0].wait()
    owner = window_ref[...] ^ turn_ref[0]
    named = lax.broadcasted_iota(I32, (N_WIDE, OBS_DEV), 0) == owner
    named_f = jnp.where(named, 1.0, 0.0)
    before = dot(named_f.astype(BF16), earlier)
    position = jnp.sum(before * named_f, axis=0, keepdims=True).astype(I32)
    slot = owner * CAP + position
    slot_ref[...] = slot
    pick[...] = slot_matrix(slot)
    group = 2 * LANES
    share = group // NT
    out_row = lax.broadcasted_iota(I32, (group, group), 0)
    in_row = lax.broadcasted_iota(I32, (group, group), 1)
    sort = jnp.where(in_row == out_row % share * NT + out_row // share, 1.0, 0.0).astype(BF16)
    copies[1].wait()
    for g in range(OBS_DEV // share):
        rows = dot(sort, foot_ref[g * group : (g + 1) * group, :]).astype(BF16)
        for k in range(NT):
            by_tile[g * share : (g + 1) * share, k * LANES : (k + 1) * LANES] = rows[
                k * share : (k + 1) * share, :
            ]
    moved[...] = dot(pick[...], by_tile[...])
    for copy in copies[2:]:
        copy.wait()
    tile = tiles_ref[...]
    day, row = tile >> 4, tile & 15
    cell = ((row >> 2) * CHUNK + day * QUAD + (row & 3)).astype(F32)
    dir_high, dir_low = split_two(dir_ref[...])
    res_high, res_low = split_two(res_ref[...])
    err_high, err_low = split_two(err_ref[...])
    zero = jnp.zeros((2, OBS_DEV), F32)
    values = jnp.concatenate(
        [
            dir_high,
            jnp.concatenate([cell, err_high, err_low, zero], axis=0),
            dir_low,
            res_high,
            res_low,
            jnp.zeros((8, OBS_DEV), F32),
        ],
        axis=0,
    ).astype(BF16)
    meta[...] = dot_rows(values, pick[...])
    sends = []
    lane = lax.broadcasted_iota(I32, (16, LANES), 1)
    for block in range(N_WIDE):
        rows = slice(block * CAP, (block + 1) * CAP)
        parts = [moved[rows, k * LANES : (k + 1) * LANES] for k in range(NT)]
        send_ref[block, : NT * CAP, :] = jnp.concatenate(parts, axis=0).astype(BF16)
        groups = [take_lanes(meta, 16 * g, 16, block) for g in range(3)]
        joined = jnp.where(
            lane < CAP,
            groups[0],
            jnp.where(
                lane < 2 * CAP,
                pltpu.roll(groups[1], CAP, 1),
                jnp.where(lane < 3 * CAP, pltpu.roll(groups[2], 2 * CAP, 1), 0.0),
            ),
        )
        send_ref[block, NT * CAP :, :] = joined.astype(BF16)
        if block % SEND_BLOCKS == SEND_BLOCKS - 1:
            part = pl.ds(block + 1 - SEND_BLOCKS, SEND_BLOCKS)
            sends.append(
                pltpu.make_async_copy(
                    send_ref.at[part], send_hbm.at[part], send_sems.at[block // SEND_BLOCKS]
                )
            )
            sends[-1].start()
    for send in sends:
        send.wait()


def adjoint_kernel(recv_ref, flux_ref, meta_ref, foot_ref, rows_f, hot, weighted, total):
    meta_ref[...] = jnp.zeros((META, SLOTS), F32)
    lane = lax.broadcasted_iota(I32, (16, LANES), 1)
    for block in range(N_WIDE):
        values = recv_ref[block, : NT * CAP, :].astype(F32)
        for k in range(NT):
            rows_f[k, block * CAP : (block + 1) * CAP, :] = values[k * CAP : (k + 1) * CAP, :]
        joined = recv_ref[block, NT * CAP :, :].astype(F32)
        for g in range(3):
            piece = joined if g == 0 else pltpu.roll(joined, LANES - g * CAP, 1)
            add_lanes(meta_ref, 16 * g, 16, block, jnp.where(lane < CAP, piece, 0.0))
    cells = lax.broadcasted_iota(I32, (CELLS, SLOTS), 0)
    for k in range(NT):
        foot = rows_f[k].astype(BF16)
        foot_ref[k] = foot
        ids = meta_ref[8 + k : 9 + k, :].astype(I32)
        hot[...] = jnp.where(cells == ids, 1.0, 0.0).astype(BF16)
        for r in range(RHS):
            row = jnp.broadcast_to(meta_ref[r : r + 1, :], (16, SLOTS)).astype(BF16)
            for t in range(CELLS // 16):
                weighted[r * CELLS + t * 16 : r * CELLS + (t + 1) * 16, :] = (
                    hot[t * 16 : (t + 1) * 16, :] * row
                )
        product = dot(weighted[...], foot)
        if k == 0:
            total[...] = product
        elif k < NT - 1:
            total[...] += product
        else:
            flux_ref[...] = (total[...] + product).astype(BF16)


def lat_kernel(turn_ref, mix_ref, flux_ref, out_ref, rows_f, columns):
    turn = turn_ref[0]
    for n in range(N_NARROW):
        rows_f[n * CELLS : (n + 1) * CELLS, :] = flux_ref[n ^ turn].astype(F32)
    for a in range(QUAD):
        for d in range(DAY_DEV):
            columns[a * N_WIDE : (a + 1) * N_WIDE, d * LANES : (d + 1) * LANES] = rows_f[
                pl.ds(d * QUAD + a, N_WIDE, stride=CHUNK), :
            ].astype(BF16)
    mixed = dot(mix_ref[...], columns[...])
    for a in range(QUAD):
        for d in range(DAY_DEV):
            rows_f[pl.ds(d * QUAD + a, N_WIDE, stride=CHUNK), :] = mixed[
                a * N_WIDE : (a + 1) * N_WIDE, d * LANES : (d + 1) * LANES
            ]
    out_ref[...] = rows_f[...].astype(BF16)


def day_kernel(turn_ref, mix_ref, flux_ref, out_ref, rows_f, columns):
    turn_in, turn_out = turn_ref[0], turn_ref[1]
    for h in range(N_NARROW):
        rows_f[h * CELLS : (h + 1) * CELLS, :] = flux_ref[h ^ turn_in].astype(F32)
    for a in range(QUAD):
        columns[:, a * LANES : (a + 1) * LANES] = rows_f[
            pl.ds(a, DAYS, stride=QUAD), :
        ].astype(BF16)
    mixed = dot(mix_ref[...], columns[...])
    for a in range(QUAD):
        rows_f[pl.ds(a, DAYS, stride=QUAD), :] = mixed[:, a * LANES : (a + 1) * LANES]
    for h in range(N_NARROW):
        out_ref[h ^ turn_out] = rows_f[h * CELLS : (h + 1) * CELLS, :].astype(BF16)


def forward_kernel(
    lon_ref, spread_ref, foot_ref, meta_ref, dir_ref, res_ref, err_ref, send_ref, table, picked, model
):
    table[...] = dot_rows(spread_ref[...], lon_ref[...]).astype(BF16)
    width = 2 * LANES
    cells = lax.broadcasted_iota(I32, (CELLS, width), 0)
    for tile in range(SLOTS // width):
        at = slice(tile * width, (tile + 1) * width)
        sums = [jnp.zeros((1, width), F32)] * RHS
        for k in range(NT):
            picked[...] = dot_rows(table[...], foot_ref[k, at, :])
            mask = cells == meta_ref[8 + k : 9 + k, at].astype(I32)
            for r in range(RHS):
                rows = picked[r * CELLS : (r + 1) * CELLS, :]
                sums[r] = sums[r] + jnp.sum(jnp.where(mask, rows, 0.0), axis=0, keepdims=True)
        model[:, at] = jnp.concatenate(sums, axis=0)
    held_dir = meta_ref[0:8, :] + meta_ref[16:24, :]
    held_res = meta_ref[24:32, :] + meta_ref[32:40, :]
    held_err = meta_ref[12:13, :] + meta_ref[13:14, :]
    modelled = model[...]
    held = jnp.concatenate([modelled, held_dir, held_res, held_err * held_dir], axis=0)
    far = dot_rows(held, held, HIGHEST)
    direction = dir_ref[...]
    own = jnp.concatenate([direction, res_ref[...], err_ref[...] * direction], axis=0)
    near = dot_rows(own, own, HIGHEST)
    gram = jnp.concatenate(
        [
            jnp.zeros((RHS, GRAM_AT), F32),
            far[0:8, 8:16] + near[16:24, 0:8],
            far[8:16, 0:8] + near[0:8, 16:24],
            far[0:8, 16:24] + near[16:24, 8:16],
            far[16:24, 0:8] + near[8:16, 16:24],
            far[0:8, 0:8] + far[0:8, 24:32] + far[24:32, 0:8] + near[16:24, 16:24],
            near[8:16, 8:16],
            jnp.zeros((RHS, LANES - GRAM_AT - 48), F32),
        ],
        axis=1,
    )
    lane = lax.broadcasted_iota(I32, (RHS, LANES), 1)
    for block in range(N_WIDE):
        send_ref[block] = jnp.where(lane < CAP, take_lanes(model, 0, RHS, block), gram)


def gather_kernel(home_ref, slot_ref, dir_ref, err_ref, image_ref, lined):
    lined[...] = jnp.zeros((RHS, SLOTS), F32)
    lane = lax.broadcasted_iota(I32, (RHS, LANES), 1)
    for block in range(N_WIDE):
        add_lanes(lined, 0, RHS, block, jnp.where(lane < CAP, home_ref[block], 0.0))
    high, rest = split_two(lined[...])
    middle, low = split_two(rest)
    parts = jnp.concatenate([high, middle, low], axis=0).astype(BF16)
    placed = dot(parts, slot_matrix(slot_ref[...]))
    image_ref[...] = placed[0:8] + placed[8:16] + placed[16:24] + err_ref[...] * dir_ref[...]


def inverses(matrices):
    row = lax.broadcasted_iota(I32, (RHS, RHS), 0)
    column = lax.broadcasted_iota(I32, (RHS, RHS), 1)
    unit = jnp.where(row == column, 1.0, 0.0)
    state = [jnp.concatenate([m, unit], axis=1) for m in matrices]
    side = lax.broadcasted_iota(I32, (RHS, 2 * RHS), 0)
    for j in range(RHS):
        following = []
        for m in state:
            pivot = m[j : j + 1, :] / m[j : j + 1, j : j + 1]
            following.append(jnp.where(side == j, pivot, m - m[:, j : j + 1] * pivot))
        state = following
    return [m[:, RHS:] for m in state]


def update_kernel(gram_ref, sol_ref, res_ref, dir_ref, image_ref, sol_out, res_out, dir_out):
    total = gram_ref[0]
    for n in range(1, N_NARROW):
        total = total + gram_ref[n]
    block = lambda g: total[:, GRAM_AT + 8 * g : GRAM_AT + 8 * g + 8]
    image_dir, dir_image, image_res, res_image, image_image, res_norm = [block(g) for g in range(6)]
    sym = 0.5 * (image_dir + dir_image)
    sym_inverse, norm_inverse = inverses([sym, res_norm])
    step = dot(sym_inverse, res_norm, HIGHEST)
    step_t = dot(res_norm, sym_inverse, HIGHEST)
    crossed = dot(step_t, image_res, HIGHEST) + dot(res_image, step, HIGHEST)
    squared = dot(dot(step_t, image_image, HIGHEST), step, HIGHEST)
    norm_new = res_norm - crossed + squared
    ratio_t = dot(norm_new, norm_inverse, HIGHEST)
    direction = dir_ref[...]
    sol_out[...] = sol_ref[...] + dot(step_t, direction, HIGHEST)
    residual = res_ref[...] - dot(step_t, image_ref[...], HIGHEST)
    res_out[...] = residual
    dir_out[...] = residual + dot(ratio_t, direction, HIGHEST)


VMEM = pl.BlockSpec(memory_space=pltpu.VMEM)
SMEM = pl.BlockSpec(memory_space=pltpu.SMEM)
HBM = pl.BlockSpec(memory_space=pltpu.HBM)


def call(kernel, places, outs, scratch, flops, moved, out_places=None, limit=VMEM_LIMIT):
    return pl.pallas_call(
        kernel,
        in_specs=places,
        out_specs=out_places or [VMEM] * len(outs),
        out_shape=[jax.ShapeDtypeStruct(shape, dtype) for shape, dtype in outs],
        scratch_shapes=scratch,
        compiler_params=pltpu.CompilerParams(vmem_limit_bytes=limit),
        cost_estimate=pl.CostEstimate(flops=flops, bytes_accessed=moved, transcendentals=0),
    )


def exchange(array, axis, groups=None):
    return lax.all_to_all(
        array, axis, split_axis=0, concat_axis=0, tiled=True, axis_index_groups=groups
    )


BOTH = ("wide", "narrow")
WINDOW_GROUPS = [
    [((h ^ n) * QUAD + q) * N_NARROW + n for n in range(N_NARROW)]
    for h in range(N_NARROW)
    for q in range(QUAD)
]
WINDOW_GROUPS = [sorted(group) for group in WINDOW_GROUPS]
PLANE_GROUPS = [
    [(plane * QUAD + i % QUAD) * N_NARROW + i // QUAD for i in range(N_WIDE)]
    for plane in range(N_NARROW)
]


def on_device(
    solution,
    residual,
    direction,
    error_var,
    footprint,
    tiles,
    window,
    temporal,
    spatial_lat,
    spatial_lon,
):
    errors = error_var.reshape(1, OBS_DEV)
    plane = lax.axis_index("wide") >> 2
    band = lax.axis_index("narrow")
    vmem = lambda shape, dtype: pltpu.VMEM(shape, dtype)
    with jax.named_scope("pack"):
        packed, slot = call(
            pack_kernel,
            [HBM] * 6 + [SMEM],
            [((N_WIDE, PAYLOAD, LANES), BF16), ((1, OBS_DEV), I32)],
            [
                vmem((N_WIDE, PAYLOAD, LANES), BF16),
                vmem((1, OBS_DEV), I32),
                vmem((NT, OBS_DEV), I32),
                vmem((OBS_DEV * NT, LANES), BF16),
                vmem((RHS, OBS_DEV), F32),
                vmem((RHS, OBS_DEV), F32),
                vmem((1, OBS_DEV), F32),
                vmem((OBS_DEV, NT * LANES), BF16),
                vmem((SLOTS, OBS_DEV), BF16),
                vmem((SLOTS, NT * LANES), F32),
                vmem((META, SLOTS), F32),
                pltpu.SemaphoreType.DMA((6,)),
                pltpu.SemaphoreType.DMA((N_WIDE // SEND_BLOCKS,)),
            ],
            2 * SLOTS * OBS_DEV * NT * LANES,
            2 * SLOTS * OBS_DEV,
            [HBM, VMEM],
            VMEM_WHOLE,
        )(
            window.reshape(1, OBS_DEV),
            tiles.T,
            footprint.reshape(OBS_DEV * NT, LANES),
            direction,
            residual,
            errors,
            (band * QUAD).reshape(1),
        )
    with jax.named_scope("route"):
        routed = exchange(packed, "wide")
    with jax.named_scope("adjoint"):
        flux, meta, foot = call(
            adjoint_kernel,
            [VMEM],
            [((ROWS, LANES), BF16), ((META, SLOTS), F32), ((NT, SLOTS, LANES), BF16)],
            [
                vmem((NT, SLOTS, LANES), F32),
                vmem((CELLS, SLOTS), BF16),
                vmem((ROWS, SLOTS), BF16),
                vmem((ROWS, LANES), F32),
            ],
            2 * ROWS * NT * SLOTS * LANES,
            4 * NT * SLOTS * LANES,
        )(routed)
    with jax.named_scope("to_rhs"):
        by_rhs = exchange(flux.reshape(N_NARROW, CELLS, LANES), BOTH, WINDOW_GROUPS)
    with jax.named_scope("lat_mix"):
        lat_mix = (
            spatial_lat.reshape(N_WIDE, QUAD, N_WIDE, QUAD).transpose(1, 0, 3, 2).reshape(LAT, LAT)
        )
        (spread,) = call(
            lat_kernel,
            [SMEM, VMEM, VMEM],
            [((ROWS, LANES), BF16)],
            [vmem((ROWS, LANES), F32), vmem((LAT, DAY_DEV * LANES), BF16)],
            2 * LAT * LAT * DAY_DEV * LANES,
            4 * ROWS * LANES,
        )((plane ^ band).reshape(1), lat_mix, by_rhs)
    with jax.named_scope("to_days"):
        by_day = exchange(spread.reshape(N_WIDE, CHUNK, LANES), BOTH, PLANE_GROUPS)
    with jax.named_scope("day_mix"):
        (timed,) = call(
            day_kernel,
            [SMEM, VMEM, VMEM],
            [((N_NARROW, CELLS, LANES), BF16)],
            [vmem((ROWS, LANES), F32), vmem((DAYS, QUAD * LANES), BF16)],
            2 * DAYS * DAYS * QUAD * LANES,
            4 * ROWS * LANES,
        )(jnp.stack([plane, band]), temporal, by_day.reshape(N_NARROW, CELLS, LANES))
    with jax.named_scope("to_windows"):
        by_window = exchange(timed.reshape(N_WIDE, CHUNK, LANES), "wide")
    with jax.named_scope("forward"):
        (modelled,) = call(
            forward_kernel,
            [VMEM] * 7,
            [((N_WIDE, RHS, LANES), F32)],
            [vmem((ROWS, LANES), BF16), vmem((ROWS, 2 * LANES), F32), vmem((RHS, SLOTS), F32)],
            2 * ROWS * NT * SLOTS * LANES,
            4 * NT * SLOTS * LANES,
        )(
            spatial_lon,
            by_window.reshape(ROWS, LANES),
            foot,
            meta,
            direction,
            residual,
            errors,
        )
    with jax.named_scope("home"):
        home = exchange(modelled, "wide")
    with jax.named_scope("gram_sum"):
        partial = jnp.broadcast_to(home.sum(axis=0)[None], (N_NARROW, RHS, LANES))
        grams = exchange(partial, "narrow")
    with jax.named_scope("image"):
        (image,) = call(
            gather_kernel,
            [VMEM] * 4,
            [((RHS, OBS_DEV), F32)],
            [vmem((RHS, SLOTS), F32)],
            2 * 24 * SLOTS * OBS_DEV,
            4 * SLOTS * RHS,
        )(home, slot, direction, errors)
    with jax.named_scope("update"):
        return tuple(
            call(
                update_kernel,
                [VMEM] * 5,
                [((RHS, OBS_DEV), F32)] * 3,
                [],
                2 * 18 * 8 * 8 * OBS_DEV,
                28 * RHS * OBS_DEV,
            )(grams, solution, residual, direction, image)
        )


def solution(mesh):
    both = BOTH
    in_specs = (
        P(None, both),
        P(None, both),
        P(None, both),
        P(both),
        P(both, None, None),
        P(both, None),
        P(both, None),
        P(),
        P(),
        P(),
    )
    out_specs = (P(None, both), P(None, both), P(None, both))
    return jax.shard_map(
        on_device, mesh=mesh, in_specs=in_specs, out_specs=out_specs, check_vma=False
    )
```

```python
import jax
import jax.numpy as jnp
from jax import lax
from jax.experimental import pallas as pl
from jax.experimental.pallas import tpu as pltpu
from jax.sharding import PartitionSpec as P

F32 = jnp.float32
BF16 = jnp.bfloat16
I32 = jnp.int32
HIGHEST = lax.Precision.HIGHEST
LANES = 128
RHS = 8
NT = 4
N_WIDE = 32
N_NARROW = 8
OBS_DEV = 512
CAP = 40
SLOTS = N_WIDE * CAP
DAY_DEV = 10
DAYS = N_WIDE * DAY_DEV
LAT = 128
CELLS = 160
HALF = CELLS // 2
QUAD = 4
CHUNK = DAY_DEV * QUAD
ROWS = RHS * CELLS
META = 48
PAYLOAD = NT * CAP + 16
GRAM_AT = CAP
SEND_BLOCKS = 8
VMEM_LIMIT = 48 * 1024 * 1024
VMEM_WHOLE = 63 * 1024 * 1024


def dot_rows(left, right, precision=None):
    return lax.dot_general(
        left, right, (((1,), (1,)), ((), ())), precision=precision, preferred_element_type=F32
    )


def dot(left, right, precision=None):
    return lax.dot_general(
        left, right, (((1,), (0,)), ((), ())), precision=precision, preferred_element_type=F32
    )


def lane_window(block):
    start = min(block * CAP // LANES * LANES, SLOTS - 2 * LANES)
    return start, block * CAP - start


def take_lanes(ref, row, rows, block):
    start, shift = lane_window(block)
    part = ref[row : row + rows, start : start + 2 * LANES]
    return pltpu.roll(part, (2 * LANES - shift) % (2 * LANES), 1)[:, :LANES]


def add_lanes(ref, row, rows, block, piece):
    start, shift = lane_window(block)
    wide = jnp.concatenate([piece, jnp.zeros((rows, LANES), F32)], axis=1)
    ref[row : row + rows, start : start + 2 * LANES] += pltpu.roll(wide, shift, 1)


def split_two(value):
    high = value.astype(BF16)
    return high.astype(F32), value - high.astype(F32)


def slot_matrix(slot_row):
    rows = lax.broadcasted_iota(I32, (SLOTS, OBS_DEV), 0)
    return jnp.where(rows == slot_row, 1.0, 0.0).astype(BF16)


def pack_kernel(
    window_hbm,
    tiles_hbm,
    foot_hbm,
    dir_hbm,
    res_hbm,
    err_hbm,
    send_hbm,
    slot_ref,
    send_ref,
    window_ref,
    tiles_ref,
    foot_ref,
    dir_ref,
    res_ref,
    err_ref,
    by_tile,
    pick,
    moved,
    meta,
    sems,
    send_sems,
):
    copies = [
        pltpu.make_async_copy(source, target, sems.at[i])
        for i, (source, target) in enumerate(
            [
                (window_hbm, window_ref),
                (foot_hbm, foot_ref),
                (dir_hbm, dir_ref),
                (res_hbm, res_ref),
                (err_hbm, err_ref),
                (tiles_hbm, tiles_ref),
            ]
        )
    ]
    for copy in copies:
        copy.start()
    earlier = lax.broadcasted_iota(I32, (OBS_DEV, OBS_DEV), 0) < lax.broadcasted_iota(
        I32, (OBS_DEV, OBS_DEV), 1
    )
    earlier = jnp.where(earlier, 1.0, 0.0).astype(BF16)
    copies[0].wait()
    owner = window_ref[...] ^ (lax.axis_index("narrow") * QUAD)
    named = lax.broadcasted_iota(I32, (N_WIDE, OBS_DEV), 0) == owner
    named_f = jnp.where(named, 1.0, 0.0)
    before = dot(named_f.astype(BF16), earlier)
    position = jnp.sum(before * named_f, axis=0, keepdims=True).astype(I32)
    slot = owner * CAP + position
    slot_ref[...] = slot
    pick[...] = slot_matrix(slot)
    group = 2 * LANES
    share = group // NT
    out_row = lax.broadcasted_iota(I32, (group, group), 0)
    in_row = lax.broadcasted_iota(I32, (group, group), 1)
    sort = jnp.where(in_row == out_row % share * NT + out_row // share, 1.0, 0.0).astype(BF16)
    copies[1].wait()
    for g in range(OBS_DEV // share):
        rows = dot(sort, foot_ref[g * group : (g + 1) * group, :]).astype(BF16)
        for k in range(NT):
            by_tile[g * share : (g + 1) * share, k * LANES : (k + 1) * LANES] = rows[
                k * share : (k + 1) * share, :
            ]
    moved[...] = dot(pick[...], by_tile[...])
    for copy in copies[2:]:
        copy.wait()
    tile = tiles_ref[...]
    day, row = tile >> 4, tile & 15
    cell = ((row >> 2) * CHUNK + day * QUAD + (row & 3)).astype(F32)
    dir_high, dir_low = split_two(dir_ref[...])
    res_high, res_low = split_two(res_ref[...])
    err_high, err_low = split_two(err_ref[...])
    zero = jnp.zeros((2, OBS_DEV), F32)
    values = jnp.concatenate(
        [
            dir_high,
            jnp.concatenate([cell, err_high, err_low, zero], axis=0),
            dir_low,
            res_high,
            res_low,
            jnp.zeros((8, OBS_DEV), F32),
        ],
        axis=0,
    ).astype(BF16)
    meta[...] = dot_rows(values, pick[...])
    sends = []
    lane = lax.broadcasted_iota(I32, (16, LANES), 1)
    for block in range(N_WIDE):
        rows = slice(block * CAP, (block + 1) * CAP)
        parts = [moved[rows, k * LANES : (k + 1) * LANES] for k in range(NT)]
        send_ref[block, : NT * CAP, :] = jnp.concatenate(parts, axis=0).astype(BF16)
        groups = [take_lanes(meta, 16 * g, 16, block) for g in range(3)]
        joined = jnp.where(
            lane < CAP,
            groups[0],
            jnp.where(
                lane < 2 * CAP,
                pltpu.roll(groups[1], CAP, 1),
                jnp.where(lane < 3 * CAP, pltpu.roll(groups[2], 2 * CAP, 1), 0.0),
            ),
        )
        send_ref[block, NT * CAP :, :] = joined.astype(BF16)
        if block % SEND_BLOCKS == SEND_BLOCKS - 1:
            part = pl.ds(block + 1 - SEND_BLOCKS, SEND_BLOCKS)
            sends.append(
                pltpu.make_async_copy(
                    send_ref.at[part], send_hbm.at[part], send_sems.at[block // SEND_BLOCKS]
                )
            )
            sends[-1].start()
    for send in sends:
        send.wait()


def half_cell(ids):
    return jnp.where(ids >= HALF, ids - HALF, ids).astype(I32)


def adjoint_kernel(
    recv_ref, flux_ref, meta_ref, foot_ref, rows_f, sides, hot, weighted, total
):
    meta_ref[...] = jnp.zeros((META, SLOTS), F32)
    lane = lax.broadcasted_iota(I32, (16, LANES), 1)
    for block in range(N_WIDE):
        values = recv_ref[block, : NT * CAP, :].astype(F32)
        for k in range(NT):
            rows_f[k, block * CAP : (block + 1) * CAP, :] = values[k * CAP : (k + 1) * CAP, :]
        joined = recv_ref[block, NT * CAP :, :].astype(F32)
        for g in range(3):
            piece = joined if g == 0 else pltpu.roll(joined, LANES - g * CAP, 1)
            add_lanes(meta_ref, 16 * g, 16, block, jnp.where(lane < CAP, piece, 0.0))
    upper = jnp.where(meta_ref[8:16, :] >= HALF, 1.0, 0.0).astype(BF16)
    spread_to = lax.broadcasted_iota(I32, (8, NT * LANES), 1) // LANES
    spread_to = spread_to == lax.broadcasted_iota(I32, (8, NT * LANES), 0)
    sides[...] = lax.dot_general(
        upper,
        jnp.where(spread_to, 1.0, 0.0).astype(BF16),
        (((0,), (0,)), ((), ())),
        preferred_element_type=F32,
    )
    cells = lax.broadcasted_iota(I32, (HALF, SLOTS), 0)
    for k in range(NT):
        is_upper = sides[:, k * LANES : (k + 1) * LANES] > 0.5
        foot = rows_f[k]
        foot_ref[k, :, :LANES] = jnp.where(is_upper, 0.0, foot).astype(BF16)
        foot_ref[k, :, LANES:] = jnp.where(is_upper, foot, 0.0).astype(BF16)
        hot[...] = jnp.where(cells == half_cell(meta_ref[8 + k : 9 + k, :]), 1.0, 0.0).astype(BF16)
        for r in range(RHS):
            row = jnp.broadcast_to(meta_ref[r : r + 1, :], (16, SLOTS)).astype(BF16)
            for t in range(HALF // 16):
                weighted[r * HALF + t * 16 : r * HALF + (t + 1) * 16, :] = (
                    hot[t * 16 : (t + 1) * 16, :] * row
                )
        product = dot(weighted[...], foot_ref[k])
        if k == 0:
            total[...] = product
        else:
            total[...] += product
    for r in range(RHS):
        for side in range(2):
            at = r * CELLS + side * HALF
            flux_ref[at : at + HALF, :] = total[
                r * HALF : (r + 1) * HALF, side * LANES : (side + 1) * LANES
            ].astype(BF16)


def lat_kernel(mix_ref, flux_ref, out_ref, rows_f, columns):
    turn = (lax.axis_index("wide") >> 2) ^ lax.axis_index("narrow")
    for n in range(N_NARROW):
        rows_f[n * CELLS : (n + 1) * CELLS, :] = flux_ref[n ^ turn].astype(F32)
    for a in range(QUAD):
        for d in range(DAY_DEV):
            columns[a * N_WIDE : (a + 1) * N_WIDE, d * LANES : (d + 1) * LANES] = rows_f[
                pl.ds(d * QUAD + a, N_WIDE, stride=CHUNK), :
            ].astype(BF16)
    mixed = dot(mix_ref[...], columns[...])
    for a in range(QUAD):
        for d in range(DAY_DEV):
            rows_f[pl.ds(d * QUAD + a, N_WIDE, stride=CHUNK), :] = mixed[
                a * N_WIDE : (a + 1) * N_WIDE, d * LANES : (d + 1) * LANES
            ]
    out_ref[...] = rows_f[...].astype(BF16)


def day_kernel(mix_ref, flux_ref, out_ref, rows_f, columns):
    turn_in, turn_out = lax.axis_index("wide") >> 2, lax.axis_index("narrow")
    for h in range(N_NARROW):
        rows_f[h * CELLS : (h + 1) * CELLS, :] = flux_ref[h ^ turn_in].astype(F32)
    for a in range(QUAD):
        columns[:, a * LANES : (a + 1) * LANES] = rows_f[
            pl.ds(a, DAYS, stride=QUAD), :
        ].astype(BF16)
    mixed = dot(mix_ref[...], columns[...])
    for a in range(QUAD):
        rows_f[pl.ds(a, DAYS, stride=QUAD), :] = mixed[:, a * LANES : (a + 1) * LANES]
    for h in range(N_NARROW):
        out_ref[h ^ turn_out] = rows_f[h * CELLS : (h + 1) * CELLS, :].astype(BF16)


def forward_kernel(
    lon_ref, spread_ref, foot_ref, meta_ref, dir_ref, res_ref, err_ref, send_ref, table, picked, model
):
    smoothed = dot_rows(spread_ref[...], lon_ref[...])
    for r in range(RHS):
        for side in range(2):
            at = r * CELLS + side * HALF
            table[r * HALF : (r + 1) * HALF, side * LANES : (side + 1) * LANES] = smoothed[
                at : at + HALF, :
            ].astype(BF16)
    width = 2 * LANES
    cells = lax.broadcasted_iota(I32, (HALF, width), 0)
    for tile in range(SLOTS // width):
        at = slice(tile * width, (tile + 1) * width)
        sums = [jnp.zeros((1, width), F32)] * RHS
        for k in range(NT):
            picked[k % 2] = dot_rows(table[...], foot_ref[k, at, :])
            mask = cells == half_cell(meta_ref[8 + k : 9 + k, at])
            for r in range(RHS):
                rows = picked[k % 2, r * HALF : (r + 1) * HALF, :]
                sums[r] = sums[r] + jnp.sum(jnp.where(mask, rows, 0.0), axis=0, keepdims=True)
        model[:, at] = jnp.concatenate(sums, axis=0)
    held_dir = meta_ref[0:8, :] + meta_ref[16:24, :]
    held_res = meta_ref[24:32, :] + meta_ref[32:40, :]
    held_err = meta_ref[12:13, :] + meta_ref[13:14, :]
    modelled = model[...]
    held = jnp.concatenate([modelled, held_dir, held_res, held_err * held_dir], axis=0)
    far = dot_rows(held, held, HIGHEST)
    direction = dir_ref[...]
    own = jnp.concatenate([direction, res_ref[...], err_ref[...] * direction], axis=0)
    near = dot_rows(own, own, HIGHEST)
    gram = jnp.concatenate(
        [
            jnp.zeros((RHS, GRAM_AT), F32),
            far[0:8, 8:16] + near[16:24, 0:8],
            far[8:16, 0:8] + near[0:8, 16:24],
            far[0:8, 16:24] + near[16:24, 8:16],
            far[16:24, 0:8] + near[8:16, 16:24],
            far[0:8, 0:8] + far[0:8, 24:32] + far[24:32, 0:8] + near[16:24, 16:24],
            near[8:16, 8:16],
            jnp.zeros((RHS, LANES - GRAM_AT - 48), F32),
        ],
        axis=1,
    )
    lane = lax.broadcasted_iota(I32, (RHS, LANES), 1)
    for block in range(N_WIDE):
        send_ref[block] = jnp.where(lane < CAP, take_lanes(model, 0, RHS, block), gram)


def gather_kernel(home_ref, slot_ref, dir_ref, err_ref, image_ref, lined):
    lined[...] = jnp.zeros((RHS, SLOTS), F32)
    lane = lax.broadcasted_iota(I32, (RHS, LANES), 1)
    for block in range(N_WIDE):
        add_lanes(lined, 0, RHS, block, jnp.where(lane < CAP, home_ref[block], 0.0))
    high, rest = split_two(lined[...])
    middle, low = split_two(rest)
    parts = jnp.concatenate([high, middle, low], axis=0).astype(BF16)
    placed = dot(parts, slot_matrix(slot_ref[...]))
    image_ref[...] = placed[0:8] + placed[8:16] + placed[16:24] + err_ref[...] * dir_ref[...]


def sum_kernel(home_ref, out_ref):
    total = home_ref[0]
    for block in range(1, N_WIDE):
        total = total + home_ref[block]
    for n in range(N_NARROW):
        out_ref[n] = total


def inverses(matrices):
    row = lax.broadcasted_iota(I32, (RHS, RHS), 0)
    column = lax.broadcasted_iota(I32, (RHS, RHS), 1)
    unit = jnp.where(row == column, 1.0, 0.0)
    state = [jnp.concatenate([m, unit], axis=1) for m in matrices]
    side = lax.broadcasted_iota(I32, (RHS, 2 * RHS), 0)
    for j in range(RHS):
        following = []
        for m in state:
            pivot = m[j : j + 1, :] / m[j : j + 1, j : j + 1]
            following.append(jnp.where(side == j, pivot, m - m[:, j : j + 1] * pivot))
        state = following
    return [m[:, RHS:] for m in state]


def update_kernel(gram_ref, sol_ref, res_ref, dir_ref, image_ref, sol_out, res_out, dir_out):
    total = gram_ref[0]
    for n in range(1, N_NARROW):
        total = total + gram_ref[n]
    block = lambda g: total[:, GRAM_AT + 8 * g : GRAM_AT + 8 * g + 8]
    image_dir, dir_image, image_res, res_image, image_image, res_norm = [block(g) for g in range(6)]
    sym = 0.5 * (image_dir + dir_image)
    sym_inverse, norm_inverse = inverses([sym, res_norm])
    step = dot(sym_inverse, res_norm, HIGHEST)
    step_t = dot(res_norm, sym_inverse, HIGHEST)
    crossed = dot(step_t, image_res, HIGHEST) + dot(res_image, step, HIGHEST)
    squared = dot(dot(step_t, image_image, HIGHEST), step, HIGHEST)
    norm_new = res_norm - crossed + squared
    ratio_t = dot(norm_new, norm_inverse, HIGHEST)
    direction = dir_ref[...]
    sol_out[...] = sol_ref[...] + dot(step_t, direction, HIGHEST)
    residual = res_ref[...] - dot(step_t, image_ref[...], HIGHEST)
    res_out[...] = residual
    dir_out[...] = residual + dot(ratio_t, direction, HIGHEST)


VMEM = pl.BlockSpec(memory_space=pltpu.VMEM)
HBM = pl.BlockSpec(memory_space=pltpu.HBM)


def call(kernel, places, outs, scratch, flops, moved, out_places=None, limit=VMEM_LIMIT):
    return pl.pallas_call(
        kernel,
        in_specs=places,
        out_specs=out_places or [VMEM] * len(outs),
        out_shape=[jax.ShapeDtypeStruct(shape, dtype) for shape, dtype in outs],
        scratch_shapes=scratch,
        compiler_params=pltpu.CompilerParams(vmem_limit_bytes=limit),
        cost_estimate=pl.CostEstimate(flops=flops, bytes_accessed=moved, transcendentals=0),
    )


def exchange(array, axis, groups=None):
    return lax.all_to_all(
        array, axis, split_axis=0, concat_axis=0, tiled=True, axis_index_groups=groups
    )


BOTH = ("wide", "narrow")
WINDOW_GROUPS = [
    [((h ^ n) * QUAD + q) * N_NARROW + n for n in range(N_NARROW)]
    for h in range(N_NARROW)
    for q in range(QUAD)
]
WINDOW_GROUPS = [sorted(group) for group in WINDOW_GROUPS]
PLANE_GROUPS = [
    [(plane * QUAD + i % QUAD) * N_NARROW + i // QUAD for i in range(N_WIDE)]
    for plane in range(N_NARROW)
]


def on_device(
    solution,
    residual,
    direction,
    error_var,
    footprint,
    tiles,
    window,
    temporal,
    spatial_lat,
    spatial_lon,
):
    errors = error_var.reshape(1, OBS_DEV)
    vmem = lambda shape, dtype: pltpu.VMEM(shape, dtype)
    with jax.named_scope("pack"):
        packed, slot = call(
            pack_kernel,
            [HBM] * 6,
            [((N_WIDE, PAYLOAD, LANES), BF16), ((1, OBS_DEV), I32)],
            [
                vmem((N_WIDE, PAYLOAD, LANES), BF16),
                vmem((1, OBS_DEV), I32),
                vmem((NT, OBS_DEV), I32),
                vmem((OBS_DEV * NT, LANES), BF16),
                vmem((RHS, OBS_DEV), F32),
                vmem((RHS, OBS_DEV), F32),
                vmem((1, OBS_DEV), F32),
                vmem((OBS_DEV, NT * LANES), BF16),
                vmem((SLOTS, OBS_DEV), BF16),
                vmem((SLOTS, NT * LANES), F32),
                vmem((META, SLOTS), F32),
                pltpu.SemaphoreType.DMA((6,)),
                pltpu.SemaphoreType.DMA((N_WIDE // SEND_BLOCKS,)),
            ],
            2 * SLOTS * OBS_DEV * NT * LANES,
            2 * SLOTS * OBS_DEV,
            [HBM, VMEM],
            VMEM_WHOLE,
        )(
            window.reshape(1, OBS_DEV),
            tiles.T,
            footprint.reshape(OBS_DEV * NT, LANES),
            direction,
            residual,
            errors,
        )
    with jax.named_scope("route"):
        routed = exchange(packed, "wide")
    with jax.named_scope("adjoint"):
        flux, meta, foot = call(
            adjoint_kernel,
            [VMEM],
            [((ROWS, LANES), BF16), ((META, SLOTS), F32), ((NT, SLOTS, 2 * LANES), BF16)],
            [
                vmem((NT, SLOTS, LANES), F32),
                vmem((SLOTS, NT * LANES), F32),
                vmem((HALF, SLOTS), BF16),
                vmem((ROWS // 2, SLOTS), BF16),
                vmem((ROWS // 2, 2 * LANES), F32),
            ],
            2 * ROWS * NT * SLOTS * LANES,
            4 * NT * SLOTS * LANES,
        )(routed)
    with jax.named_scope("to_rhs"):
        by_rhs = exchange(flux.reshape(N_NARROW, CELLS, LANES), BOTH, WINDOW_GROUPS)
    with jax.named_scope("lat_mix"):
        lat_mix = (
            spatial_lat.reshape(N_WIDE, QUAD, N_WIDE, QUAD).transpose(1, 0, 3, 2).reshape(LAT, LAT)
        )
        (spread,) = call(
            lat_kernel,
            [VMEM, VMEM],
            [((ROWS, LANES), BF16)],
            [vmem((ROWS, LANES), F32), vmem((LAT, DAY_DEV * LANES), BF16)],
            2 * LAT * LAT * DAY_DEV * LANES,
            4 * ROWS * LANES,
        )(lat_mix, by_rhs)
    with jax.named_scope("to_days"):
        by_day = exchange(spread.reshape(N_WIDE, CHUNK, LANES), BOTH, PLANE_GROUPS)
    with jax.named_scope("day_mix"):
        (timed,) = call(
            day_kernel,
            [VMEM, VMEM],
            [((N_NARROW, CELLS, LANES), BF16)],
            [vmem((ROWS, LANES), F32), vmem((DAYS, QUAD * LANES), BF16)],
            2 * DAYS * DAYS * QUAD * LANES,
            4 * ROWS * LANES,
        )(temporal, by_day.reshape(N_NARROW, CELLS, LANES))
    with jax.named_scope("to_windows"):
        by_window = exchange(timed.reshape(N_WIDE, CHUNK, LANES), "wide")
    with jax.named_scope("forward"):
        (modelled,) = call(
            forward_kernel,
            [VMEM] * 7,
            [((N_WIDE, RHS, LANES), F32)],
            [
                vmem((ROWS // 2, 2 * LANES), BF16),
                vmem((2, ROWS // 2, 2 * LANES), F32),
                vmem((RHS, SLOTS), F32),
            ],
            2 * ROWS * NT * SLOTS * LANES,
            4 * NT * SLOTS * LANES,
        )(
            spatial_lon,
            by_window.reshape(ROWS, LANES),
            foot,
            meta,
            direction,
            residual,
            errors,
        )
    with jax.named_scope("home"):
        home = exchange(modelled, "wide")
    with jax.named_scope("gram_sum"):
        (partial,) = call(
            sum_kernel,
            [VMEM],
            [((N_NARROW, RHS, LANES), F32)],
            [],
            N_WIDE * RHS * LANES,
            4 * N_WIDE * RHS * LANES,
        )(home)
        grams = exchange(partial, "narrow")
    with jax.named_scope("image"):
        (image,) = call(
            gather_kernel,
            [VMEM] * 4,
            [((RHS, OBS_DEV), F32)],
            [vmem((RHS, SLOTS), F32)],
            2 * 24 * SLOTS * OBS_DEV,
            4 * SLOTS * RHS,
        )(home, slot, direction, errors)
    with jax.named_scope("update"):
        return tuple(
            call(
                update_kernel,
                [VMEM] * 5,
                [((RHS, OBS_DEV), F32)] * 3,
                [],
                2 * 18 * 8 * 8 * OBS_DEV,
                28 * RHS * OBS_DEV,
            )(grams, solution, residual, direction, image)
        )


def solution(mesh):
    both = BOTH
    in_specs = (
        P(None, both),
        P(None, both),
        P(None, both),
        P(both),
        P(both, None, None),
        P(both, None),
        P(both, None),
        P(),
        P(),
        P(),
    )
    out_specs = (P(None, both), P(None, both), P(None, both))
    return jax.shard_map(
        on_device, mesh=mesh, in_specs=in_specs, out_specs=out_specs, check_vma=False
    )
```

```python
import jax
import jax.numpy as jnp
from jax import lax
from jax.experimental import pallas as pl
from jax.experimental.pallas import tpu as pltpu
from jax.sharding import PartitionSpec as P

F32 = jnp.float32
BF16 = jnp.bfloat16
I32 = jnp.int32
HIGHEST = lax.Precision.HIGHEST
LANES = 128
RHS = 8
NT = 4
N_WIDE = 32
N_NARROW = 8
OBS_DEV = 512
CAP = 40
SLOTS = N_WIDE * CAP
DAY_DEV = 10
DAYS = N_WIDE * DAY_DEV
LAT = 128
CELLS = 160
HALF = CELLS // 2
QUAD = 4
CHUNK = DAY_DEV * QUAD
ROWS = RHS * CELLS
META = 48
PAYLOAD = NT * CAP + 16
GRAM_AT = CAP
SEND_BLOCKS = 8
VMEM_LIMIT = 48 * 1024 * 1024
VMEM_WHOLE = 63 * 1024 * 1024


def dot_rows(left, right, precision=None):
    return lax.dot_general(
        left, right, (((1,), (1,)), ((), ())), precision=precision, preferred_element_type=F32
    )


def dot(left, right, precision=None):
    return lax.dot_general(
        left, right, (((1,), (0,)), ((), ())), precision=precision, preferred_element_type=F32
    )


def lane_window(block):
    start = min(block * CAP // LANES * LANES, SLOTS - 2 * LANES)
    return start, block * CAP - start


def take_lanes(ref, row, rows, block):
    start, shift = lane_window(block)
    part = ref[row : row + rows, start : start + 2 * LANES]
    return pltpu.roll(part, (2 * LANES - shift) % (2 * LANES), 1)[:, :LANES]


def add_lanes(ref, row, rows, block, piece):
    start, shift = lane_window(block)
    wide = jnp.concatenate([piece, jnp.zeros((rows, LANES), F32)], axis=1)
    ref[row : row + rows, start : start + 2 * LANES] += pltpu.roll(wide, shift, 1)


def split_two(value):
    high = value.astype(BF16)
    return high.astype(F32), value - high.astype(F32)


def slot_matrix(slot_row):
    rows = lax.broadcasted_iota(I32, (SLOTS, OBS_DEV), 0)
    return jnp.where(rows == slot_row, 1.0, 0.0).astype(BF16)


def pack_kernel(
    window_hbm,
    tiles_hbm,
    foot_hbm,
    dir_hbm,
    res_hbm,
    err_hbm,
    send_hbm,
    slot_hbm,
    send_ref,
    slot_ref,
    window_ref,
    tiles_ref,
    foot_ref,
    dir_ref,
    res_ref,
    err_ref,
    by_tile,
    pick,
    moved,
    meta,
    sems,
    send_sems,
):
    copies = [
        pltpu.make_async_copy(source, target, sems.at[i])
        for i, (source, target) in enumerate(
            [
                (window_hbm, window_ref),
                (foot_hbm, foot_ref),
                (dir_hbm, dir_ref),
                (res_hbm, res_ref),
                (err_hbm, err_ref),
                (tiles_hbm, tiles_ref),
            ]
        )
    ]
    for copy in copies:
        copy.start()
    earlier = lax.broadcasted_iota(I32, (OBS_DEV, OBS_DEV), 0) < lax.broadcasted_iota(
        I32, (OBS_DEV, OBS_DEV), 1
    )
    earlier = jnp.where(earlier, 1.0, 0.0).astype(BF16)
    copies[0].wait()
    owner = window_ref[...] ^ (lax.axis_index("narrow") * QUAD)
    named = lax.broadcasted_iota(I32, (N_WIDE, OBS_DEV), 0) == owner
    named_f = jnp.where(named, 1.0, 0.0)
    before = dot(named_f.astype(BF16), earlier)
    position = jnp.sum(before * named_f, axis=0, keepdims=True).astype(I32)
    slot = owner * CAP + position
    slot_ref[...] = slot
    slot_copy = pltpu.make_async_copy(slot_ref, slot_hbm, sems.at[6])
    slot_copy.start()
    pick[...] = slot_matrix(slot)
    for copy in copies[2:]:
        copy.wait()
    tile = tiles_ref[...]
    day, row = tile >> 4, tile & 15
    cell = ((row >> 2) * CHUNK + day * QUAD + (row & 3)).astype(F32)
    dir_high, dir_low = split_two(dir_ref[...])
    res_high, res_low = split_two(res_ref[...])
    err_high, err_low = split_two(err_ref[...])
    zero = jnp.zeros((2, OBS_DEV), F32)
    values = jnp.concatenate(
        [
            dir_high,
            jnp.concatenate([cell, err_high, err_low, zero], axis=0),
            dir_low,
            res_high,
            res_low,
            jnp.zeros((8, OBS_DEV), F32),
        ],
        axis=0,
    ).astype(BF16)
    meta[...] = dot_rows(values, pick[...])
    group = 2 * LANES
    share = group // NT
    out_row = lax.broadcasted_iota(I32, (group, group), 0)
    in_row = lax.broadcasted_iota(I32, (group, group), 1)
    sort = jnp.where(in_row == out_row % share * NT + out_row // share, 1.0, 0.0).astype(BF16)
    copies[1].wait()
    for g in range(OBS_DEV // share):
        rows = dot(sort, foot_ref[g * group : (g + 1) * group, :]).astype(BF16)
        for k in range(NT):
            by_tile[g * share : (g + 1) * share, k * LANES : (k + 1) * LANES] = rows[
                k * share : (k + 1) * share, :
            ]
    lane = lax.broadcasted_iota(I32, (16, LANES), 1)
    sends = []
    for first in range(0, N_WIDE, SEND_BLOCKS):
        part = slice(first * CAP, (first + SEND_BLOCKS) * CAP)
        moved[part, :] = dot(pick[part, :], by_tile[...])
        for block in range(first, first + SEND_BLOCKS):
            rows = slice(block * CAP, (block + 1) * CAP)
            parts = [moved[rows, k * LANES : (k + 1) * LANES] for k in range(NT)]
            send_ref[block, : NT * CAP, :] = jnp.concatenate(parts, axis=0).astype(BF16)
            groups = [take_lanes(meta, 16 * g, 16, block) for g in range(3)]
            joined = jnp.where(
                lane < CAP,
                groups[0],
                jnp.where(
                    lane < 2 * CAP,
                    pltpu.roll(groups[1], CAP, 1),
                    jnp.where(lane < 3 * CAP, pltpu.roll(groups[2], 2 * CAP, 1), 0.0),
                ),
            )
            send_ref[block, NT * CAP :, :] = joined.astype(BF16)
        blocks = pl.ds(first, SEND_BLOCKS)
        sends.append(
            pltpu.make_async_copy(
                send_ref.at[blocks], send_hbm.at[blocks], send_sems.at[first // SEND_BLOCKS]
            )
        )
        sends[-1].start()
    slot_copy.wait()
    for send in sends:
        send.wait()


def half_cell(ids):
    return jnp.where(ids >= HALF, ids - HALF, ids).astype(I32)


def adjoint_kernel(
    recv_ref, flux_ref, meta_ref, foot_ref, rows_f, sides, hot, weighted, total
):
    meta_ref[...] = jnp.zeros((META, SLOTS), F32)
    lane = lax.broadcasted_iota(I32, (16, LANES), 1)
    for block in range(N_WIDE):
        values = recv_ref[block, : NT * CAP, :].astype(F32)
        for k in range(NT):
            rows_f[k, block * CAP : (block + 1) * CAP, :] = values[k * CAP : (k + 1) * CAP, :]
        joined = recv_ref[block, NT * CAP :, :].astype(F32)
        for g in range(3):
            piece = joined if g == 0 else pltpu.roll(joined, LANES - g * CAP, 1)
            add_lanes(meta_ref, 16 * g, 16, block, jnp.where(lane < CAP, piece, 0.0))
    upper = jnp.where(meta_ref[8:16, :] >= HALF, 1.0, 0.0).astype(BF16)
    spread_to = lax.broadcasted_iota(I32, (8, NT * LANES), 1) // LANES
    spread_to = spread_to == lax.broadcasted_iota(I32, (8, NT * LANES), 0)
    sides[...] = lax.dot_general(
        upper,
        jnp.where(spread_to, 1.0, 0.0).astype(BF16),
        (((0,), (0,)), ((), ())),
        preferred_element_type=F32,
    )
    cells = lax.broadcasted_iota(I32, (HALF, SLOTS), 0)
    for k in range(NT):
        is_upper = sides[:, k * LANES : (k + 1) * LANES] > 0.5
        foot = rows_f[k]
        foot_ref[k, :, :LANES] = jnp.where(is_upper, 0.0, foot).astype(BF16)
        foot_ref[k, :, LANES:] = jnp.where(is_upper, foot, 0.0).astype(BF16)
        hot[...] = jnp.where(cells == half_cell(meta_ref[8 + k : 9 + k, :]), 1.0, 0.0).astype(BF16)
        for r in range(RHS):
            row = jnp.broadcast_to(meta_ref[r : r + 1, :], (16, SLOTS)).astype(BF16)
            for t in range(HALF // 16):
                weighted[r * HALF + t * 16 : r * HALF + (t + 1) * 16, :] = (
                    hot[t * 16 : (t + 1) * 16, :] * row
                )
        product = dot(weighted[...], foot_ref[k])
        if k == 0:
            total[...] = product
        else:
            total[...] += product
    for r in range(RHS):
        for side in range(2):
            at = r * CELLS + side * HALF
            flux_ref[at : at + HALF, :] = total[
                r * HALF : (r + 1) * HALF, side * LANES : (side + 1) * LANES
            ].astype(BF16)


def lat_kernel(mix_ref, flux_ref, out_ref, rows_f, columns):
    turn = (lax.axis_index("wide") >> 2) ^ lax.axis_index("narrow")
    for n in range(N_NARROW):
        rows_f[n * CELLS : (n + 1) * CELLS, :] = flux_ref[n ^ turn].astype(F32)
    for a in range(QUAD):
        for d in range(DAY_DEV):
            columns[d, pl.ds(a, N_WIDE, stride=QUAD), :] = rows_f[
                pl.ds(d * QUAD + a, N_WIDE, stride=CHUNK), :
            ]
    side_by_side = jnp.concatenate([columns[d].astype(BF16) for d in range(DAY_DEV)], axis=1)
    mixed = dot(mix_ref[...], side_by_side)
    for d in range(DAY_DEV):
        columns[d] = mixed[:, d * LANES : (d + 1) * LANES]
        for a in range(QUAD):
            rows_f[pl.ds(d * QUAD + a, N_WIDE, stride=CHUNK), :] = columns[
                d, pl.ds(a, N_WIDE, stride=QUAD), :
            ]
    out_ref[...] = rows_f[...].astype(BF16)


def day_kernel(mix_ref, flux_ref, out_ref, rows_f, columns):
    turn_in, turn_out = lax.axis_index("wide") >> 2, lax.axis_index("narrow")
    for h in range(N_NARROW):
        rows_f[h * CELLS : (h + 1) * CELLS, :] = flux_ref[h ^ turn_in].astype(F32)
    for a in range(QUAD):
        columns[:, a * LANES : (a + 1) * LANES] = rows_f[
            pl.ds(a, DAYS, stride=QUAD), :
        ].astype(BF16)
    mixed = dot(mix_ref[...], columns[...])
    for a in range(QUAD):
        rows_f[pl.ds(a, DAYS, stride=QUAD), :] = mixed[:, a * LANES : (a + 1) * LANES]
    for h in range(N_NARROW):
        out_ref[h ^ turn_out] = rows_f[h * CELLS : (h + 1) * CELLS, :].astype(BF16)


def forward_kernel(
    lon_ref, spread_ref, foot_ref, meta_ref, dir_ref, res_ref, err_ref, send_ref, table, picked, model
):
    smoothed = dot_rows(spread_ref[...], lon_ref[...])
    for r in range(RHS):
        for side in range(2):
            at = r * CELLS + side * HALF
            table[r * HALF : (r + 1) * HALF, side * LANES : (side + 1) * LANES] = smoothed[
                at : at + HALF, :
            ].astype(BF16)
    width = 2 * LANES
    cells = lax.broadcasted_iota(I32, (HALF, width), 0)
    for tile in range(SLOTS // width):
        at = slice(tile * width, (tile + 1) * width)
        sums = [jnp.zeros((1, width), F32)] * RHS
        for k in range(NT):
            picked[k % 2] = dot_rows(table[...], foot_ref[k, at, :])
            mask = cells == half_cell(meta_ref[8 + k : 9 + k, at])
            for r in range(RHS):
                rows = picked[k % 2, r * HALF : (r + 1) * HALF, :]
                sums[r] = sums[r] + jnp.sum(jnp.where(mask, rows, 0.0), axis=0, keepdims=True)
        model[:, at] = jnp.concatenate(sums, axis=0)
    held_dir = meta_ref[0:8, :] + meta_ref[16:24, :]
    held_res = meta_ref[24:32, :] + meta_ref[32:40, :]
    held_err = meta_ref[12:13, :] + meta_ref[13:14, :]
    modelled = model[...]
    held = jnp.concatenate([modelled, held_dir, held_res, held_err * held_dir], axis=0)
    far = dot_rows(held, held, HIGHEST)
    direction = dir_ref[...]
    own = jnp.concatenate([direction, res_ref[...], err_ref[...] * direction], axis=0)
    near = dot_rows(own, own, HIGHEST)
    gram = jnp.concatenate(
        [
            jnp.zeros((RHS, GRAM_AT), F32),
            far[0:8, 8:16] + near[16:24, 0:8],
            far[8:16, 0:8] + near[0:8, 16:24],
            far[0:8, 16:24] + near[16:24, 8:16],
            far[16:24, 0:8] + near[8:16, 16:24],
            far[0:8, 0:8] + far[0:8, 24:32] + far[24:32, 0:8] + near[16:24, 16:24],
            near[8:16, 8:16],
            jnp.zeros((RHS, LANES - GRAM_AT - 48), F32),
        ],
        axis=1,
    )
    lane = lax.broadcasted_iota(I32, (RHS, LANES), 1)
    for block in range(N_WIDE):
        send_ref[block] = jnp.where(lane < CAP, take_lanes(model, 0, RHS, block), gram)


def sum_kernel(home_ref, out_ref):
    total = home_ref[0]
    for block in range(1, N_WIDE):
        total = total + home_ref[block]
    for n in range(N_NARROW):
        out_ref[n] = total


def inverses(matrices):
    row = lax.broadcasted_iota(I32, (RHS, RHS), 0)
    column = lax.broadcasted_iota(I32, (RHS, RHS), 1)
    unit = jnp.where(row == column, 1.0, 0.0)
    state = [jnp.concatenate([m, unit], axis=1) for m in matrices]
    side = lax.broadcasted_iota(I32, (RHS, 2 * RHS), 0)
    for j in range(RHS):
        following = []
        for m in state:
            pivot = m[j : j + 1, :] / m[j : j + 1, j : j + 1]
            following.append(jnp.where(side == j, pivot, m - m[:, j : j + 1] * pivot))
        state = following
    return [m[:, RHS:] for m in state]


def small_dot(left, right):
    terms = [left[:, k : k + 1] * right[k : k + 1, :] for k in range(RHS)]
    while len(terms) > 1:
        terms = [a + b for a, b in zip(terms[::2], terms[1::2])]
    return terms[0]


def update_kernel(
    gram_ref, home_ref, slot_ref, err_ref, sol_ref, res_ref, dir_ref, sol_out, res_out, dir_out, lined
):
    lined[...] = jnp.zeros((RHS, SLOTS), F32)
    lane = lax.broadcasted_iota(I32, (RHS, LANES), 1)
    for block in range(N_WIDE):
        add_lanes(lined, 0, RHS, block, jnp.where(lane < CAP, home_ref[block], 0.0))
    high, rest = split_two(lined[...])
    middle, low = split_two(rest)
    parts = jnp.concatenate([high, middle, low], axis=0).astype(BF16)
    placed = dot(parts, slot_matrix(slot_ref[...]))
    direction = dir_ref[...]
    image = placed[0:8] + placed[8:16] + placed[16:24] + err_ref[...] * direction
    total = gram_ref[0]
    for n in range(1, N_NARROW):
        total = total + gram_ref[n]
    block = lambda g: total[:, GRAM_AT + 8 * g : GRAM_AT + 8 * g + 8]
    image_dir, dir_image, image_res, res_image, image_image, res_norm = [block(g) for g in range(6)]
    sym = 0.5 * (image_dir + dir_image)
    sym_inverse, norm_inverse = inverses([sym, res_norm])
    step = small_dot(sym_inverse, res_norm)
    step_t = small_dot(res_norm, sym_inverse)
    sol_out[...] = sol_ref[...] + small_dot(step_t, direction)
    residual = res_ref[...] - small_dot(step_t, image)
    res_out[...] = residual
    remaining = res_image - small_dot(step_t, image_image)
    norm_new = res_norm - small_dot(step_t, image_res) - small_dot(remaining, step)
    ratio_t = small_dot(norm_new, norm_inverse)
    dir_out[...] = residual + small_dot(ratio_t, direction)


VMEM = pl.BlockSpec(memory_space=pltpu.VMEM)
HBM = pl.BlockSpec(memory_space=pltpu.HBM)


def call(kernel, places, outs, scratch, flops, moved, out_places=None, limit=VMEM_LIMIT):
    return pl.pallas_call(
        kernel,
        in_specs=places,
        out_specs=out_places or [VMEM] * len(outs),
        out_shape=[jax.ShapeDtypeStruct(shape, dtype) for shape, dtype in outs],
        scratch_shapes=scratch,
        compiler_params=pltpu.CompilerParams(vmem_limit_bytes=limit),
        cost_estimate=pl.CostEstimate(flops=flops, bytes_accessed=moved, transcendentals=0),
    )


def exchange(array, axis, groups=None):
    return lax.all_to_all(
        array, axis, split_axis=0, concat_axis=0, tiled=True, axis_index_groups=groups
    )


BOTH = ("wide", "narrow")
WINDOW_GROUPS = [
    [((h ^ n) * QUAD + q) * N_NARROW + n for n in range(N_NARROW)]
    for h in range(N_NARROW)
    for q in range(QUAD)
]
WINDOW_GROUPS = [sorted(group) for group in WINDOW_GROUPS]
PLANE_GROUPS = [
    [(plane * QUAD + i % QUAD) * N_NARROW + i // QUAD for i in range(N_WIDE)]
    for plane in range(N_NARROW)
]


def on_device(
    solution,
    residual,
    direction,
    error_var,
    footprint,
    tiles,
    window,
    temporal,
    spatial_lat,
    spatial_lon,
):
    errors = error_var.reshape(1, OBS_DEV)
    vmem = lambda shape, dtype: pltpu.VMEM(shape, dtype)
    with jax.named_scope("pack"):
        packed, slot = call(
            pack_kernel,
            [HBM] * 6,
            [((N_WIDE, PAYLOAD, LANES), BF16), ((1, OBS_DEV), I32)],
            [
                vmem((N_WIDE, PAYLOAD, LANES), BF16),
                vmem((1, OBS_DEV), I32),
                vmem((1, OBS_DEV), I32),
                vmem((NT, OBS_DEV), I32),
                vmem((OBS_DEV * NT, LANES), BF16),
                vmem((RHS, OBS_DEV), F32),
                vmem((RHS, OBS_DEV), F32),
                vmem((1, OBS_DEV), F32),
                vmem((OBS_DEV, NT * LANES), BF16),
                vmem((SLOTS, OBS_DEV), BF16),
                vmem((SLOTS, NT * LANES), F32),
                vmem((META, SLOTS), F32),
                pltpu.SemaphoreType.DMA((7,)),
                pltpu.SemaphoreType.DMA((N_WIDE // SEND_BLOCKS,)),
            ],
            2 * SLOTS * OBS_DEV * NT * LANES,
            2 * SLOTS * OBS_DEV,
            [HBM, HBM],
            VMEM_WHOLE,
        )(
            window.reshape(1, OBS_DEV),
            tiles.T,
            footprint.reshape(OBS_DEV * NT, LANES),
            direction,
            residual,
            errors,
        )
    with jax.named_scope("route"):
        routed = exchange(packed, "wide")
    with jax.named_scope("adjoint"):
        flux, meta, foot = call(
            adjoint_kernel,
            [VMEM],
            [((ROWS, LANES), BF16), ((META, SLOTS), F32), ((NT, SLOTS, 2 * LANES), BF16)],
            [
                vmem((NT, SLOTS, LANES), F32),
                vmem((SLOTS, NT * LANES), F32),
                vmem((HALF, SLOTS), BF16),
                vmem((ROWS // 2, SLOTS), BF16),
                vmem((ROWS // 2, 2 * LANES), F32),
            ],
            2 * ROWS * NT * SLOTS * LANES,
            4 * NT * SLOTS * LANES,
        )(routed)
    with jax.named_scope("to_rhs"):
        by_rhs = exchange(flux.reshape(N_NARROW, CELLS, LANES), BOTH, WINDOW_GROUPS)
    with jax.named_scope("lat_mix"):
        (spread,) = call(
            lat_kernel,
            [VMEM, VMEM],
            [((ROWS, LANES), BF16)],
            [vmem((ROWS, LANES), F32), vmem((DAY_DEV, LAT, LANES), F32)],
            2 * LAT * LAT * DAY_DEV * LANES,
            4 * ROWS * LANES,
        )(spatial_lat, by_rhs)
    with jax.named_scope("to_days"):
        by_day = exchange(spread.reshape(N_WIDE, CHUNK, LANES), BOTH, PLANE_GROUPS)
    with jax.named_scope("day_mix"):
        (timed,) = call(
            day_kernel,
            [VMEM, VMEM],
            [((N_NARROW, CELLS, LANES), BF16)],
            [vmem((ROWS, LANES), F32), vmem((DAYS, QUAD * LANES), BF16)],
            2 * DAYS * DAYS * QUAD * LANES,
            4 * ROWS * LANES,
        )(temporal, by_day.reshape(N_NARROW, CELLS, LANES))
    with jax.named_scope("to_windows"):
        by_window = exchange(timed.reshape(N_WIDE, CHUNK, LANES), "wide")
    with jax.named_scope("forward"):
        (modelled,) = call(
            forward_kernel,
            [VMEM] * 7,
            [((N_WIDE, RHS, LANES), F32)],
            [
                vmem((ROWS // 2, 2 * LANES), BF16),
                vmem((2, ROWS // 2, 2 * LANES), F32),
                vmem((RHS, SLOTS), F32),
            ],
            2 * ROWS * NT * SLOTS * LANES,
            4 * NT * SLOTS * LANES,
        )(
            spatial_lon,
            by_window.reshape(ROWS, LANES),
            foot,
            meta,
            direction,
            residual,
            errors,
        )
    with jax.named_scope("home"):
        home = exchange(modelled, "wide")
    with jax.named_scope("gram_sum"):
        (partial,) = call(
            sum_kernel,
            [VMEM],
            [((N_NARROW, RHS, LANES), F32)],
            [],
            N_WIDE * RHS * LANES,
            4 * N_WIDE * RHS * LANES,
        )(home)
        grams = exchange(partial, "narrow")
    with jax.named_scope("update"):
        return tuple(
            call(
                update_kernel,
                [VMEM] * 7,
                [((RHS, OBS_DEV), F32)] * 3,
                [vmem((RHS, SLOTS), F32)],
                2 * 24 * SLOTS * OBS_DEV,
                28 * RHS * OBS_DEV,
            )(grams, home, slot, errors, solution, residual, direction)
        )


def solution(mesh):
    both = BOTH
    in_specs = (
        P(None, both),
        P(None, both),
        P(None, both),
        P(both),
        P(both, None, None),
        P(both, None),
        P(both, None),
        P(),
        P(),
        P(),
    )
    out_specs = (P(None, both), P(None, both), P(None, both))
    return jax.shard_map(
        on_device, mesh=mesh, in_specs=in_specs, out_specs=out_specs, check_vma=False
    )
```

```python
import jax
import jax.numpy as jnp
from jax import lax
from jax.experimental import pallas as pl
from jax.experimental.pallas import tpu as pltpu
from jax.sharding import PartitionSpec as P

F32 = jnp.float32
BF16 = jnp.bfloat16
I32 = jnp.int32
HIGHEST = lax.Precision.HIGHEST
LANES = 128
RHS = 8
NT = 4
N_WIDE = 32
N_NARROW = 8
OBS_DEV = 512
CAP = 40
SLOTS = N_WIDE * CAP
DAY_DEV = 10
DAYS = N_WIDE * DAY_DEV
LAT = 128
CELLS = 160
HALF = CELLS // 2
QUAD = 4
CHUNK = DAY_DEV * QUAD
ROWS = RHS * CELLS
META = 48
PAYLOAD = NT * CAP + 16
GRAM_AT = CAP
SEND_BLOCKS = 8
VMEM_LIMIT = 48 * 1024 * 1024


def dot_rows(left, right, precision=None):
    return lax.dot_general(
        left, right, (((1,), (1,)), ((), ())), precision=precision, preferred_element_type=F32
    )


def dot(left, right, precision=None):
    return lax.dot_general(
        left, right, (((1,), (0,)), ((), ())), precision=precision, preferred_element_type=F32
    )


def here():
    band = lax.axis_index("narrow")
    return lax.axis_index("wide") >> 2, (band & 1) * (N_NARROW // 2) + (band >> 1)


def band_of(turn):
    return (turn & 3) * 2 + (turn >> 2)


def lane_window(block):
    start = min(block * CAP // LANES * LANES, SLOTS - 2 * LANES)
    return start, block * CAP - start


def take_lanes(ref, row, rows, block):
    start, shift = lane_window(block)
    part = ref[row : row + rows, start : start + 2 * LANES]
    return pltpu.roll(part, (2 * LANES - shift) % (2 * LANES), 1)[:, :LANES]


def add_lanes(ref, row, rows, block, piece):
    start, shift = lane_window(block)
    wide = jnp.concatenate([piece, jnp.zeros((rows, LANES), F32)], axis=1)
    ref[row : row + rows, start : start + 2 * LANES] += pltpu.roll(wide, shift, 1)


def split_two(value):
    high = value.astype(BF16)
    return high.astype(F32), value - high.astype(F32)


def slot_matrix(slot_row):
    rows = lax.broadcasted_iota(I32, (SLOTS, OBS_DEV), 0)
    return jnp.where(rows == slot_row, 1.0, 0.0).astype(BF16)


def pack_kernel(
    window_hbm,
    tiles_hbm,
    foot_hbm,
    dir_hbm,
    res_hbm,
    err_hbm,
    send_ref,
    slot_ref,
    window_ref,
    tiles_ref,
    foot_ref,
    dir_ref,
    res_ref,
    err_ref,
    by_tile,
    pick,
    moved,
    meta,
    sems,
):
    copies = [
        pltpu.make_async_copy(source, target, sems.at[i])
        for i, (source, target) in enumerate(
            [
                (window_hbm, window_ref),
                (foot_hbm, foot_ref),
                (dir_hbm, dir_ref),
                (res_hbm, res_ref),
                (err_hbm, err_ref),
                (tiles_hbm, tiles_ref),
            ]
        )
    ]
    for copy in copies:
        copy.start()
    earlier = lax.broadcasted_iota(I32, (OBS_DEV, OBS_DEV), 0) < lax.broadcasted_iota(
        I32, (OBS_DEV, OBS_DEV), 1
    )
    earlier = jnp.where(earlier, 1.0, 0.0).astype(BF16)
    copies[0].wait()
    window = window_ref[...]
    turn = here()[1]
    owner = ((turn - (window >> 2)) & 7) * QUAD + (window & 3)
    named = lax.broadcasted_iota(I32, (N_WIDE, OBS_DEV), 0) == owner
    named_f = jnp.where(named, 1.0, 0.0)
    before = dot(named_f.astype(BF16), earlier)
    position = jnp.sum(before * named_f, axis=0, keepdims=True).astype(I32)
    slot = owner * CAP + position
    slot_ref[...] = slot
    pick[...] = slot_matrix(slot)
    for copy in copies[2:]:
        copy.wait()
    tile = tiles_ref[...]
    day, row = tile >> 4, tile & 15
    cell = ((row >> 2) * CHUNK + day * QUAD + (row & 3)).astype(F32)
    dir_high, dir_low = split_two(dir_ref[...])
    res_high, res_low = split_two(res_ref[...])
    err_high, err_low = split_two(err_ref[...])
    zero = jnp.zeros((2, OBS_DEV), F32)
    values = jnp.concatenate(
        [
            dir_high,
            jnp.concatenate([cell, err_high, err_low, zero], axis=0),
            dir_low,
            res_high,
            res_low,
            jnp.zeros((8, OBS_DEV), F32),
        ],
        axis=0,
    ).astype(BF16)
    meta[...] = dot_rows(values, pick[...])
    group = 2 * LANES
    share = group // NT
    out_row = lax.broadcasted_iota(I32, (group, group), 0)
    in_row = lax.broadcasted_iota(I32, (group, group), 1)
    sort = jnp.where(in_row == out_row % share * NT + out_row // share, 1.0, 0.0).astype(BF16)
    copies[1].wait()
    for g in range(OBS_DEV // share):
        rows = dot(sort, foot_ref[g * group : (g + 1) * group, :]).astype(BF16)
        for k in range(NT):
            by_tile[g * share : (g + 1) * share, k * LANES : (k + 1) * LANES] = rows[
                k * share : (k + 1) * share, :
            ]
    lane = lax.broadcasted_iota(I32, (16, LANES), 1)
    for first in range(0, N_WIDE, SEND_BLOCKS):
        part = slice(first * CAP, (first + SEND_BLOCKS) * CAP)
        moved[part, :] = dot(pick[part, :], by_tile[...])
        for block in range(first, first + SEND_BLOCKS):
            rows = slice(block * CAP, (block + 1) * CAP)
            parts = [moved[rows, k * LANES : (k + 1) * LANES] for k in range(NT)]
            send_ref[block, : NT * CAP, :] = jnp.concatenate(parts, axis=0).astype(BF16)
            groups = [take_lanes(meta, 16 * g, 16, block) for g in range(3)]
            joined = jnp.where(
                lane < CAP,
                groups[0],
                jnp.where(
                    lane < 2 * CAP,
                    pltpu.roll(groups[1], CAP, 1),
                    jnp.where(lane < 3 * CAP, pltpu.roll(groups[2], 2 * CAP, 1), 0.0),
                ),
            )
            send_ref[block, NT * CAP :, :] = joined.astype(BF16)


def half_cell(ids):
    return jnp.where(ids >= HALF, ids - HALF, ids).astype(I32)


def adjoint_kernel(
    recv_ref, flux_ref, meta_ref, foot_ref, rows_f, sides, hot, weighted, total
):
    meta_ref[...] = jnp.zeros((META, SLOTS), F32)
    lane = lax.broadcasted_iota(I32, (16, LANES), 1)
    for block in range(N_WIDE):
        values = recv_ref[block, : NT * CAP, :].astype(F32)
        for k in range(NT):
            rows_f[k, block * CAP : (block + 1) * CAP, :] = values[k * CAP : (k + 1) * CAP, :]
        joined = recv_ref[block, NT * CAP :, :].astype(F32)
        for g in range(3):
            piece = joined if g == 0 else pltpu.roll(joined, LANES - g * CAP, 1)
            add_lanes(meta_ref, 16 * g, 16, block, jnp.where(lane < CAP, piece, 0.0))
    upper = jnp.where(meta_ref[8:16, :] >= HALF, 1.0, 0.0).astype(BF16)
    spread_to = lax.broadcasted_iota(I32, (8, NT * LANES), 1) // LANES
    spread_to = spread_to == lax.broadcasted_iota(I32, (8, NT * LANES), 0)
    sides[...] = lax.dot_general(
        upper,
        jnp.where(spread_to, 1.0, 0.0).astype(BF16),
        (((0,), (0,)), ((), ())),
        preferred_element_type=F32,
    )
    cells = lax.broadcasted_iota(I32, (HALF, SLOTS), 0)
    for k in range(NT):
        is_upper = sides[:, k * LANES : (k + 1) * LANES] > 0.5
        foot = rows_f[k]
        foot_ref[k, :, :LANES] = jnp.where(is_upper, 0.0, foot).astype(BF16)
        foot_ref[k, :, LANES:] = jnp.where(is_upper, foot, 0.0).astype(BF16)
        hot[...] = jnp.where(cells == half_cell(meta_ref[8 + k : 9 + k, :]), 1.0, 0.0).astype(BF16)
        for r in range(RHS):
            row = jnp.broadcast_to(meta_ref[r : r + 1, :], (16, SLOTS)).astype(BF16)
            for t in range(HALF // 16):
                weighted[r * HALF + t * 16 : r * HALF + (t + 1) * 16, :] = (
                    hot[t * 16 : (t + 1) * 16, :] * row
                )
        product = dot(weighted[...], foot_ref[k])
        if k == 0:
            total[...] = product
        else:
            total[...] += product
    plane, turn = here()
    for r in range(RHS):
        for side in range(2):
            at = side * HALF
            flux_ref[(r + turn - plane) & 7, at : at + HALF, :] = total[
                r * HALF : (r + 1) * HALF, side * LANES : (side + 1) * LANES
            ].astype(BF16)


def lat_kernel(mix_ref, flux_ref, out_ref, rows_f, columns):
    for t in range(N_NARROW):
        n = band_of(t)
        rows_f[n * CELLS : (n + 1) * CELLS, :] = flux_ref[t].astype(F32)
    for a in range(QUAD):
        for d in range(DAY_DEV):
            columns[d, pl.ds(a, N_WIDE, stride=QUAD), :] = rows_f[
                pl.ds(d * QUAD + a, N_WIDE, stride=CHUNK), :
            ]
    side_by_side = jnp.concatenate([columns[d].astype(BF16) for d in range(DAY_DEV)], axis=1)
    mixed = dot(mix_ref[...], side_by_side)
    for d in range(DAY_DEV):
        columns[d] = mixed[:, d * LANES : (d + 1) * LANES]
        for a in range(QUAD):
            rows_f[pl.ds(d * QUAD + a, N_WIDE, stride=CHUNK), :] = columns[
                d, pl.ds(a, N_WIDE, stride=QUAD), :
            ]
    out_ref[...] = rows_f[...].astype(BF16)


def day_kernel(mix_ref, flux_ref, out_ref, rows_f, columns):
    plane, turn = here()
    for h in range(N_NARROW):
        rows_f[h * CELLS : (h + 1) * CELLS, :] = flux_ref[band_of((h + plane) & 7)].astype(F32)
    for a in range(QUAD):
        columns[:, a * LANES : (a + 1) * LANES] = rows_f[
            pl.ds(a, DAYS, stride=QUAD), :
        ].astype(BF16)
    mixed = dot(mix_ref[...], columns[...])
    for a in range(QUAD):
        rows_f[pl.ds(a, DAYS, stride=QUAD), :] = mixed[:, a * LANES : (a + 1) * LANES]
    for h in range(N_NARROW):
        out_ref[(turn - h) & 7] = rows_f[h * CELLS : (h + 1) * CELLS, :].astype(BF16)


def forward_kernel(
    lon_ref, spread_ref, foot_ref, meta_ref, dir_ref, res_ref, err_ref, send_ref, table, picked, model
):
    smoothed = dot_rows(spread_ref[...], lon_ref[...])
    for r in range(RHS):
        for side in range(2):
            at = r * CELLS + side * HALF
            table[r * HALF : (r + 1) * HALF, side * LANES : (side + 1) * LANES] = smoothed[
                at : at + HALF, :
            ].astype(BF16)
    width = 2 * LANES
    cells = lax.broadcasted_iota(I32, (HALF, width), 0)
    for tile in range(SLOTS // width):
        at = slice(tile * width, (tile + 1) * width)
        sums = [jnp.zeros((1, width), F32)] * RHS
        for k in range(NT):
            picked[k % 2] = dot_rows(table[...], foot_ref[k, at, :])
            mask = cells == half_cell(meta_ref[8 + k : 9 + k, at])
            for r in range(RHS):
                rows = picked[k % 2, r * HALF : (r + 1) * HALF, :]
                sums[r] = sums[r] + jnp.sum(jnp.where(mask, rows, 0.0), axis=0, keepdims=True)
        model[:, at] = jnp.concatenate(sums, axis=0)
    held_dir = meta_ref[0:8, :] + meta_ref[16:24, :]
    held_res = meta_ref[24:32, :] + meta_ref[32:40, :]
    held_err = meta_ref[12:13, :] + meta_ref[13:14, :]
    modelled = model[...]
    held = jnp.concatenate([modelled, held_dir, held_res, held_err * held_dir], axis=0)
    far = dot_rows(held, held, HIGHEST)
    direction = dir_ref[...]
    own = jnp.concatenate([direction, res_ref[...], err_ref[...] * direction], axis=0)
    near = dot_rows(own, own, HIGHEST)
    gram = jnp.concatenate(
        [
            jnp.zeros((RHS, GRAM_AT), F32),
            far[0:8, 8:16] + near[16:24, 0:8],
            far[8:16, 0:8] + near[0:8, 16:24],
            far[0:8, 16:24] + near[16:24, 8:16],
            far[16:24, 0:8] + near[8:16, 16:24],
            far[0:8, 0:8] + far[0:8, 24:32] + far[24:32, 0:8] + near[16:24, 16:24],
            near[8:16, 8:16],
            jnp.zeros((RHS, LANES - GRAM_AT - 48), F32),
        ],
        axis=1,
    )
    lane = lax.broadcasted_iota(I32, (RHS, LANES), 1)
    for block in range(N_WIDE):
        send_ref[block] = jnp.where(lane < CAP, take_lanes(model, 0, RHS, block), gram)


def sum_kernel(home_ref, out_ref):
    total = home_ref[0]
    for block in range(1, N_WIDE):
        total = total + home_ref[block]
    for n in range(N_NARROW):
        out_ref[n] = total


def inverses(matrices):
    row = lax.broadcasted_iota(I32, (RHS, RHS), 0)
    column = lax.broadcasted_iota(I32, (RHS, RHS), 1)
    unit = jnp.where(row == column, 1.0, 0.0)
    state = [jnp.concatenate([m, unit], axis=1) for m in matrices]
    side = lax.broadcasted_iota(I32, (RHS, 2 * RHS), 0)
    for j in range(RHS):
        following = []
        for m in state:
            pivot = m[j : j + 1, :] / m[j : j + 1, j : j + 1]
            following.append(jnp.where(side == j, pivot, m - m[:, j : j + 1] * pivot))
        state = following
    return [m[:, RHS:] for m in state]


def small_dot(left, right):
    terms = [left[:, k : k + 1] * right[k : k + 1, :] for k in range(RHS)]
    while len(terms) > 1:
        terms = [a + b for a, b in zip(terms[::2], terms[1::2])]
    return terms[0]


def update_kernel(
    gram_ref, home_ref, slot_ref, err_ref, sol_ref, res_ref, dir_ref, sol_out, res_out, dir_out, lined
):
    lined[...] = jnp.zeros((RHS, SLOTS), F32)
    lane = lax.broadcasted_iota(I32, (RHS, LANES), 1)
    for block in range(N_WIDE):
        add_lanes(lined, 0, RHS, block, jnp.where(lane < CAP, home_ref[block], 0.0))
    high, rest = split_two(lined[...])
    middle, low = split_two(rest)
    parts = jnp.concatenate([high, middle, low], axis=0).astype(BF16)
    placed = dot(parts, slot_matrix(slot_ref[...]))
    direction = dir_ref[...]
    image = placed[0:8] + placed[8:16] + placed[16:24] + err_ref[...] * direction
    total = gram_ref[0]
    for n in range(1, N_NARROW):
        total = total + gram_ref[n]
    block = lambda g: total[:, GRAM_AT + 8 * g : GRAM_AT + 8 * g + 8]
    image_dir, dir_image, image_res, res_image, image_image, res_norm = [block(g) for g in range(6)]
    sym = 0.5 * (image_dir + dir_image)
    sym_inverse, norm_inverse = inverses([sym, res_norm])
    step = small_dot(sym_inverse, res_norm)
    step_t = small_dot(res_norm, sym_inverse)
    sol_out[...] = sol_ref[...] + small_dot(step_t, direction)
    residual = res_ref[...] - small_dot(step_t, image)
    res_out[...] = residual
    remaining = res_image - small_dot(step_t, image_image)
    norm_new = res_norm - small_dot(step_t, image_res) - small_dot(remaining, step)
    ratio_t = small_dot(norm_new, norm_inverse)
    dir_out[...] = residual + small_dot(ratio_t, direction)


VMEM = pl.BlockSpec(memory_space=pltpu.VMEM)
HBM = pl.BlockSpec(memory_space=pltpu.HBM)


def in_hbm(array):
    return pltpu.with_memory_space_constraint(array, pltpu.HBM)


def call(kernel, places, outs, scratch, flops, moved):
    return pl.pallas_call(
        kernel,
        in_specs=places,
        out_specs=[VMEM] * len(outs),
        out_shape=[jax.ShapeDtypeStruct(shape, dtype) for shape, dtype in outs],
        scratch_shapes=scratch,
        compiler_params=pltpu.CompilerParams(vmem_limit_bytes=VMEM_LIMIT),
        cost_estimate=pl.CostEstimate(flops=flops, bytes_accessed=moved, transcendentals=0),
    )


def exchange(array, axis, groups=None):
    return lax.all_to_all(
        array, axis, split_axis=0, concat_axis=0, tiled=True, axis_index_groups=groups
    )


BOTH = ("wide", "narrow")
WINDOW_GROUPS = [
    [((turn - h) % N_NARROW * QUAD + q) * N_NARROW + band_of(turn) for turn in range(N_NARROW)]
    for h in range(N_NARROW)
    for q in range(QUAD)
]
PLANE_GROUPS = [
    [(plane * QUAD + i % QUAD) * N_NARROW + i // QUAD for i in range(N_WIDE)]
    for plane in range(N_NARROW)
]


def on_device(
    solution,
    residual,
    direction,
    error_var,
    footprint,
    tiles,
    window,
    temporal,
    spatial_lat,
    spatial_lon,
):
    errors = error_var.reshape(1, OBS_DEV)
    vmem = lambda shape, dtype: pltpu.VMEM(shape, dtype)
    with jax.named_scope("pack"):
        packed, slot = call(
            pack_kernel,
            [HBM] * 6,
            [((N_WIDE, PAYLOAD, LANES), BF16), ((1, OBS_DEV), I32)],
            [
                vmem((1, OBS_DEV), I32),
                vmem((NT, OBS_DEV), I32),
                vmem((OBS_DEV * NT, LANES), BF16),
                vmem((RHS, OBS_DEV), F32),
                vmem((RHS, OBS_DEV), F32),
                vmem((1, OBS_DEV), F32),
                vmem((OBS_DEV, NT * LANES), BF16),
                vmem((SLOTS, OBS_DEV), BF16),
                vmem((SLOTS, NT * LANES), F32),
                vmem((META, SLOTS), F32),
                pltpu.SemaphoreType.DMA((6,)),
            ],
            2 * SLOTS * OBS_DEV * NT * LANES,
            2 * SLOTS * OBS_DEV,
        )(
            in_hbm(window.reshape(1, OBS_DEV)),
            in_hbm(tiles.T),
            in_hbm(footprint.reshape(OBS_DEV * NT, LANES)),
            in_hbm(direction),
            in_hbm(residual),
            in_hbm(errors),
        )
    with jax.named_scope("route"):
        routed = exchange(packed, "wide")
    with jax.named_scope("adjoint"):
        flux, meta, foot = call(
            adjoint_kernel,
            [VMEM],
            [
                ((N_NARROW, CELLS, LANES), BF16),
                ((META, SLOTS), F32),
                ((NT, SLOTS, 2 * LANES), BF16),
            ],
            [
                vmem((NT, SLOTS, LANES), F32),
                vmem((SLOTS, NT * LANES), F32),
                vmem((HALF, SLOTS), BF16),
                vmem((ROWS // 2, SLOTS), BF16),
                vmem((ROWS // 2, 2 * LANES), F32),
            ],
            2 * ROWS * NT * SLOTS * LANES,
            4 * NT * SLOTS * LANES,
        )(routed)
    with jax.named_scope("to_rhs"):
        by_rhs = exchange(flux, BOTH, WINDOW_GROUPS)
    with jax.named_scope("lat_mix"):
        (spread,) = call(
            lat_kernel,
            [VMEM, VMEM],
            [((ROWS, LANES), BF16)],
            [vmem((ROWS, LANES), F32), vmem((DAY_DEV, LAT, LANES), F32)],
            2 * LAT * LAT * DAY_DEV * LANES,
            4 * ROWS * LANES,
        )(spatial_lat, by_rhs)
    with jax.named_scope("to_days"):
        by_day = exchange(spread.reshape(N_WIDE, CHUNK, LANES), BOTH, PLANE_GROUPS)
    with jax.named_scope("day_mix"):
        (timed,) = call(
            day_kernel,
            [VMEM, VMEM],
            [((N_NARROW, CELLS, LANES), BF16)],
            [vmem((ROWS, LANES), F32), vmem((DAYS, QUAD * LANES), BF16)],
            2 * DAYS * DAYS * QUAD * LANES,
            4 * ROWS * LANES,
        )(temporal, by_day.reshape(N_NARROW, CELLS, LANES))
    with jax.named_scope("to_windows"):
        by_window = exchange(timed.reshape(N_WIDE, CHUNK, LANES), "wide")
    with jax.named_scope("forward"):
        (modelled,) = call(
            forward_kernel,
            [VMEM] * 7,
            [((N_WIDE, RHS, LANES), F32)],
            [
                vmem((ROWS // 2, 2 * LANES), BF16),
                vmem((2, ROWS // 2, 2 * LANES), F32),
                vmem((RHS, SLOTS), F32),
            ],
            2 * ROWS * NT * SLOTS * LANES,
            4 * NT * SLOTS * LANES,
        )(
            spatial_lon,
            by_window.reshape(ROWS, LANES),
            foot,
            meta,
            direction,
            residual,
            errors,
        )
    with jax.named_scope("home"):
        home = exchange(modelled, "wide")
    with jax.named_scope("gram_sum"):
        (partial,) = call(
            sum_kernel,
            [VMEM],
            [((N_NARROW, RHS, LANES), F32)],
            [],
            N_WIDE * RHS * LANES,
            4 * N_WIDE * RHS * LANES,
        )(home)
        grams = exchange(partial, "narrow")
    with jax.named_scope("update"):
        return tuple(
            call(
                update_kernel,
                [VMEM] * 7,
                [((RHS, OBS_DEV), F32)] * 3,
                [vmem((RHS, SLOTS), F32)],
                2 * 24 * SLOTS * OBS_DEV,
                28 * RHS * OBS_DEV,
            )(grams, home, slot, errors, solution, residual, direction)
        )


def solution(mesh):
    both = BOTH
    in_specs = (
        P(None, both),
        P(None, both),
        P(None, both),
        P(both),
        P(both, None, None),
        P(both, None),
        P(both, None),
        P(),
        P(),
        P(),
    )
    out_specs = (P(None, both), P(None, both), P(None, both))
    return jax.shard_map(
        on_device, mesh=mesh, in_specs=in_specs, out_specs=out_specs, check_vma=False
    )
```

```python
import jax
import jax.numpy as jnp
from jax import lax
from jax.experimental import pallas as pl
from jax.experimental.pallas import tpu as pltpu
from jax.sharding import PartitionSpec as P

F32 = jnp.float32
BF16 = jnp.bfloat16
I32 = jnp.int32
HIGHEST = lax.Precision.HIGHEST
LANES = 128
RHS = 8
NT = 4
N_WIDE = 32
N_NARROW = 8
OBS_DEV = 512
CAP = 40
SLOTS = N_WIDE * CAP
DAY_DEV = 10
DAYS = N_WIDE * DAY_DEV
LAT = 128
CELLS = 160
HALF = CELLS // 2
QUAD = 4
CHUNK = DAY_DEV * QUAD
ROWS = RHS * CELLS
META = 48
PAYLOAD = NT * CAP + 16
GRAM_AT = CAP
SEND_BLOCKS = 8
VMEM_LIMIT = 48 * 1024 * 1024


def dot_rows(left, right, precision=None):
    return lax.dot_general(
        left, right, (((1,), (1,)), ((), ())), precision=precision, preferred_element_type=F32
    )


def dot(left, right, precision=None):
    return lax.dot_general(
        left, right, (((1,), (0,)), ((), ())), precision=precision, preferred_element_type=F32
    )


def here():
    band = lax.axis_index("narrow")
    return lax.axis_index("wide") >> 2, (band & 1) * (N_NARROW // 2) + (band >> 1)


def band_of(turn):
    return (turn & 3) * 2 + (turn >> 2)


def take_lanes(columns, lane, block, target):
    start = block * CAP
    first = start // LANES
    part = columns[first]
    if (start + CAP - 1) // LANES != first:
        part = jnp.where(lane >= start % LANES, part, columns[first + 1])
    return pltpu.roll(part, (target - start) % LANES, 1)


def join_lanes(pieces, source, lane):
    turned = [
        pltpu.roll(piece, (block * CAP - source) % LANES, 1) for block, piece in enumerate(pieces)
    ]
    columns = []
    for start in range(0, SLOTS, LANES):
        blocks = range(start // CAP, (start + LANES - 1) // CAP + 1)
        column = turned[blocks[-1]]
        for block in reversed(blocks[:-1]):
            column = jnp.where(lane < (block + 1) * CAP - start, turned[block], column)
        columns.append(column)
    return columns


def columns_of(ref, row, rows):
    return [ref[row : row + rows, at : at + LANES] for at in range(0, SLOTS, LANES)]


def split_two(value):
    high = value.astype(BF16)
    return high.astype(F32), value - high.astype(F32)


def slot_matrix(slot_row):
    rows = lax.broadcasted_iota(I32, (SLOTS, OBS_DEV), 0)
    return jnp.where(rows == slot_row, 1.0, 0.0).astype(BF16)


def pack_kernel(
    window_hbm,
    tiles_hbm,
    foot_hbm,
    dir_hbm,
    res_hbm,
    err_hbm,
    send_ref,
    slot_ref,
    window_ref,
    tiles_ref,
    foot_ref,
    dir_ref,
    res_ref,
    err_ref,
    by_tile,
    pick,
    moved,
    meta,
    sems,
):
    copies = [
        pltpu.make_async_copy(source, target, sems.at[i])
        for i, (source, target) in enumerate(
            [
                (window_hbm, window_ref),
                (foot_hbm, foot_ref),
                (dir_hbm, dir_ref),
                (res_hbm, res_ref),
                (err_hbm, err_ref),
                (tiles_hbm, tiles_ref),
            ]
        )
    ]
    for copy in copies:
        copy.start()
    earlier = lax.broadcasted_iota(I32, (OBS_DEV, OBS_DEV), 0) < lax.broadcasted_iota(
        I32, (OBS_DEV, OBS_DEV), 1
    )
    earlier = jnp.where(earlier, 1.0, 0.0).astype(BF16)
    copies[0].wait()
    window = window_ref[...]
    turn = here()[1]
    owner = ((turn - (window >> 2)) & 7) * QUAD + (window & 3)
    named = lax.broadcasted_iota(I32, (N_WIDE, OBS_DEV), 0) == owner
    named_f = jnp.where(named, 1.0, 0.0)
    before = dot(named_f.astype(BF16), earlier)
    position = jnp.sum(before * named_f, axis=0, keepdims=True).astype(I32)
    slot = owner * CAP + position
    slot_ref[...] = slot
    pick[...] = slot_matrix(slot)
    for copy in copies[2:]:
        copy.wait()
    tile = tiles_ref[...]
    day, row = tile >> 4, tile & 15
    cell = ((row >> 2) * CHUNK + day * QUAD + (row & 3)).astype(F32)
    dir_high, dir_low = split_two(dir_ref[...])
    res_high, res_low = split_two(res_ref[...])
    err_high, err_low = split_two(err_ref[...])
    zero = jnp.zeros((2, OBS_DEV), F32)
    values = jnp.concatenate(
        [
            dir_high,
            jnp.concatenate([cell, err_high, err_low, zero], axis=0),
            dir_low,
            res_high,
            res_low,
            jnp.zeros((8, OBS_DEV), F32),
        ],
        axis=0,
    ).astype(BF16)
    meta[...] = dot_rows(values, pick[...])
    group = 2 * LANES
    share = group // NT
    out_row = lax.broadcasted_iota(I32, (group, group), 0)
    in_row = lax.broadcasted_iota(I32, (group, group), 1)
    sort = jnp.where(in_row == out_row % share * NT + out_row // share, 1.0, 0.0).astype(BF16)
    copies[1].wait()
    for g in range(OBS_DEV // share):
        rows = dot(sort, foot_ref[g * group : (g + 1) * group, :]).astype(BF16)
        for k in range(NT):
            by_tile[g * share : (g + 1) * share, k * LANES : (k + 1) * LANES] = rows[
                k * share : (k + 1) * share, :
            ]
    lane = lax.broadcasted_iota(I32, (16, LANES), 1)
    groups = [columns_of(meta, 16 * g, 16) for g in range(3)]
    for first in range(0, N_WIDE, SEND_BLOCKS):
        part = slice(first * CAP, (first + SEND_BLOCKS) * CAP)
        moved[part, :] = dot(pick[part, :], by_tile[...])
        for block in range(first, first + SEND_BLOCKS):
            rows = slice(block * CAP, (block + 1) * CAP)
            parts = [moved[rows, k * LANES : (k + 1) * LANES] for k in range(NT)]
            send_ref[block, : NT * CAP, :] = jnp.concatenate(parts, axis=0).astype(BF16)
            parts = [take_lanes(groups[g], lane, block, g * CAP) for g in range(3)]
            joined = jnp.where(lane < CAP, parts[0], jnp.where(lane < 2 * CAP, parts[1], parts[2]))
            send_ref[block, NT * CAP :, :] = joined.astype(BF16)


def half_cell(ids):
    return jnp.where(ids >= HALF, ids - HALF, ids).astype(I32)


def adjoint_kernel(
    recv_ref, flux_ref, meta_ref, foot_ref, rows_f, sides, hot, weighted, total
):
    lane = lax.broadcasted_iota(I32, (16, LANES), 1)
    joined = [recv_ref[block, NT * CAP :, :].astype(F32) for block in range(N_WIDE)]
    for g in range(3):
        for c, column in enumerate(join_lanes(joined, g * CAP, lane)):
            meta_ref[16 * g : 16 * (g + 1), c * LANES : (c + 1) * LANES] = column
    for block in range(N_WIDE):
        values = recv_ref[block, : NT * CAP, :].astype(F32)
        for k in range(NT):
            rows_f[k, block * CAP : (block + 1) * CAP, :] = values[k * CAP : (k + 1) * CAP, :]
    upper = jnp.where(meta_ref[8:16, :] >= HALF, 1.0, 0.0).astype(BF16)
    spread_to = lax.broadcasted_iota(I32, (8, NT * LANES), 1) // LANES
    spread_to = spread_to == lax.broadcasted_iota(I32, (8, NT * LANES), 0)
    sides[...] = lax.dot_general(
        upper,
        jnp.where(spread_to, 1.0, 0.0).astype(BF16),
        (((0,), (0,)), ((), ())),
        preferred_element_type=F32,
    )
    cells = lax.broadcasted_iota(I32, (HALF, SLOTS), 0)
    for k in range(NT):
        is_upper = sides[:, k * LANES : (k + 1) * LANES] > 0.5
        foot = rows_f[k]
        foot_ref[k, :, :LANES] = jnp.where(is_upper, 0.0, foot).astype(BF16)
        foot_ref[k, :, LANES:] = jnp.where(is_upper, foot, 0.0).astype(BF16)
        hot[...] = jnp.where(cells == half_cell(meta_ref[8 + k : 9 + k, :]), 1.0, 0.0).astype(BF16)
        for r in range(RHS):
            row = jnp.broadcast_to(meta_ref[r : r + 1, :], (16, SLOTS)).astype(BF16)
            for t in range(HALF // 16):
                weighted[r * HALF + t * 16 : r * HALF + (t + 1) * 16, :] = (
                    hot[t * 16 : (t + 1) * 16, :] * row
                )
        product = dot(weighted[...], foot_ref[k])
        if k == 0:
            total[...] = product
        else:
            total[...] += product
    plane, turn = here()
    for r in range(RHS):
        for side in range(2):
            at = side * HALF
            flux_ref[(r + turn - plane) & 7, at : at + HALF, :] = total[
                r * HALF : (r + 1) * HALF, side * LANES : (side + 1) * LANES
            ].astype(BF16)


def lat_kernel(mix_ref, flux_ref, out_ref, rows_f, columns):
    for t in range(N_NARROW):
        n = band_of(t)
        rows_f[n * CELLS : (n + 1) * CELLS, :] = flux_ref[t].astype(F32)
    for a in range(QUAD):
        for d in range(DAY_DEV):
            columns[d, pl.ds(a, N_WIDE, stride=QUAD), :] = rows_f[
                pl.ds(d * QUAD + a, N_WIDE, stride=CHUNK), :
            ]
    side_by_side = jnp.concatenate([columns[d].astype(BF16) for d in range(DAY_DEV)], axis=1)
    mixed = dot(mix_ref[...], side_by_side)
    for d in range(DAY_DEV):
        columns[d] = mixed[:, d * LANES : (d + 1) * LANES]
        for a in range(QUAD):
            rows_f[pl.ds(d * QUAD + a, N_WIDE, stride=CHUNK), :] = columns[
                d, pl.ds(a, N_WIDE, stride=QUAD), :
            ]
    out_ref[...] = rows_f[...].astype(BF16)


def day_kernel(mix_ref, flux_ref, out_ref, rows_f, columns):
    plane, turn = here()
    for h in range(N_NARROW):
        rows_f[h * CELLS : (h + 1) * CELLS, :] = flux_ref[band_of((h + plane) & 7)].astype(F32)
    for a in range(QUAD):
        columns[:, a * LANES : (a + 1) * LANES] = rows_f[
            pl.ds(a, DAYS, stride=QUAD), :
        ].astype(BF16)
    mixed = dot(mix_ref[...], columns[...])
    for a in range(QUAD):
        rows_f[pl.ds(a, DAYS, stride=QUAD), :] = mixed[:, a * LANES : (a + 1) * LANES]
    for h in range(N_NARROW):
        out_ref[(turn - h) & 7] = rows_f[h * CELLS : (h + 1) * CELLS, :].astype(BF16)


def forward_kernel(
    lon_ref, spread_ref, foot_ref, meta_ref, dir_ref, res_ref, err_ref, send_ref, table, picked, model
):
    smoothed = dot_rows(spread_ref[...], lon_ref[...])
    for r in range(RHS):
        for side in range(2):
            at = r * CELLS + side * HALF
            table[r * HALF : (r + 1) * HALF, side * LANES : (side + 1) * LANES] = smoothed[
                at : at + HALF, :
            ].astype(BF16)
    width = 2 * LANES
    cells = lax.broadcasted_iota(I32, (HALF, width), 0)
    for tile in range(SLOTS // width):
        at = slice(tile * width, (tile + 1) * width)
        sums = [jnp.zeros((1, width), F32)] * RHS
        for k in range(NT):
            picked[k % 2] = dot_rows(table[...], foot_ref[k, at, :])
            mask = cells == half_cell(meta_ref[8 + k : 9 + k, at])
            for r in range(RHS):
                rows = picked[k % 2, r * HALF : (r + 1) * HALF, :]
                sums[r] = sums[r] + jnp.sum(jnp.where(mask, rows, 0.0), axis=0, keepdims=True)
        model[:, at] = jnp.concatenate(sums, axis=0)
    held_dir = meta_ref[0:8, :] + meta_ref[16:24, :]
    held_res = meta_ref[24:32, :] + meta_ref[32:40, :]
    held_err = meta_ref[12:13, :] + meta_ref[13:14, :]
    modelled = model[...]
    held = jnp.concatenate([modelled, held_dir, held_res, held_err * held_dir], axis=0)
    far = dot_rows(held, held, HIGHEST)
    direction = dir_ref[...]
    own = jnp.concatenate([direction, res_ref[...], err_ref[...] * direction], axis=0)
    near = dot_rows(own, own, HIGHEST)
    gram = jnp.concatenate(
        [
            jnp.zeros((RHS, GRAM_AT), F32),
            far[0:8, 8:16] + near[16:24, 0:8],
            far[8:16, 0:8] + near[0:8, 16:24],
            far[0:8, 16:24] + near[16:24, 8:16],
            far[16:24, 0:8] + near[8:16, 16:24],
            far[0:8, 0:8] + far[0:8, 24:32] + far[24:32, 0:8] + near[16:24, 16:24],
            near[8:16, 8:16],
            jnp.zeros((RHS, LANES - GRAM_AT - 48), F32),
        ],
        axis=1,
    )
    lane = lax.broadcasted_iota(I32, (RHS, LANES), 1)
    columns = columns_of(model, 0, RHS)
    for block in range(N_WIDE):
        send_ref[block] = jnp.where(lane < CAP, take_lanes(columns, lane, block, 0), gram)


def sum_kernel(home_ref, out_ref):
    total = home_ref[0]
    for block in range(1, N_WIDE):
        total = total + home_ref[block]
    for n in range(N_NARROW):
        out_ref[n] = total


def inverses(matrices):
    row = lax.broadcasted_iota(I32, (RHS, RHS), 0)
    column = lax.broadcasted_iota(I32, (RHS, RHS), 1)
    unit = jnp.where(row == column, 1.0, 0.0)
    state = [jnp.concatenate([m, unit], axis=1) for m in matrices]
    side = lax.broadcasted_iota(I32, (RHS, 2 * RHS), 0)
    for j in range(RHS):
        following = []
        for m in state:
            pivot = m[j : j + 1, :] / m[j : j + 1, j : j + 1]
            following.append(jnp.where(side == j, pivot, m - m[:, j : j + 1] * pivot))
        state = following
    return [m[:, RHS:] for m in state]


def small_dot(left, right):
    terms = [left[:, k : k + 1] * right[k : k + 1, :] for k in range(RHS)]
    while len(terms) > 1:
        terms = [a + b for a, b in zip(terms[::2], terms[1::2])]
    return terms[0]


def update_kernel(
    gram_ref, home_ref, slot_ref, err_ref, sol_ref, res_ref, dir_ref, sol_out, res_out, dir_out
):
    lane = lax.broadcasted_iota(I32, (RHS, LANES), 1)
    pieces = [home_ref[block] for block in range(N_WIDE)]
    high, rest = split_two(jnp.concatenate(join_lanes(pieces, 0, lane), axis=1))
    middle, low = split_two(rest)
    parts = jnp.concatenate([high, middle, low], axis=0).astype(BF16)
    placed = dot(parts, slot_matrix(slot_ref[...]))
    direction = dir_ref[...]
    image = placed[0:8] + placed[8:16] + placed[16:24] + err_ref[...] * direction
    total = gram_ref[0]
    for n in range(1, N_NARROW):
        total = total + gram_ref[n]
    block = lambda g: total[:, GRAM_AT + 8 * g : GRAM_AT + 8 * g + 8]
    image_dir, dir_image, image_res, res_image, image_image, res_norm = [block(g) for g in range(6)]
    sym = 0.5 * (image_dir + dir_image)
    sym_inverse, norm_inverse = inverses([sym, res_norm])
    step = small_dot(sym_inverse, res_norm)
    step_t = small_dot(res_norm, sym_inverse)
    sol_out[...] = sol_ref[...] + small_dot(step_t, direction)
    residual = res_ref[...] - small_dot(step_t, image)
    res_out[...] = residual
    remaining = res_image - small_dot(step_t, image_image)
    norm_new = res_norm - small_dot(step_t, image_res) - small_dot(remaining, step)
    ratio_t = small_dot(norm_new, norm_inverse)
    dir_out[...] = residual + small_dot(ratio_t, direction)


VMEM = pl.BlockSpec(memory_space=pltpu.VMEM)
HBM = pl.BlockSpec(memory_space=pltpu.HBM)


def in_hbm(array):
    return pltpu.with_memory_space_constraint(array, pltpu.HBM)


def call(kernel, places, outs, scratch, flops, moved):
    return pl.pallas_call(
        kernel,
        in_specs=places,
        out_specs=[VMEM] * len(outs),
        out_shape=[jax.ShapeDtypeStruct(shape, dtype) for shape, dtype in outs],
        scratch_shapes=scratch,
        compiler_params=pltpu.CompilerParams(vmem_limit_bytes=VMEM_LIMIT),
        cost_estimate=pl.CostEstimate(flops=flops, bytes_accessed=moved, transcendentals=0),
    )


def exchange(array, axis, groups=None):
    return lax.all_to_all(
        array, axis, split_axis=0, concat_axis=0, tiled=True, axis_index_groups=groups
    )


BOTH = ("wide", "narrow")
WINDOW_GROUPS = [
    [((turn - h) % N_NARROW * QUAD + q) * N_NARROW + band_of(turn) for turn in range(N_NARROW)]
    for h in range(N_NARROW)
    for q in range(QUAD)
]
PLANE_GROUPS = [
    [(plane * QUAD + i % QUAD) * N_NARROW + i // QUAD for i in range(N_WIDE)]
    for plane in range(N_NARROW)
]


def on_device(
    solution,
    residual,
    direction,
    error_var,
    footprint,
    tiles,
    window,
    temporal,
    spatial_lat,
    spatial_lon,
):
    errors = error_var.reshape(1, OBS_DEV)
    vmem = lambda shape, dtype: pltpu.VMEM(shape, dtype)
    with jax.named_scope("pack"):
        packed, slot = call(
            pack_kernel,
            [HBM] * 6,
            [((N_WIDE, PAYLOAD, LANES), BF16), ((1, OBS_DEV), I32)],
            [
                vmem((1, OBS_DEV), I32),
                vmem((NT, OBS_DEV), I32),
                vmem((OBS_DEV * NT, LANES), BF16),
                vmem((RHS, OBS_DEV), F32),
                vmem((RHS, OBS_DEV), F32),
                vmem((1, OBS_DEV), F32),
                vmem((OBS_DEV, NT * LANES), BF16),
                vmem((SLOTS, OBS_DEV), BF16),
                vmem((SLOTS, NT * LANES), F32),
                vmem((META, SLOTS), F32),
                pltpu.SemaphoreType.DMA((6,)),
            ],
            2 * SLOTS * OBS_DEV * NT * LANES,
            2 * SLOTS * OBS_DEV,
        )(
            in_hbm(window.reshape(1, OBS_DEV)),
            in_hbm(tiles.T),
            in_hbm(footprint.reshape(OBS_DEV * NT, LANES)),
            in_hbm(direction),
            in_hbm(residual),
            in_hbm(errors),
        )
    with jax.named_scope("route"):
        routed = exchange(packed, "wide")
    with jax.named_scope("adjoint"):
        flux, meta, foot = call(
            adjoint_kernel,
            [VMEM],
            [
                ((N_NARROW, CELLS, LANES), BF16),
                ((META, SLOTS), F32),
                ((NT, SLOTS, 2 * LANES), BF16),
            ],
            [
                vmem((NT, SLOTS, LANES), F32),
                vmem((SLOTS, NT * LANES), F32),
                vmem((HALF, SLOTS), BF16),
                vmem((ROWS // 2, SLOTS), BF16),
                vmem((ROWS // 2, 2 * LANES), F32),
            ],
            2 * ROWS * NT * SLOTS * LANES,
            4 * NT * SLOTS * LANES,
        )(routed)
    with jax.named_scope("to_rhs"):
        by_rhs = exchange(flux, BOTH, WINDOW_GROUPS)
    with jax.named_scope("lat_mix"):
        (spread,) = call(
            lat_kernel,
            [VMEM, VMEM],
            [((ROWS, LANES), BF16)],
            [vmem((ROWS, LANES), F32), vmem((DAY_DEV, LAT, LANES), F32)],
            2 * LAT * LAT * DAY_DEV * LANES,
            4 * ROWS * LANES,
        )(spatial_lat, by_rhs)
    with jax.named_scope("to_days"):
        by_day = exchange(spread.reshape(N_WIDE, CHUNK, LANES), BOTH, PLANE_GROUPS)
    with jax.named_scope("day_mix"):
        (timed,) = call(
            day_kernel,
            [VMEM, VMEM],
            [((N_NARROW, CELLS, LANES), BF16)],
            [vmem((ROWS, LANES), F32), vmem((DAYS, QUAD * LANES), BF16)],
            2 * DAYS * DAYS * QUAD * LANES,
            4 * ROWS * LANES,
        )(temporal, by_day.reshape(N_NARROW, CELLS, LANES))
    with jax.named_scope("to_windows"):
        by_window = exchange(timed.reshape(N_WIDE, CHUNK, LANES), "wide")
    with jax.named_scope("forward"):
        (modelled,) = call(
            forward_kernel,
            [VMEM] * 7,
            [((N_WIDE, RHS, LANES), F32)],
            [
                vmem((ROWS // 2, 2 * LANES), BF16),
                vmem((2, ROWS // 2, 2 * LANES), F32),
                vmem((RHS, SLOTS), F32),
            ],
            2 * ROWS * NT * SLOTS * LANES,
            4 * NT * SLOTS * LANES,
        )(
            spatial_lon,
            by_window.reshape(ROWS, LANES),
            foot,
            meta,
            direction,
            residual,
            errors,
        )
    with jax.named_scope("home"):
        home = exchange(modelled, "wide")
    with jax.named_scope("gram_sum"):
        (partial,) = call(
            sum_kernel,
            [VMEM],
            [((N_NARROW, RHS, LANES), F32)],
            [],
            N_WIDE * RHS * LANES,
            4 * N_WIDE * RHS * LANES,
        )(home)
        grams = exchange(partial, "narrow")
    with jax.named_scope("update"):
        return tuple(
            call(
                update_kernel,
                [VMEM] * 7,
                [((RHS, OBS_DEV), F32)] * 3,
                [],
                2 * 24 * SLOTS * OBS_DEV,
                28 * RHS * OBS_DEV,
            )(grams, home, slot, errors, solution, residual, direction)
        )


def solution(mesh):
    both = BOTH
    in_specs = (
        P(None, both),
        P(None, both),
        P(None, both),
        P(both),
        P(both, None, None),
        P(both, None),
        P(both, None),
        P(),
        P(),
        P(),
    )
    out_specs = (P(None, both), P(None, both), P(None, both))
    return jax.shard_map(
        on_device, mesh=mesh, in_specs=in_specs, out_specs=out_specs, check_vma=False
    )
```

```python
import jax
import jax.numpy as jnp
from jax import lax
from jax.experimental import pallas as pl
from jax.experimental.pallas import tpu as pltpu
from jax.sharding import PartitionSpec as P

F32 = jnp.float32
BF16 = jnp.bfloat16
I32 = jnp.int32
HIGHEST = lax.Precision.HIGHEST
LANES = 128
RHS = 8
NT = 4
N_WIDE = 32
N_NARROW = 8
OBS_DEV = 512
CAP = 40
SLOTS = N_WIDE * CAP
DAY_DEV = 10
DAYS = N_WIDE * DAY_DEV
LAT = 128
CELLS = 160
HALF = CELLS // 2
QUAD = 4
CHUNK = DAY_DEV * QUAD
ROWS = RHS * CELLS
META = 48
PAYLOAD = NT * CAP + 16
GRAM_AT = CAP
SEND_BLOCKS = 8
VMEM_LIMIT = 48 * 1024 * 1024


def dot_rows(left, right, precision=None):
    return lax.dot_general(
        left, right, (((1,), (1,)), ((), ())), precision=precision, preferred_element_type=F32
    )


def dot(left, right, precision=None):
    return lax.dot_general(
        left, right, (((1,), (0,)), ((), ())), precision=precision, preferred_element_type=F32
    )


def here():
    band = lax.axis_index("narrow")
    return lax.axis_index("wide") >> 2, (band & 1) * (N_NARROW // 2) + (band >> 1)


def band_of(turn):
    return (turn & 3) * 2 + (turn >> 2)


def take_lanes(columns, lane, block, target):
    start = block * CAP
    first = start // LANES
    part = columns[first]
    if (start + CAP - 1) // LANES != first:
        part = jnp.where(lane >= start % LANES, part, columns[first + 1])
    return pltpu.roll(part, (target - start) % LANES, 1)


def join_lanes(pieces, source, lane):
    turned = [
        pltpu.roll(piece, (block * CAP - source) % LANES, 1) for block, piece in enumerate(pieces)
    ]
    columns = []
    for start in range(0, SLOTS, LANES):
        blocks = range(start // CAP, (start + LANES - 1) // CAP + 1)
        column = turned[blocks[-1]]
        for block in reversed(blocks[:-1]):
            column = jnp.where(lane < (block + 1) * CAP - start, turned[block], column)
        columns.append(column)
    return columns


def columns_of(ref, row, rows):
    return [ref[row : row + rows, at : at + LANES] for at in range(0, SLOTS, LANES)]


def split_two(value):
    high = value.astype(BF16)
    return high.astype(F32), value - high.astype(F32)


def slot_matrix(slot_row):
    rows = lax.broadcasted_iota(I32, (SLOTS, OBS_DEV), 0)
    return jnp.where(rows == slot_row, 1.0, 0.0).astype(BF16)


def pack_kernel(
    window_hbm,
    tiles_hbm,
    foot_hbm,
    dir_hbm,
    res_hbm,
    err_hbm,
    send_ref,
    slot_ref,
    window_ref,
    tiles_ref,
    foot_ref,
    dir_ref,
    res_ref,
    err_ref,
    by_tile,
    pick,
    moved,
    meta,
    sems,
):
    copies = [
        pltpu.make_async_copy(source, target, sems.at[i])
        for i, (source, target) in enumerate(
            [
                (window_hbm, window_ref),
                (foot_hbm, foot_ref),
                (dir_hbm, dir_ref),
                (res_hbm, res_ref),
                (err_hbm, err_ref),
                (tiles_hbm, tiles_ref),
            ]
        )
    ]
    for copy in copies:
        copy.start()
    earlier = lax.broadcasted_iota(I32, (OBS_DEV, OBS_DEV), 0) < lax.broadcasted_iota(
        I32, (OBS_DEV, OBS_DEV), 1
    )
    earlier = jnp.where(earlier, 1.0, 0.0).astype(BF16)
    for copy in copies:
        copy.wait()
    window = window_ref[...]
    turn = here()[1]
    owner = ((turn - (window >> 2)) & 7) * QUAD + (window & 3)
    named = lax.broadcasted_iota(I32, (N_WIDE, OBS_DEV), 0) == owner
    named_f = jnp.where(named, 1.0, 0.0)
    before = dot(named_f.astype(BF16), earlier)
    position = jnp.sum(before * named_f, axis=0, keepdims=True).astype(I32)
    slot = owner * CAP + position
    slot_ref[...] = slot
    pick[...] = slot_matrix(slot)
    tile = tiles_ref[...]
    day, row = tile >> 4, tile & 15
    cell = ((row >> 2) * CHUNK + day * QUAD + (row & 3)).astype(F32)
    dir_high, dir_low = split_two(dir_ref[...])
    res_high, res_low = split_two(res_ref[...])
    err_high, err_low = split_two(err_ref[...])
    zero = jnp.zeros((2, OBS_DEV), F32)
    values = jnp.concatenate(
        [
            dir_high,
            jnp.concatenate([cell, err_high, err_low, zero], axis=0),
            dir_low,
            res_high,
            res_low,
            jnp.zeros((8, OBS_DEV), F32),
        ],
        axis=0,
    ).astype(BF16)
    meta[...] = dot_rows(values, pick[...])
    group = 2 * LANES
    share = group // NT
    out_row = lax.broadcasted_iota(I32, (group, group), 0)
    in_row = lax.broadcasted_iota(I32, (group, group), 1)
    sort = jnp.where(in_row == out_row % share * NT + out_row // share, 1.0, 0.0).astype(BF16)
    for g in range(OBS_DEV // share):
        rows = dot(sort, foot_ref[g * group : (g + 1) * group, :]).astype(BF16)
        for k in range(NT):
            by_tile[g * share : (g + 1) * share, k * LANES : (k + 1) * LANES] = rows[
                k * share : (k + 1) * share, :
            ]
    lane = lax.broadcasted_iota(I32, (16, LANES), 1)
    groups = [columns_of(meta, 16 * g, 16) for g in range(3)]
    for first in range(0, N_WIDE, SEND_BLOCKS):
        part = slice(first * CAP, (first + SEND_BLOCKS) * CAP)
        moved[part, :] = dot(pick[part, :], by_tile[...])
        for block in range(first, first + SEND_BLOCKS):
            rows = slice(block * CAP, (block + 1) * CAP)
            parts = [moved[rows, k * LANES : (k + 1) * LANES] for k in range(NT)]
            send_ref[block, : NT * CAP, :] = jnp.concatenate(parts, axis=0).astype(BF16)
            parts = [take_lanes(groups[g], lane, block, g * CAP) for g in range(3)]
            joined = jnp.where(lane < CAP, parts[0], jnp.where(lane < 2 * CAP, parts[1], parts[2]))
            send_ref[block, NT * CAP :, :] = joined.astype(BF16)


def half_cell(ids):
    return jnp.where(ids >= HALF, ids - HALF, ids).astype(I32)


def adjoint_kernel(
    recv_ref, flux_ref, meta_ref, foot_ref, hot, weighted, total
):
    lane = lax.broadcasted_iota(I32, (16, LANES), 1)
    joined = [recv_ref[block, NT * CAP :, :].astype(F32) for block in range(N_WIDE)]
    for g in range(3):
        for c, column in enumerate(join_lanes(joined, g * CAP, lane)):
            meta_ref[16 * g : 16 * (g + 1), c * LANES : (c + 1) * LANES] = column
    upper = jnp.transpose(jnp.where(meta_ref[8:16, :] >= HALF, 1.0, 0.0))
    cells = lax.broadcasted_iota(I32, (HALF, SLOTS), 0)
    for k in range(NT):
        low = k * CAP // 16 * 16
        for pair in range(0, N_WIDE, 2):
            rows = slice(pair * CAP, (pair + 2) * CAP)
            pieces = [
                recv_ref[block, low : low + 48, :].astype(F32)[k * CAP - low :][:CAP]
                for block in (pair, pair + 1)
            ]
            foot = jnp.concatenate(pieces, axis=0)
            is_upper = jnp.broadcast_to(upper[rows, k : k + 1], (2 * CAP, LANES)) > 0.5
            foot_ref[k, rows, :LANES] = jnp.where(is_upper, 0.0, foot).astype(BF16)
            foot_ref[k, rows, LANES:] = jnp.where(is_upper, foot, 0.0).astype(BF16)
        hot[k] = jnp.where(cells == half_cell(meta_ref[8 + k : 9 + k, :]), 1.0, 0.0).astype(BF16)
        for r in range(RHS):
            row = jnp.broadcast_to(meta_ref[r : r + 1, :], (16, SLOTS)).astype(BF16)
            for t in range(HALF // 16):
                weighted[k, r * HALF + t * 16 : r * HALF + (t + 1) * 16, :] = (
                    hot[k, t * 16 : (t + 1) * 16, :] * row
                )
        product = dot(weighted[k], foot_ref[k])
        if k == 0:
            total[...] = product
        else:
            total[...] += product
    plane, turn = here()
    for r in range(RHS):
        for side in range(2):
            at = side * HALF
            flux_ref[(r + turn - plane) & 7, at : at + HALF, :] = total[
                r * HALF : (r + 1) * HALF, side * LANES : (side + 1) * LANES
            ].astype(BF16)


def lat_kernel(mix_ref, flux_ref, out_ref, rows_f, columns):
    for t in range(N_NARROW):
        n = band_of(t)
        rows_f[n * CELLS : (n + 1) * CELLS, :] = flux_ref[t].astype(F32)
    for a in range(QUAD):
        for d in range(DAY_DEV):
            columns[d, pl.ds(a, N_WIDE, stride=QUAD), :] = rows_f[
                pl.ds(d * QUAD + a, N_WIDE, stride=CHUNK), :
            ]
    side_by_side = jnp.concatenate([columns[d].astype(BF16) for d in range(DAY_DEV)], axis=1)
    mixed = dot(mix_ref[...], side_by_side)
    for d in range(DAY_DEV):
        columns[d] = mixed[:, d * LANES : (d + 1) * LANES]
        for a in range(QUAD):
            rows_f[pl.ds(d * QUAD + a, N_WIDE, stride=CHUNK), :] = columns[
                d, pl.ds(a, N_WIDE, stride=QUAD), :
            ]
    out_ref[...] = rows_f[...].astype(BF16)


def day_kernel(mix_ref, flux_ref, out_ref, rows_f, columns):
    plane, turn = here()
    for h in range(N_NARROW):
        rows_f[h * CELLS : (h + 1) * CELLS, :] = flux_ref[band_of((h + plane) & 7)].astype(F32)
    for a in range(QUAD):
        columns[:, a * LANES : (a + 1) * LANES] = rows_f[
            pl.ds(a, DAYS, stride=QUAD), :
        ].astype(BF16)
    mixed = dot(mix_ref[...], columns[...])
    for a in range(QUAD):
        rows_f[pl.ds(a, DAYS, stride=QUAD), :] = mixed[:, a * LANES : (a + 1) * LANES]
    for h in range(N_NARROW):
        out_ref[(turn - h) & 7] = rows_f[h * CELLS : (h + 1) * CELLS, :].astype(BF16)


def forward_kernel(
    lon_ref, spread_ref, foot_ref, meta_ref, dir_ref, res_ref, err_ref, send_ref, table, picked, model
):
    smoothed = dot_rows(spread_ref[...], lon_ref[...])
    for r in range(RHS):
        for side in range(2):
            at = r * CELLS + side * HALF
            table[r * HALF : (r + 1) * HALF, side * LANES : (side + 1) * LANES] = smoothed[
                at : at + HALF, :
            ].astype(BF16)
    width = 2 * LANES
    cells = lax.broadcasted_iota(I32, (HALF, width), 0)
    for tile in range(SLOTS // width):
        at = slice(tile * width, (tile + 1) * width)
        sums = [jnp.zeros((1, width), F32)] * RHS
        for k in range(NT):
            picked[k % 2] = dot_rows(table[...], foot_ref[k, at, :])
            mask = cells == half_cell(meta_ref[8 + k : 9 + k, at])
            for r in range(RHS):
                rows = picked[k % 2, r * HALF : (r + 1) * HALF, :]
                sums[r] = sums[r] + jnp.sum(jnp.where(mask, rows, 0.0), axis=0, keepdims=True)
        model[:, at] = jnp.concatenate(sums, axis=0)
    held_dir = meta_ref[0:8, :] + meta_ref[16:24, :]
    held_res = meta_ref[24:32, :] + meta_ref[32:40, :]
    held_err = meta_ref[12:13, :] + meta_ref[13:14, :]
    modelled = model[...]
    held = jnp.concatenate([modelled, held_dir, held_res, held_err * held_dir], axis=0)
    far = dot_rows(held, held, HIGHEST)
    direction = dir_ref[...]
    own = jnp.concatenate([direction, res_ref[...], err_ref[...] * direction], axis=0)
    near = dot_rows(own, own, HIGHEST)
    gram = jnp.concatenate(
        [
            jnp.zeros((RHS, GRAM_AT), F32),
            far[0:8, 8:16] + near[16:24, 0:8],
            far[8:16, 0:8] + near[0:8, 16:24],
            far[0:8, 16:24] + near[16:24, 8:16],
            far[16:24, 0:8] + near[8:16, 16:24],
            far[0:8, 0:8] + far[0:8, 24:32] + far[24:32, 0:8] + near[16:24, 16:24],
            near[8:16, 8:16],
            jnp.zeros((RHS, LANES - GRAM_AT - 48), F32),
        ],
        axis=1,
    )
    lane = lax.broadcasted_iota(I32, (RHS, LANES), 1)
    columns = columns_of(model, 0, RHS)
    for block in range(N_WIDE):
        send_ref[block] = jnp.where(lane < CAP, take_lanes(columns, lane, block, 0), gram)


def sum_kernel(home_ref, out_ref):
    total = home_ref[0]
    for block in range(1, N_WIDE):
        total = total + home_ref[block]
    for n in range(N_NARROW):
        out_ref[n] = total


def inverses(matrices):
    row = lax.broadcasted_iota(I32, (RHS, RHS), 0)
    column = lax.broadcasted_iota(I32, (RHS, RHS), 1)
    unit = jnp.where(row == column, 1.0, 0.0)
    state = [jnp.concatenate([m, unit], axis=1) for m in matrices]
    side = lax.broadcasted_iota(I32, (RHS, 2 * RHS), 0)
    for j in range(RHS):
        following = []
        for m in state:
            pivot = m[j : j + 1, :] / m[j : j + 1, j : j + 1]
            following.append(jnp.where(side == j, pivot, m - m[:, j : j + 1] * pivot))
        state = following
    return [m[:, RHS:] for m in state]


def small_dot(left, right):
    terms = [left[:, k : k + 1] * right[k : k + 1, :] for k in range(RHS)]
    while len(terms) > 1:
        terms = [a + b for a, b in zip(terms[::2], terms[1::2])]
    return terms[0]


def update_kernel(
    gram_ref, home_ref, slot_ref, err_ref, sol_ref, res_ref, dir_ref, sol_out, res_out, dir_out
):
    lane = lax.broadcasted_iota(I32, (RHS, LANES), 1)
    pieces = [home_ref[block] for block in range(N_WIDE)]
    high, rest = split_two(jnp.concatenate(join_lanes(pieces, 0, lane), axis=1))
    middle, low = split_two(rest)
    parts = jnp.concatenate([high, middle, low], axis=0).astype(BF16)
    placed = dot(parts, slot_matrix(slot_ref[...]))
    direction = dir_ref[...]
    image = placed[0:8] + placed[8:16] + placed[16:24] + err_ref[...] * direction
    total = gram_ref[0]
    for n in range(1, N_NARROW):
        total = total + gram_ref[n]
    block = lambda g: total[:, GRAM_AT + 8 * g : GRAM_AT + 8 * g + 8]
    image_dir, dir_image, image_res, res_image, image_image, res_norm = [block(g) for g in range(6)]
    sym = 0.5 * (image_dir + dir_image)
    sym_inverse, norm_inverse = inverses([sym, res_norm])
    step = small_dot(sym_inverse, res_norm)
    step_t = small_dot(res_norm, sym_inverse)
    sol_out[...] = sol_ref[...] + small_dot(step_t, direction)
    residual = res_ref[...] - small_dot(step_t, image)
    res_out[...] = residual
    remaining = res_image - small_dot(step_t, image_image)
    norm_new = res_norm - small_dot(step_t, image_res) - small_dot(remaining, step)
    ratio_t = small_dot(norm_new, norm_inverse)
    dir_out[...] = residual + small_dot(ratio_t, direction)


VMEM = pl.BlockSpec(memory_space=pltpu.VMEM)
HBM = pl.BlockSpec(memory_space=pltpu.HBM)


def in_hbm(array):
    return pltpu.with_memory_space_constraint(array, pltpu.HBM)


def call(kernel, places, outs, scratch, flops, moved):
    return pl.pallas_call(
        kernel,
        in_specs=places,
        out_specs=[VMEM] * len(outs),
        out_shape=[jax.ShapeDtypeStruct(shape, dtype) for shape, dtype in outs],
        scratch_shapes=scratch,
        compiler_params=pltpu.CompilerParams(vmem_limit_bytes=VMEM_LIMIT),
        cost_estimate=pl.CostEstimate(flops=flops, bytes_accessed=moved, transcendentals=0),
    )


def exchange(array, axis, groups=None):
    return lax.all_to_all(
        array, axis, split_axis=0, concat_axis=0, tiled=True, axis_index_groups=groups
    )


BOTH = ("wide", "narrow")
WINDOW_GROUPS = [
    [((turn - h) % N_NARROW * QUAD + q) * N_NARROW + band_of(turn) for turn in range(N_NARROW)]
    for h in range(N_NARROW)
    for q in range(QUAD)
]
PLANE_GROUPS = [
    [(plane * QUAD + i % QUAD) * N_NARROW + i // QUAD for i in range(N_WIDE)]
    for plane in range(N_NARROW)
]


def on_device(
    solution,
    residual,
    direction,
    error_var,
    footprint,
    tiles,
    window,
    temporal,
    spatial_lat,
    spatial_lon,
):
    errors = error_var.reshape(1, OBS_DEV)
    vmem = lambda shape, dtype: pltpu.VMEM(shape, dtype)
    with jax.named_scope("pack"):
        packed, slot = call(
            pack_kernel,
            [HBM] * 6,
            [((N_WIDE, PAYLOAD, LANES), BF16), ((1, OBS_DEV), I32)],
            [
                vmem((1, OBS_DEV), I32),
                vmem((NT, OBS_DEV), I32),
                vmem((OBS_DEV * NT, LANES), BF16),
                vmem((RHS, OBS_DEV), F32),
                vmem((RHS, OBS_DEV), F32),
                vmem((1, OBS_DEV), F32),
                vmem((OBS_DEV, NT * LANES), BF16),
                vmem((SLOTS, OBS_DEV), BF16),
                vmem((SLOTS, NT * LANES), F32),
                vmem((META, SLOTS), F32),
                pltpu.SemaphoreType.DMA((6,)),
            ],
            2 * SLOTS * OBS_DEV * NT * LANES,
            2 * SLOTS * OBS_DEV,
        )(
            in_hbm(window.reshape(1, OBS_DEV)),
            in_hbm(tiles.T),
            in_hbm(footprint.reshape(OBS_DEV * NT, LANES)),
            in_hbm(direction),
            in_hbm(residual),
            in_hbm(errors),
        )
    with jax.named_scope("route"):
        routed = exchange(packed, "wide")
    with jax.named_scope("adjoint"):
        flux, meta, foot = call(
            adjoint_kernel,
            [VMEM],
            [
                ((N_NARROW, CELLS, LANES), BF16),
                ((META, SLOTS), F32),
                ((NT, SLOTS, 2 * LANES), BF16),
            ],
            [
                vmem((NT, HALF, SLOTS), BF16),
                vmem((NT, ROWS // 2, SLOTS), BF16),
                vmem((ROWS // 2, 2 * LANES), F32),
            ],
            2 * ROWS * NT * SLOTS * LANES,
            4 * NT * SLOTS * LANES,
        )(routed)
    with jax.named_scope("to_rhs"):
        by_rhs = exchange(flux, BOTH, WINDOW_GROUPS)
    with jax.named_scope("lat_mix"):
        (spread,) = call(
            lat_kernel,
            [VMEM, VMEM],
            [((ROWS, LANES), BF16)],
            [vmem((ROWS, LANES), F32), vmem((DAY_DEV, LAT, LANES), F32)],
            2 * LAT * LAT * DAY_DEV * LANES,
            4 * ROWS * LANES,
        )(spatial_lat, by_rhs)
    with jax.named_scope("to_days"):
        by_day = exchange(spread.reshape(N_WIDE, CHUNK, LANES), BOTH, PLANE_GROUPS)
    with jax.named_scope("day_mix"):
        (timed,) = call(
            day_kernel,
            [VMEM, VMEM],
            [((N_NARROW, CELLS, LANES), BF16)],
            [vmem((ROWS, LANES), F32), vmem((DAYS, QUAD * LANES), BF16)],
            2 * DAYS * DAYS * QUAD * LANES,
            4 * ROWS * LANES,
        )(temporal, by_day.reshape(N_NARROW, CELLS, LANES))
    with jax.named_scope("to_windows"):
        by_window = exchange(timed.reshape(N_WIDE, CHUNK, LANES), "wide")
    with jax.named_scope("forward"):
        (modelled,) = call(
            forward_kernel,
            [VMEM] * 7,
            [((N_WIDE, RHS, LANES), F32)],
            [
                vmem((ROWS // 2, 2 * LANES), BF16),
                vmem((2, ROWS // 2, 2 * LANES), F32),
                vmem((RHS, SLOTS), F32),
            ],
            2 * ROWS * NT * SLOTS * LANES,
            4 * NT * SLOTS * LANES,
        )(
            spatial_lon,
            by_window.reshape(ROWS, LANES),
            foot,
            meta,
            direction,
            residual,
            errors,
        )
    with jax.named_scope("home"):
        home = exchange(modelled, "wide")
    with jax.named_scope("gram_sum"):
        (partial,) = call(
            sum_kernel,
            [VMEM],
            [((N_NARROW, RHS, LANES), F32)],
            [],
            N_WIDE * RHS * LANES,
            4 * N_WIDE * RHS * LANES,
        )(home)
        grams = exchange(partial, "narrow")
    with jax.named_scope("update"):
        return tuple(
            call(
                update_kernel,
                [VMEM] * 7,
                [((RHS, OBS_DEV), F32)] * 3,
                [],
                2 * 24 * SLOTS * OBS_DEV,
                28 * RHS * OBS_DEV,
            )(grams, home, slot, errors, solution, residual, direction)
        )


def solution(mesh):
    both = BOTH
    in_specs = (
        P(None, both),
        P(None, both),
        P(None, both),
        P(both),
        P(both, None, None),
        P(both, None),
        P(both, None),
        P(),
        P(),
        P(),
    )
    out_specs = (P(None, both), P(None, both), P(None, both))
    return jax.shard_map(
        on_device, mesh=mesh, in_specs=in_specs, out_specs=out_specs, check_vma=False
    )
```

```python
import jax
import jax.numpy as jnp
from jax import lax
from jax.experimental import pallas as pl
from jax.experimental.pallas import tpu as pltpu
from jax.sharding import PartitionSpec as P

F32 = jnp.float32
BF16 = jnp.bfloat16
I32 = jnp.int32
HIGHEST = lax.Precision.HIGHEST
LANES = 128
RHS = 8
NT = 4
N_WIDE = 32
N_NARROW = 8
OBS_DEV = 512
CAP = 40
SLOTS = N_WIDE * CAP
DAY_DEV = 10
DAYS = N_WIDE * DAY_DEV
LAT = 128
CELLS = 160
HALF = CELLS // 2
QUAD = 4
CHUNK = DAY_DEV * QUAD
ROWS = RHS * CELLS
META = 48
PAYLOAD = NT * CAP + 16
GRAM_AT = CAP
SEND_BLOCKS = 8
VMEM_LIMIT = 48 * 1024 * 1024


def dot_rows(left, right, precision=None):
    return lax.dot_general(
        left, right, (((1,), (1,)), ((), ())), precision=precision, preferred_element_type=F32
    )


def dot(left, right, precision=None):
    return lax.dot_general(
        left, right, (((1,), (0,)), ((), ())), precision=precision, preferred_element_type=F32
    )


def here():
    band = lax.axis_index("narrow")
    return lax.axis_index("wide") >> 2, (band & 1) * (N_NARROW // 2) + (band >> 1)


def band_of(turn):
    return (turn & 3) * 2 + (turn >> 2)


def take_lanes(columns, lane, block, target):
    start = block * CAP
    first = start // LANES
    part = columns[first]
    if (start + CAP - 1) // LANES != first:
        part = jnp.where(lane >= start % LANES, part, columns[first + 1])
    return pltpu.roll(part, (target - start) % LANES, 1)


def join_lanes(pieces, source, lane):
    turned = [
        pltpu.roll(piece, (block * CAP - source) % LANES, 1) for block, piece in enumerate(pieces)
    ]
    columns = []
    for start in range(0, SLOTS, LANES):
        blocks = range(start // CAP, (start + LANES - 1) // CAP + 1)
        column = turned[blocks[-1]]
        for block in reversed(blocks[:-1]):
            column = jnp.where(lane < (block + 1) * CAP - start, turned[block], column)
        columns.append(column)
    return columns


def columns_of(ref, row, rows):
    return [ref[row : row + rows, at : at + LANES] for at in range(0, SLOTS, LANES)]


def split_two(value):
    high = value.astype(BF16)
    return high.astype(F32), value - high.astype(F32)


def slot_matrix(slot_row):
    rows = lax.broadcasted_iota(I32, (SLOTS, OBS_DEV), 0)
    return jnp.where(rows == slot_row, 1.0, 0.0).astype(BF16)


def pack_kernel(
    window_hbm,
    tiles_hbm,
    foot_hbm,
    dir_hbm,
    res_hbm,
    err_hbm,
    send_ref,
    slot_ref,
    window_ref,
    tiles_ref,
    foot_ref,
    dir_ref,
    res_ref,
    err_ref,
    by_tile,
    pick,
    moved,
    meta,
    sems,
):
    copies = [
        pltpu.make_async_copy(source, target, sems.at[i])
        for i, (source, target) in enumerate(
            [
                (window_hbm, window_ref),
                (foot_hbm, foot_ref),
                (dir_hbm, dir_ref),
                (res_hbm, res_ref),
                (err_hbm, err_ref),
                (tiles_hbm, tiles_ref),
            ]
        )
    ]
    for copy in copies:
        copy.start()
    earlier = lax.broadcasted_iota(I32, (OBS_DEV, OBS_DEV), 0) < lax.broadcasted_iota(
        I32, (OBS_DEV, OBS_DEV), 1
    )
    earlier = jnp.where(earlier, 1.0, 0.0).astype(BF16)
    for copy in copies:
        copy.wait()
    window = window_ref[...]
    turn = here()[1]
    owner = ((turn - (window >> 2)) & 7) * QUAD + (window & 3)
    named = lax.broadcasted_iota(I32, (N_WIDE, OBS_DEV), 0) == owner
    named_f = jnp.where(named, 1.0, 0.0)
    before = dot(named_f.astype(BF16), earlier)
    position = jnp.sum(before * named_f, axis=0, keepdims=True).astype(I32)
    slot = owner * CAP + position
    slot_ref[...] = slot
    pick[...] = slot_matrix(slot)
    tile = tiles_ref[...]
    day, row = tile >> 4, tile & 15
    cell = ((row >> 2) * CHUNK + day * QUAD + (row & 3)).astype(F32)
    dir_high, dir_low = split_two(dir_ref[...])
    res_high, res_low = split_two(res_ref[...])
    err_high, err_low = split_two(err_ref[...])
    zero = jnp.zeros((2, OBS_DEV), F32)
    values = jnp.concatenate(
        [
            dir_high,
            jnp.concatenate([cell, err_high, err_low, zero], axis=0),
            dir_low,
            res_high,
            res_low,
            jnp.zeros((8, OBS_DEV), F32),
        ],
        axis=0,
    ).astype(BF16)
    meta[...] = dot_rows(values, pick[...])
    group = 2 * LANES
    share = group // NT
    out_row = lax.broadcasted_iota(I32, (group, group), 0)
    in_row = lax.broadcasted_iota(I32, (group, group), 1)
    sort = jnp.where(in_row == out_row % share * NT + out_row // share, 1.0, 0.0).astype(BF16)
    for g in range(OBS_DEV // share):
        rows = dot(sort, foot_ref[g * group : (g + 1) * group, :]).astype(BF16)
        for k in range(NT):
            by_tile[g * share : (g + 1) * share, k * LANES : (k + 1) * LANES] = rows[
                k * share : (k + 1) * share, :
            ]
    lane = lax.broadcasted_iota(I32, (16, LANES), 1)
    groups = [columns_of(meta, 16 * g, 16) for g in range(3)]
    for first in range(0, N_WIDE, SEND_BLOCKS):
        part = slice(first * CAP, (first + SEND_BLOCKS) * CAP)
        moved[part, :] = dot(pick[part, :], by_tile[...])
        for block in range(first, first + SEND_BLOCKS):
            rows = slice(block * CAP, (block + 1) * CAP)
            parts = [moved[rows, k * LANES : (k + 1) * LANES] for k in range(NT)]
            send_ref[block, : NT * CAP, :] = jnp.concatenate(parts, axis=0).astype(BF16)
            parts = [take_lanes(groups[g], lane, block, g * CAP) for g in range(3)]
            joined = jnp.where(lane < CAP, parts[0], jnp.where(lane < 2 * CAP, parts[1], parts[2]))
            send_ref[block, NT * CAP :, :] = joined.astype(BF16)


def half_cell(ids):
    return jnp.where(ids >= HALF, ids - HALF, ids).astype(I32)


def adjoint_kernel(
    recv_ref, flux_ref, meta_ref, foot_ref, hot, weighted, total
):
    lane = lax.broadcasted_iota(I32, (16, LANES), 1)
    joined = [recv_ref[block, NT * CAP :, :].astype(F32) for block in range(N_WIDE)]
    for g in range(3):
        for c, column in enumerate(join_lanes(joined, g * CAP, lane)):
            meta_ref[16 * g : 16 * (g + 1), c * LANES : (c + 1) * LANES] = column
    upper = jnp.transpose(jnp.where(meta_ref[8:16, :] >= HALF, 1.0, 0.0))
    cells = lax.broadcasted_iota(I32, (HALF, SLOTS), 0)
    for k in range(NT):
        low = k * CAP // 16 * 16
        for pair in range(0, N_WIDE, 2):
            rows = slice(pair * CAP, (pair + 2) * CAP)
            pieces = [
                recv_ref[block, low : low + 48, :].astype(F32)[k * CAP - low :][:CAP]
                for block in (pair, pair + 1)
            ]
            foot = jnp.concatenate(pieces, axis=0)
            is_upper = jnp.broadcast_to(upper[rows, k : k + 1], (2 * CAP, LANES)) > 0.5
            foot_ref[k, rows, :LANES] = jnp.where(is_upper, 0.0, foot).astype(BF16)
            foot_ref[k, rows, LANES:] = jnp.where(is_upper, foot, 0.0).astype(BF16)
        hot[k] = jnp.where(cells == half_cell(meta_ref[8 + k : 9 + k, :]), 1.0, 0.0).astype(BF16)
        for r in range(RHS):
            row = jnp.broadcast_to(meta_ref[r : r + 1, :], (16, SLOTS)).astype(BF16)
            for t in range(HALF // 16):
                weighted[k, r * HALF + t * 16 : r * HALF + (t + 1) * 16, :] = (
                    hot[k, t * 16 : (t + 1) * 16, :] * row
                )
        product = dot(weighted[k], foot_ref[k])
        if k == 0:
            total[...] = product
        else:
            total[...] += product
    plane, turn = here()
    for r in range(RHS):
        for side in range(2):
            at = side * HALF
            flux_ref[(r + turn - plane) & 7, at : at + HALF, :] = total[
                r * HALF : (r + 1) * HALF, side * LANES : (side + 1) * LANES
            ].astype(BF16)


def lat_kernel(mix_ref, flux_ref, out_ref, rows_f, columns):
    for t in range(N_NARROW):
        n = band_of(t)
        rows_f[n * CELLS : (n + 1) * CELLS, :] = flux_ref[t].astype(F32)
    for a in range(QUAD):
        for d in range(DAY_DEV):
            columns[d, pl.ds(a, N_WIDE, stride=QUAD), :] = rows_f[
                pl.ds(d * QUAD + a, N_WIDE, stride=CHUNK), :
            ]
    side_by_side = [columns[d, :LAT, :].astype(BF16) for d in range(DAY_DEV)]
    side_by_side = jnp.concatenate(side_by_side, axis=1)
    mixed = dot(mix_ref[...], side_by_side)
    for d in range(DAY_DEV):
        columns[d, :LAT, :] = mixed[:, d * LANES : (d + 1) * LANES]
        for a in range(QUAD):
            rows_f[pl.ds(d * QUAD + a, N_WIDE, stride=CHUNK), :] = columns[
                d, pl.ds(a, N_WIDE, stride=QUAD), :
            ]
    out_ref[...] = rows_f[:ROWS, :].astype(BF16)


def day_kernel(mix_ref, flux_ref, out_ref, rows_f, columns):
    plane, turn = here()
    for h in range(N_NARROW):
        rows_f[h * CELLS : (h + 1) * CELLS, :] = flux_ref[band_of((h + plane) & 7)].astype(F32)
    for a in range(QUAD):
        columns[:, a * LANES : (a + 1) * LANES] = rows_f[
            pl.ds(a, DAYS, stride=QUAD), :
        ].astype(BF16)
    mixed = dot(mix_ref[...], columns[...])
    for a in range(QUAD):
        rows_f[pl.ds(a, DAYS, stride=QUAD), :] = mixed[:, a * LANES : (a + 1) * LANES]
    for h in range(N_NARROW):
        out_ref[(turn - h) & 7] = rows_f[h * CELLS : (h + 1) * CELLS, :].astype(BF16)


def forward_kernel(
    lon_ref, spread_ref, foot_ref, meta_ref, dir_ref, res_ref, err_ref, send_ref, table, picked, model
):
    smoothed = dot_rows(spread_ref[...], lon_ref[...])
    for r in range(RHS):
        for side in range(2):
            at = r * CELLS + side * HALF
            table[r * HALF : (r + 1) * HALF, side * LANES : (side + 1) * LANES] = smoothed[
                at : at + HALF, :
            ].astype(BF16)
    width = 2 * LANES
    cells = lax.broadcasted_iota(I32, (HALF, width), 0)
    for tile in range(SLOTS // width):
        at = slice(tile * width, (tile + 1) * width)
        sums = [jnp.zeros((1, width), F32)] * RHS
        for k in range(NT):
            picked[k % 2] = dot_rows(table[...], foot_ref[k, at, :])
            mask = cells == half_cell(meta_ref[8 + k : 9 + k, at])
            for r in range(RHS):
                rows = picked[k % 2, r * HALF : (r + 1) * HALF, :]
                sums[r] = sums[r] + jnp.sum(jnp.where(mask, rows, 0.0), axis=0, keepdims=True)
        model[:, at] = jnp.concatenate(sums, axis=0)
    held_dir = meta_ref[0:8, :] + meta_ref[16:24, :]
    held_res = meta_ref[24:32, :] + meta_ref[32:40, :]
    held_err = meta_ref[12:13, :] + meta_ref[13:14, :]
    modelled = model[...]
    held = jnp.concatenate([modelled, held_dir, held_res, held_err * held_dir], axis=0)
    far = dot_rows(held, held, HIGHEST)
    direction = dir_ref[...]
    own = jnp.concatenate([direction, res_ref[...], err_ref[...] * direction], axis=0)
    near = dot_rows(own, own, HIGHEST)
    gram = jnp.concatenate(
        [
            jnp.zeros((RHS, GRAM_AT), F32),
            far[0:8, 8:16] + near[16:24, 0:8],
            far[8:16, 0:8] + near[0:8, 16:24],
            far[0:8, 16:24] + near[16:24, 8:16],
            far[16:24, 0:8] + near[8:16, 16:24],
            far[0:8, 0:8] + far[0:8, 24:32] + far[24:32, 0:8] + near[16:24, 16:24],
            near[8:16, 8:16],
            jnp.zeros((RHS, LANES - GRAM_AT - 48), F32),
        ],
        axis=1,
    )
    lane = lax.broadcasted_iota(I32, (RHS, LANES), 1)
    columns = columns_of(model, 0, RHS)
    for block in range(N_WIDE):
        send_ref[block] = jnp.where(lane < CAP, take_lanes(columns, lane, block, 0), gram)


def sum_kernel(home_ref, out_ref):
    total = home_ref[0]
    for block in range(1, N_WIDE):
        total = total + home_ref[block]
    for n in range(N_NARROW):
        out_ref[n] = total


def inverses(matrices):
    row = lax.broadcasted_iota(I32, (RHS, RHS), 0)
    column = lax.broadcasted_iota(I32, (RHS, RHS), 1)
    unit = jnp.where(row == column, 1.0, 0.0)
    state = [jnp.concatenate([m, unit], axis=1) for m in matrices]
    side = lax.broadcasted_iota(I32, (RHS, 2 * RHS), 0)
    for j in range(RHS):
        following = []
        for m in state:
            pivot = m[j : j + 1, :] / m[j : j + 1, j : j + 1]
            following.append(jnp.where(side == j, pivot, m - m[:, j : j + 1] * pivot))
        state = following
    return [m[:, RHS:] for m in state]


def small_dot(left, right):
    terms = [left[:, k : k + 1] * right[k : k + 1, :] for k in range(RHS)]
    while len(terms) > 1:
        terms = [a + b for a, b in zip(terms[::2], terms[1::2])]
    return terms[0]


def update_kernel(
    gram_ref, home_ref, slot_ref, err_ref, sol_ref, res_ref, dir_ref, sol_out, res_out, dir_out
):
    lane = lax.broadcasted_iota(I32, (RHS, LANES), 1)
    pieces = [home_ref[block] for block in range(N_WIDE)]
    high, rest = split_two(jnp.concatenate(join_lanes(pieces, 0, lane), axis=1))
    middle, low = split_two(rest)
    parts = jnp.concatenate([high, middle, low], axis=0).astype(BF16)
    placed = dot(parts, slot_matrix(slot_ref[...]))
    direction = dir_ref[...]
    image = placed[0:8] + placed[8:16] + placed[16:24] + err_ref[...] * direction
    total = gram_ref[0]
    for n in range(1, N_NARROW):
        total = total + gram_ref[n]
    block = lambda g: total[:, GRAM_AT + 8 * g : GRAM_AT + 8 * g + 8]
    image_dir, dir_image, image_res, res_image, image_image, res_norm = [block(g) for g in range(6)]
    sym = 0.5 * (image_dir + dir_image)
    sym_inverse, norm_inverse = inverses([sym, res_norm])
    step = small_dot(sym_inverse, res_norm)
    step_t = small_dot(res_norm, sym_inverse)
    sol_out[...] = sol_ref[...] + small_dot(step_t, direction)
    residual = res_ref[...] - small_dot(step_t, image)
    res_out[...] = residual
    remaining = res_image - small_dot(step_t, image_image)
    norm_new = res_norm - small_dot(step_t, image_res) - small_dot(remaining, step)
    ratio_t = small_dot(norm_new, norm_inverse)
    dir_out[...] = residual + small_dot(ratio_t, direction)


VMEM = pl.BlockSpec(memory_space=pltpu.VMEM)
HBM = pl.BlockSpec(memory_space=pltpu.HBM)


def in_hbm(array):
    return pltpu.with_memory_space_constraint(array, pltpu.HBM)


def call(kernel, places, outs, scratch, flops, moved):
    return pl.pallas_call(
        kernel,
        in_specs=places,
        out_specs=[VMEM] * len(outs),
        out_shape=[jax.ShapeDtypeStruct(shape, dtype) for shape, dtype in outs],
        scratch_shapes=scratch,
        compiler_params=pltpu.CompilerParams(vmem_limit_bytes=VMEM_LIMIT),
        cost_estimate=pl.CostEstimate(flops=flops, bytes_accessed=moved, transcendentals=0),
    )


def exchange(array, axis, groups=None):
    return lax.all_to_all(
        array, axis, split_axis=0, concat_axis=0, tiled=True, axis_index_groups=groups
    )


BOTH = ("wide", "narrow")
WINDOW_GROUPS = [
    [((turn - h) % N_NARROW * QUAD + q) * N_NARROW + band_of(turn) for turn in range(N_NARROW)]
    for h in range(N_NARROW)
    for q in range(QUAD)
]
PLANE_GROUPS = [
    [(plane * QUAD + i % QUAD) * N_NARROW + i // QUAD for i in range(N_WIDE)]
    for plane in range(N_NARROW)
]


def on_device(
    solution,
    residual,
    direction,
    error_var,
    footprint,
    tiles,
    window,
    temporal,
    spatial_lat,
    spatial_lon,
):
    errors = error_var.reshape(1, OBS_DEV)
    vmem = lambda shape, dtype: pltpu.VMEM(shape, dtype)
    with jax.named_scope("pack"):
        packed, slot = call(
            pack_kernel,
            [HBM] * 6,
            [((N_WIDE, PAYLOAD, LANES), BF16), ((1, OBS_DEV), I32)],
            [
                vmem((1, OBS_DEV), I32),
                vmem((NT, OBS_DEV), I32),
                vmem((OBS_DEV * NT, LANES), BF16),
                vmem((RHS, OBS_DEV), F32),
                vmem((RHS, OBS_DEV), F32),
                vmem((1, OBS_DEV), F32),
                vmem((OBS_DEV, NT * LANES), BF16),
                vmem((SLOTS, OBS_DEV), BF16),
                vmem((SLOTS, NT * LANES), F32),
                vmem((META, SLOTS), F32),
                pltpu.SemaphoreType.DMA((6,)),
            ],
            2 * SLOTS * OBS_DEV * NT * LANES,
            2 * SLOTS * OBS_DEV,
        )(
            in_hbm(window.reshape(1, OBS_DEV)),
            in_hbm(tiles.T),
            in_hbm(footprint.reshape(OBS_DEV * NT, LANES)),
            in_hbm(direction),
            in_hbm(residual),
            in_hbm(errors),
        )
    with jax.named_scope("route"):
        routed = exchange(packed, "wide")
    with jax.named_scope("adjoint"):
        flux, meta, foot = call(
            adjoint_kernel,
            [VMEM],
            [
                ((N_NARROW, CELLS, LANES), BF16),
                ((META, SLOTS), F32),
                ((NT, SLOTS, 2 * LANES), BF16),
            ],
            [
                vmem((NT, HALF, SLOTS), BF16),
                vmem((NT, ROWS // 2, SLOTS), BF16),
                vmem((ROWS // 2, 2 * LANES), F32),
            ],
            2 * ROWS * NT * SLOTS * LANES,
            4 * NT * SLOTS * LANES,
        )(routed)
    with jax.named_scope("to_rhs"):
        by_rhs = exchange(flux, BOTH, WINDOW_GROUPS)
    with jax.named_scope("lat_mix"):
        (spread,) = call(
            lat_kernel,
            [VMEM, VMEM],
            [((ROWS, LANES), BF16)],
            [vmem((ROWS + CHUNK, LANES), F32), vmem((DAY_DEV, LAT + 8, LANES), F32)],
            2 * LAT * LAT * DAY_DEV * LANES,
            4 * ROWS * LANES,
        )(spatial_lat, by_rhs)
    with jax.named_scope("to_days"):
        by_day = exchange(spread.reshape(N_WIDE, CHUNK, LANES), BOTH, PLANE_GROUPS)
    with jax.named_scope("day_mix"):
        (timed,) = call(
            day_kernel,
            [VMEM, VMEM],
            [((N_NARROW, CELLS, LANES), BF16)],
            [vmem((ROWS + 8, LANES), F32), vmem((DAYS, QUAD * LANES), BF16)],
            2 * DAYS * DAYS * QUAD * LANES,
            4 * ROWS * LANES,
        )(temporal, by_day.reshape(N_NARROW, CELLS, LANES))
    with jax.named_scope("to_windows"):
        by_window = exchange(timed.reshape(N_WIDE, CHUNK, LANES), "wide")
    with jax.named_scope("forward"):
        (modelled,) = call(
            forward_kernel,
            [VMEM] * 7,
            [((N_WIDE, RHS, LANES), F32)],
            [
                vmem((ROWS // 2, 2 * LANES), BF16),
                vmem((2, ROWS // 2, 2 * LANES), F32),
                vmem((RHS, SLOTS), F32),
            ],
            2 * ROWS * NT * SLOTS * LANES,
            4 * NT * SLOTS * LANES,
        )(
            spatial_lon,
            by_window.reshape(ROWS, LANES),
            foot,
            meta,
            direction,
            residual,
            errors,
        )
    with jax.named_scope("home"):
        home = exchange(modelled, "wide")
    with jax.named_scope("gram_sum"):
        (partial,) = call(
            sum_kernel,
            [VMEM],
            [((N_NARROW, RHS, LANES), F32)],
            [],
            N_WIDE * RHS * LANES,
            4 * N_WIDE * RHS * LANES,
        )(home)
        grams = exchange(partial, "narrow")
    with jax.named_scope("update"):
        return tuple(
            call(
                update_kernel,
                [VMEM] * 7,
                [((RHS, OBS_DEV), F32)] * 3,
                [],
                2 * 24 * SLOTS * OBS_DEV,
                28 * RHS * OBS_DEV,
            )(grams, home, slot, errors, solution, residual, direction)
        )


def solution(mesh):
    both = BOTH
    in_specs = (
        P(None, both),
        P(None, both),
        P(None, both),
        P(both),
        P(both, None, None),
        P(both, None),
        P(both, None),
        P(),
        P(),
        P(),
    )
    out_specs = (P(None, both), P(None, both), P(None, both))
    return jax.shard_map(
        on_device, mesh=mesh, in_specs=in_specs, out_specs=out_specs, check_vma=False
    )
```

```python
import jax
import jax.numpy as jnp
from jax import lax
from jax.experimental import pallas as pl
from jax.experimental.pallas import tpu as pltpu
from jax.sharding import PartitionSpec as P

F32 = jnp.float32
BF16 = jnp.bfloat16
I32 = jnp.int32
HIGHEST = lax.Precision.HIGHEST
LANES = 128
RHS = 8
NT = 4
N_WIDE = 32
N_NARROW = 8
OBS_DEV = 512
CAP = 40
SLOTS = N_WIDE * CAP
DAY_DEV = 10
DAYS = N_WIDE * DAY_DEV
LAT = 128
CELLS = 160
HALF = CELLS // 2
QUAD = 4
CHUNK = DAY_DEV * QUAD
ROWS = RHS * CELLS
META = 48
PAYLOAD = NT * CAP + 16
GRAM_AT = CAP
SEND_BLOCKS = 8
VMEM_LIMIT = 48 * 1024 * 1024


def dot_rows(left, right, precision=None):
    return lax.dot_general(
        left, right, (((1,), (1,)), ((), ())), precision=precision, preferred_element_type=F32
    )


def dot(left, right, precision=None):
    return lax.dot_general(
        left, right, (((1,), (0,)), ((), ())), precision=precision, preferred_element_type=F32
    )


def here():
    band = lax.axis_index("narrow")
    return lax.axis_index("wide") >> 2, (band & 1) * (N_NARROW // 2) + (band >> 1)


def band_of(turn):
    return (turn & 3) * 2 + (turn >> 2)


def take_lanes(columns, lane, block, target):
    start = block * CAP
    first = start // LANES
    part = columns[first]
    if (start + CAP - 1) // LANES != first:
        part = jnp.where(lane >= start % LANES, part, columns[first + 1])
    return pltpu.roll(part, (target - start) % LANES, 1)


def join_lanes(pieces, source, lane):
    turned = [
        pltpu.roll(piece, (block * CAP - source) % LANES, 1) for block, piece in enumerate(pieces)
    ]
    columns = []
    for start in range(0, SLOTS, LANES):
        blocks = range(start // CAP, (start + LANES - 1) // CAP + 1)
        column = turned[blocks[-1]]
        for block in reversed(blocks[:-1]):
            column = jnp.where(lane < (block + 1) * CAP - start, turned[block], column)
        columns.append(column)
    return columns


def columns_of(ref, row, rows):
    return [ref[row : row + rows, at : at + LANES] for at in range(0, SLOTS, LANES)]


def split_two(value):
    high = value.astype(BF16)
    return high.astype(F32), value - high.astype(F32)


def slot_matrix(slot_row):
    rows = lax.broadcasted_iota(I32, (SLOTS, OBS_DEV), 0)
    return jnp.where(rows == slot_row, 1.0, 0.0).astype(BF16)


def pack_kernel(
    window_hbm,
    tiles_hbm,
    foot_hbm,
    dir_hbm,
    res_hbm,
    err_hbm,
    send_ref,
    slot_ref,
    window_ref,
    tiles_ref,
    foot_ref,
    dir_ref,
    res_ref,
    err_ref,
    by_tile,
    pick,
    moved,
    meta,
    sems,
):
    copies = [
        pltpu.make_async_copy(source, target, sems.at[i])
        for i, (source, target) in enumerate(
            [
                (window_hbm, window_ref),
                (foot_hbm, foot_ref),
                (dir_hbm, dir_ref),
                (res_hbm, res_ref),
                (err_hbm, err_ref),
                (tiles_hbm, tiles_ref),
            ]
        )
    ]
    for copy in copies:
        copy.start()
    earlier = lax.broadcasted_iota(I32, (OBS_DEV, OBS_DEV), 0) < lax.broadcasted_iota(
        I32, (OBS_DEV, OBS_DEV), 1
    )
    earlier = jnp.where(earlier, 1.0, 0.0).astype(BF16)
    for copy in copies:
        copy.wait()
    window = window_ref[...]
    turn = here()[1]
    owner = ((turn - (window >> 2)) & 7) * QUAD + (window & 3)
    named = lax.broadcasted_iota(I32, (N_WIDE, OBS_DEV), 0) == owner
    named_f = jnp.where(named, 1.0, 0.0)
    before = dot(named_f.astype(BF16), earlier)
    position = jnp.sum(before * named_f, axis=0, keepdims=True).astype(I32)
    slot = owner * CAP + position
    slot_ref[...] = slot
    pick[...] = slot_matrix(slot)
    tile = tiles_ref[...]
    day, row = tile >> 4, tile & 15
    cell = ((row >> 2) * CHUNK + day * QUAD + (row & 3)).astype(F32)
    dir_high, dir_low = split_two(dir_ref[...])
    res_high, res_low = split_two(res_ref[...])
    err_high, err_low = split_two(err_ref[...])
    zero = jnp.zeros((2, OBS_DEV), F32)
    values = jnp.concatenate(
        [
            dir_high,
            jnp.concatenate([cell, err_high, err_low, zero], axis=0),
            dir_low,
            res_high,
            res_low,
            jnp.zeros((8, OBS_DEV), F32),
        ],
        axis=0,
    ).astype(BF16)
    meta[...] = dot_rows(values, pick[...])
    group = 2 * LANES
    share = group // NT
    out_row = lax.broadcasted_iota(I32, (group, group), 0)
    in_row = lax.broadcasted_iota(I32, (group, group), 1)
    sort = jnp.where(in_row == out_row % share * NT + out_row // share, 1.0, 0.0).astype(BF16)
    for g in range(OBS_DEV // share):
        rows = dot(sort, foot_ref[g * group : (g + 1) * group, :]).astype(BF16)
        for k in range(NT):
            by_tile[g * share : (g + 1) * share, k * LANES : (k + 1) * LANES] = rows[
                k * share : (k + 1) * share, :
            ]
    lane = lax.broadcasted_iota(I32, (16, LANES), 1)
    groups = [columns_of(meta, 16 * g, 16) for g in range(3)]
    for first in range(0, N_WIDE, SEND_BLOCKS):
        part = slice(first * CAP, (first + SEND_BLOCKS) * CAP)
        moved[part, :] = dot(pick[part, :], by_tile[...])
        for block in range(first, first + SEND_BLOCKS):
            rows = slice(block * CAP, (block + 1) * CAP)
            parts = [moved[rows, k * LANES : (k + 1) * LANES] for k in range(NT)]
            send_ref[block, : NT * CAP, :] = jnp.concatenate(parts, axis=0).astype(BF16)
            parts = [take_lanes(groups[g], lane, block, g * CAP) for g in range(3)]
            joined = jnp.where(lane < CAP, parts[0], jnp.where(lane < 2 * CAP, parts[1], parts[2]))
            send_ref[block, NT * CAP :, :] = joined.astype(BF16)


def half_cell(ids):
    return jnp.where(ids >= HALF, ids - HALF, ids).astype(I32)


def adjoint_kernel(
    recv_ref, flux_ref, meta_ref, foot_ref, hot, weighted, total
):
    lane = lax.broadcasted_iota(I32, (16, LANES), 1)
    joined = [recv_ref[block, NT * CAP :, :].astype(F32) for block in range(N_WIDE)]
    for g in range(3):
        for c, column in enumerate(join_lanes(joined, g * CAP, lane)):
            meta_ref[16 * g : 16 * (g + 1), c * LANES : (c + 1) * LANES] = column
    upper = jnp.where(meta_ref[8:12, :] >= HALF, 1.0, 0.0)
    code = (upper[0:1] + 2.0 * upper[1:2]) + (4.0 * upper[2:3] + 8.0 * upper[3:4])
    code = jnp.transpose(jnp.broadcast_to(code, (8, SLOTS)))
    for pair in range(0, N_WIDE, 2):
        rows = slice(pair * CAP, (pair + 2) * CAP)
        bits = jnp.broadcast_to(code[rows, 0:1], (2 * CAP, LANES)).astype(I32)
        first, second = [
            recv_ref[block, : NT * CAP, :].astype(F32) for block in (pair, pair + 1)
        ]
        for k in range(NT):
            part = slice(k * CAP, (k + 1) * CAP)
            foot = jnp.concatenate([first[part], second[part]], axis=0)
            is_upper = (bits & (1 << k)) != 0
            foot_ref[k, rows, :LANES] = jnp.where(is_upper, 0.0, foot).astype(BF16)
            foot_ref[k, rows, LANES:] = jnp.where(is_upper, foot, 0.0).astype(BF16)
    cells = lax.broadcasted_iota(I32, (HALF, SLOTS), 0)
    for k in range(NT):
        hot[k] = jnp.where(cells == half_cell(meta_ref[8 + k : 9 + k, :]), 1.0, 0.0).astype(BF16)
        for r in range(RHS):
            row = jnp.broadcast_to(meta_ref[r : r + 1, :], (16, SLOTS)).astype(BF16)
            for t in range(HALF // 16):
                weighted[k, r * HALF + t * 16 : r * HALF + (t + 1) * 16, :] = (
                    hot[k, t * 16 : (t + 1) * 16, :] * row
                )
        product = dot(weighted[k], foot_ref[k])
        if k == 0:
            total[...] = product
        else:
            total[...] += product
    plane, turn = here()
    for r in range(RHS):
        for side in range(2):
            at = side * HALF
            flux_ref[(r + turn - plane) & 7, at : at + HALF, :] = total[
                r * HALF : (r + 1) * HALF, side * LANES : (side + 1) * LANES
            ].astype(BF16)


def lat_kernel(mix_ref, flux_ref, out_ref, rows_f, columns):
    for t in range(N_NARROW):
        n = band_of(t)
        rows_f[n * CELLS : (n + 1) * CELLS, :] = flux_ref[t].astype(F32)
    for a in range(QUAD):
        for d in range(DAY_DEV):
            columns[d, pl.ds(a, N_WIDE, stride=QUAD), :] = rows_f[
                pl.ds(d * QUAD + a, N_WIDE, stride=CHUNK), :
            ]
    side_by_side = [columns[d, :LAT, :].astype(BF16) for d in range(DAY_DEV)]
    side_by_side = jnp.concatenate(side_by_side, axis=1)
    mixed = dot(mix_ref[...], side_by_side)
    for d in range(DAY_DEV):
        columns[d, :LAT, :] = mixed[:, d * LANES : (d + 1) * LANES]
        for a in range(QUAD):
            rows_f[pl.ds(d * QUAD + a, N_WIDE, stride=CHUNK), :] = columns[
                d, pl.ds(a, N_WIDE, stride=QUAD), :
            ]
    out_ref[...] = rows_f[:ROWS, :].astype(BF16)


def day_kernel(mix_ref, flux_ref, out_ref, rows_f, columns):
    plane, turn = here()
    for h in range(N_NARROW):
        rows_f[h * CELLS : (h + 1) * CELLS, :] = flux_ref[band_of((h + plane) & 7)].astype(F32)
    for a in range(QUAD):
        columns[:, a * LANES : (a + 1) * LANES] = rows_f[
            pl.ds(a, DAYS, stride=QUAD), :
        ].astype(BF16)
    mixed = dot(mix_ref[...], columns[...])
    for a in range(QUAD):
        rows_f[pl.ds(a, DAYS, stride=QUAD), :] = mixed[:, a * LANES : (a + 1) * LANES]
    for h in range(N_NARROW):
        out_ref[(turn - h) & 7] = rows_f[h * CELLS : (h + 1) * CELLS, :].astype(BF16)


def forward_kernel(
    lon_ref, spread_ref, foot_ref, meta_ref, dir_ref, res_ref, err_ref, send_ref, table, picked, model
):
    smoothed = dot_rows(spread_ref[...], lon_ref[...])
    for r in range(RHS):
        for side in range(2):
            at = r * CELLS + side * HALF
            table[r * HALF : (r + 1) * HALF, side * LANES : (side + 1) * LANES] = smoothed[
                at : at + HALF, :
            ].astype(BF16)
    width = 2 * LANES
    cells = lax.broadcasted_iota(I32, (HALF, width), 0)
    for tile in range(SLOTS // width):
        at = slice(tile * width, (tile + 1) * width)
        sums = [jnp.zeros((1, width), F32)] * RHS
        for k in range(NT):
            picked[k % 2] = dot_rows(table[...], foot_ref[k, at, :])
            mask = cells == half_cell(meta_ref[8 + k : 9 + k, at])
            for r in range(RHS):
                rows = picked[k % 2, r * HALF : (r + 1) * HALF, :]
                sums[r] = sums[r] + jnp.sum(jnp.where(mask, rows, 0.0), axis=0, keepdims=True)
        model[:, at] = jnp.concatenate(sums, axis=0)
    held_dir = meta_ref[0:8, :] + meta_ref[16:24, :]
    held_res = meta_ref[24:32, :] + meta_ref[32:40, :]
    held_err = meta_ref[12:13, :] + meta_ref[13:14, :]
    modelled = model[...]
    held = jnp.concatenate([modelled, held_dir, held_res, held_err * held_dir], axis=0)
    far = dot_rows(held, held, HIGHEST)
    direction = dir_ref[...]
    own = jnp.concatenate([direction, res_ref[...], err_ref[...] * direction], axis=0)
    near = dot_rows(own, own, HIGHEST)
    gram = jnp.concatenate(
        [
            jnp.zeros((RHS, GRAM_AT), F32),
            far[0:8, 8:16] + near[16:24, 0:8],
            far[8:16, 0:8] + near[0:8, 16:24],
            far[0:8, 16:24] + near[16:24, 8:16],
            far[16:24, 0:8] + near[8:16, 16:24],
            far[0:8, 0:8] + far[0:8, 24:32] + far[24:32, 0:8] + near[16:24, 16:24],
            near[8:16, 8:16],
            jnp.zeros((RHS, LANES - GRAM_AT - 48), F32),
        ],
        axis=1,
    )
    lane = lax.broadcasted_iota(I32, (RHS, LANES), 1)
    columns = columns_of(model, 0, RHS)
    for block in range(N_WIDE):
        send_ref[block] = jnp.where(lane < CAP, take_lanes(columns, lane, block, 0), gram)


def sum_kernel(home_ref, out_ref):
    total = home_ref[0]
    for block in range(1, N_WIDE):
        total = total + home_ref[block]
    for n in range(N_NARROW):
        out_ref[n] = total


def inverses(matrices):
    row = lax.broadcasted_iota(I32, (RHS, RHS), 0)
    column = lax.broadcasted_iota(I32, (RHS, RHS), 1)
    unit = jnp.where(row == column, 1.0, 0.0)
    state = [jnp.concatenate([m, unit], axis=1) for m in matrices]
    side = lax.broadcasted_iota(I32, (RHS, 2 * RHS), 0)
    for j in range(RHS):
        following = []
        for m in state:
            pivot = m[j : j + 1, :] / m[j : j + 1, j : j + 1]
            following.append(jnp.where(side == j, pivot, m - m[:, j : j + 1] * pivot))
        state = following
    return [m[:, RHS:] for m in state]


def small_dot(left, right):
    terms = [left[:, k : k + 1] * right[k : k + 1, :] for k in range(RHS)]
    while len(terms) > 1:
        terms = [a + b for a, b in zip(terms[::2], terms[1::2])]
    return terms[0]


def update_kernel(
    gram_ref, home_ref, slot_ref, err_ref, sol_ref, res_ref, dir_ref, sol_out, res_out, dir_out
):
    lane = lax.broadcasted_iota(I32, (RHS, LANES), 1)
    pieces = [home_ref[block] for block in range(N_WIDE)]
    high, rest = split_two(jnp.concatenate(join_lanes(pieces, 0, lane), axis=1))
    middle, low = split_two(rest)
    parts = jnp.concatenate([high, middle, low], axis=0).astype(BF16)
    placed = dot(parts, slot_matrix(slot_ref[...]))
    direction = dir_ref[...]
    image = placed[0:8] + placed[8:16] + placed[16:24] + err_ref[...] * direction
    total = gram_ref[0]
    for n in range(1, N_NARROW):
        total = total + gram_ref[n]
    block = lambda g: total[:, GRAM_AT + 8 * g : GRAM_AT + 8 * g + 8]
    image_dir, dir_image, image_res, res_image, image_image, res_norm = [block(g) for g in range(6)]
    sym = 0.5 * (image_dir + dir_image)
    sym_inverse, norm_inverse = inverses([sym, res_norm])
    step = small_dot(sym_inverse, res_norm)
    step_t = small_dot(res_norm, sym_inverse)
    sol_out[...] = sol_ref[...] + small_dot(step_t, direction)
    residual = res_ref[...] - small_dot(step_t, image)
    res_out[...] = residual
    remaining = res_image - small_dot(step_t, image_image)
    norm_new = res_norm - small_dot(step_t, image_res) - small_dot(remaining, step)
    ratio_t = small_dot(norm_new, norm_inverse)
    dir_out[...] = residual + small_dot(ratio_t, direction)


VMEM = pl.BlockSpec(memory_space=pltpu.VMEM)
HBM = pl.BlockSpec(memory_space=pltpu.HBM)


def in_hbm(array):
    return pltpu.with_memory_space_constraint(array, pltpu.HBM)


def call(kernel, places, outs, scratch, flops, moved):
    return pl.pallas_call(
        kernel,
        in_specs=places,
        out_specs=[VMEM] * len(outs),
        out_shape=[jax.ShapeDtypeStruct(shape, dtype) for shape, dtype in outs],
        scratch_shapes=scratch,
        compiler_params=pltpu.CompilerParams(vmem_limit_bytes=VMEM_LIMIT),
        cost_estimate=pl.CostEstimate(flops=flops, bytes_accessed=moved, transcendentals=0),
    )


def exchange(array, axis, groups=None):
    return lax.all_to_all(
        array, axis, split_axis=0, concat_axis=0, tiled=True, axis_index_groups=groups
    )


BOTH = ("wide", "narrow")
WINDOW_GROUPS = [
    [((turn - h) % N_NARROW * QUAD + q) * N_NARROW + band_of(turn) for turn in range(N_NARROW)]
    for h in range(N_NARROW)
    for q in range(QUAD)
]
PLANE_GROUPS = [
    [(plane * QUAD + i % QUAD) * N_NARROW + i // QUAD for i in range(N_WIDE)]
    for plane in range(N_NARROW)
]


def on_device(
    solution,
    residual,
    direction,
    error_var,
    footprint,
    tiles,
    window,
    temporal,
    spatial_lat,
    spatial_lon,
):
    errors = error_var.reshape(1, OBS_DEV)
    vmem = lambda shape, dtype: pltpu.VMEM(shape, dtype)
    with jax.named_scope("pack"):
        packed, slot = call(
            pack_kernel,
            [HBM] * 6,
            [((N_WIDE, PAYLOAD, LANES), BF16), ((1, OBS_DEV), I32)],
            [
                vmem((1, OBS_DEV), I32),
                vmem((NT, OBS_DEV), I32),
                vmem((OBS_DEV * NT, LANES), BF16),
                vmem((RHS, OBS_DEV), F32),
                vmem((RHS, OBS_DEV), F32),
                vmem((1, OBS_DEV), F32),
                vmem((OBS_DEV, NT * LANES), BF16),
                vmem((SLOTS, OBS_DEV), BF16),
                vmem((SLOTS, NT * LANES), F32),
                vmem((META, SLOTS), F32),
                pltpu.SemaphoreType.DMA((6,)),
            ],
            2 * SLOTS * OBS_DEV * NT * LANES,
            2 * SLOTS * OBS_DEV,
        )(
            in_hbm(window.reshape(1, OBS_DEV)),
            in_hbm(tiles.T),
            in_hbm(footprint.reshape(OBS_DEV * NT, LANES)),
            in_hbm(direction),
            in_hbm(residual),
            in_hbm(errors),
        )
    with jax.named_scope("route"):
        routed = exchange(packed, "wide")
    with jax.named_scope("adjoint"):
        flux, meta, foot = call(
            adjoint_kernel,
            [VMEM],
            [
                ((N_NARROW, CELLS, LANES), BF16),
                ((META, SLOTS), F32),
                ((NT, SLOTS, 2 * LANES), BF16),
            ],
            [
                vmem((NT, HALF, SLOTS), BF16),
                vmem((NT, ROWS // 2, SLOTS), BF16),
                vmem((ROWS // 2, 2 * LANES), F32),
            ],
            2 * ROWS * NT * SLOTS * LANES,
            4 * NT * SLOTS * LANES,
        )(routed)
    with jax.named_scope("to_rhs"):
        by_rhs = exchange(flux, BOTH, WINDOW_GROUPS)
    with jax.named_scope("lat_mix"):
        (spread,) = call(
            lat_kernel,
            [VMEM, VMEM],
            [((ROWS, LANES), BF16)],
            [vmem((ROWS + CHUNK, LANES), F32), vmem((DAY_DEV, LAT + 8, LANES), F32)],
            2 * LAT * LAT * DAY_DEV * LANES,
            4 * ROWS * LANES,
        )(spatial_lat, by_rhs)
    with jax.named_scope("to_days"):
        by_day = exchange(spread.reshape(N_WIDE, CHUNK, LANES), BOTH, PLANE_GROUPS)
    with jax.named_scope("day_mix"):
        (timed,) = call(
            day_kernel,
            [VMEM, VMEM],
            [((N_NARROW, CELLS, LANES), BF16)],
            [vmem((ROWS + 8, LANES), F32), vmem((DAYS, QUAD * LANES), BF16)],
            2 * DAYS * DAYS * QUAD * LANES,
            4 * ROWS * LANES,
        )(temporal, by_day.reshape(N_NARROW, CELLS, LANES))
    with jax.named_scope("to_windows"):
        by_window = exchange(timed.reshape(N_WIDE, CHUNK, LANES), "wide")
    with jax.named_scope("forward"):
        (modelled,) = call(
            forward_kernel,
            [VMEM] * 7,
            [((N_WIDE, RHS, LANES), F32)],
            [
                vmem((ROWS // 2, 2 * LANES), BF16),
                vmem((2, ROWS // 2, 2 * LANES), F32),
                vmem((RHS, SLOTS), F32),
            ],
            2 * ROWS * NT * SLOTS * LANES,
            4 * NT * SLOTS * LANES,
        )(
            spatial_lon,
            by_window.reshape(ROWS, LANES),
            foot,
            meta,
            direction,
            residual,
            errors,
        )
    with jax.named_scope("home"):
        home = exchange(modelled, "wide")
    with jax.named_scope("gram_sum"):
        (partial,) = call(
            sum_kernel,
            [VMEM],
            [((N_NARROW, RHS, LANES), F32)],
            [],
            N_WIDE * RHS * LANES,
            4 * N_WIDE * RHS * LANES,
        )(home)
        grams = exchange(partial, "narrow")
    with jax.named_scope("update"):
        return tuple(
            call(
                update_kernel,
                [VMEM] * 7,
                [((RHS, OBS_DEV), F32)] * 3,
                [],
                2 * 24 * SLOTS * OBS_DEV,
                28 * RHS * OBS_DEV,
            )(grams, home, slot, errors, solution, residual, direction)
        )


def solution(mesh):
    both = BOTH
    in_specs = (
        P(None, both),
        P(None, both),
        P(None, both),
        P(both),
        P(both, None, None),
        P(both, None),
        P(both, None),
        P(),
        P(),
        P(),
    )
    out_specs = (P(None, both), P(None, both), P(None, both))
    return jax.shard_map(
        on_device, mesh=mesh, in_specs=in_specs, out_specs=out_specs, check_vma=False
    )
```
